32 devices in a mesh: dp: 16 (over z, x, core), mp: 2 (over y).
Axes of the slice: x: 2, y: 2, z: 4, core: 2. Of those that a mesh axis runs over, the one named last changes fastest.
Arguments:
- kernel_state: float32 [3, 1024, 2304], P(None, 'mp'), may hold values from -2 to 2, as said below
- qkv_state: float32 [3, 768, 2304], P(None, 'dp', 'mp'), may hold values from -2 to 2, as said below
- proj_state: float32 [3, 768, 768], P(None, 'dp', 'mp'), may hold values from -4 to 4, as said below
- fc1_state: float32 [3, 768, 3072], P(None, 'dp', 'mp'), may hold values from -2 to 2, as said below
- fc2_state: float32 [3, 3072, 768], P(None, 'dp', 'mp'), may hold values from -2 to 2, as said below
- table_state: float32 [3, 60, 768], replicated, may hold values from -4 to 8, as said below
- patches_s: bfloat16 [32, 784, 192], P('dp'), may hold values from -6 to 6
- patches_l: bfloat16 [64, 16, 6912], P('dp'), may hold values from -6 to 6
- resize_s: float32 [64, 1024], P(None, 'mp'), may hold values from -2 to 2
- resize_l: float32 [2304, 1024], P(None, 'mp'), may hold values from -0.3125 to 0.3125
- bilin_s: float32 [784, 49], replicated, may hold values from 0 to 0.040816326
- bilin_l: float32 [16, 49], replicated, may hold values from 0 to 0.040816326
- cotangent: float32 [26112, 768], P(('dp', 'mp')), may hold values from -6 to 6
- rates: float32 [6], replicated, may hold values from 0 to 2, as said below
- step: int32 [1], replicated, may hold values from 1 to 3
Outputs:
- block_out: float32 [26112, 768], P(('dp', 'mp'))
- grad_norm: float32 [], replicated
- kernel_new: float32 [1024, 2304], P('mp')
- kernel_moments: float32 [2, 1024, 2304], P(None, 'mp')
- qkv_new: float32 [768, 2304], P('dp', 'mp')
- qkv_moments: float32 [2, 768, 2304], P(None, 'dp', 'mp')
- proj_new: float32 [768, 768], P('dp', 'mp')
- proj_moments: float32 [2, 768, 768], P(None, 'dp', 'mp')
- fc1_new: float32 [768, 3072], P('dp', 'mp')
- fc1_moments: float32 [2, 768, 3072], P(None, 'dp', 'mp')
- fc2_new: float32 [3072, 768], P('dp', 'mp')
- fc2_moments: float32 [2, 3072, 768], P(None, 'dp', 'mp')
- table_new: float32 [60, 768], replicated
- table_moments: float32 [2, 60, 768], replicated
The draws below stay inside these ranges and needn't reach their ends.
Inputs may be any that keep to these rules, and one draw needn't show every extreme that they name: `kernel_state`: entry 2 of every state (the second moment) is positive. `qkv_state`: entry 2 is positive. `proj_state`: entry 2 is positive. `fc1_state`: entry 2 is positive. `fc2_state`: entry 2 is positive. `table_state`: entry 2 is positive. `rates`: Positive.
All inputs are finite; a program needn't handle non-finite values.
Results may differ from the reference program's by a relative error of at most 0.019.
Values may be sent and summed in bfloat16 or wider, within the bound.
No kernel may reach another device: no remote copies, remote signals or barrier semaphores. Data moves between devices by JAX's collectives and lax.ppermute only.
A program may use at most 256 MiB of HBM per device.

```python
import math
import jax
import jax.numpy as jnp
from jax import lax

D = 768
HEADS = 12
HEAD_DIM = 64
FF = 3072
BASE = 32
POS_GRID = 7
PATCH_S = 8
PATCH_L = 48
GRID_S = 28
GRID_L = 4
IMG_L = 2
TOK_DEV = 816
NTOKENS = 26112
TROWS = 60
N_DP = 16
N_MP = 2


def grad_size():
    return 0.5


def rough(key, shape):
    return jnp.clip(jax.random.normal(key, shape, jnp.float32), -3.5, 3.5)


def make_state(key, shape, spread, offset, grad_scale):
    keys = jax.random.split(key, 3)
    master = offset + spread * rough(keys[0], shape)
    moment = grad_scale * rough(keys[1], shape)
    second = grad_scale * grad_scale * jnp.exp(jax.random.uniform(keys[2], shape, jnp.float32, math.log(0.5), math.log(8.0)))
    return jnp.stack([master, moment, second])


def draw_kernel_state(key, part):
    return make_state(key, (BASE * BASE, 3 * D), (3 * BASE * BASE) ** (-0.5), 0.0, grad_size())


def draw_qkv_state(key, part):
    return make_state(key, (D, 3 * D), D ** (-0.5), 0.0, grad_size())


def draw_proj_state(key, part):
    return make_state(key, (D, D), max(D // 64, 1) ** (-0.5), 0.0, grad_size())


def draw_fc1_state(key, part):
    return make_state(key, (D, FF), D ** (-0.5), 0.0, grad_size())


def draw_fc2_state(key, part):
    return make_state(key, (FF, D), FF ** (-0.5), 0.0, grad_size())


def draw_table_state(key, part):
    table_count = POS_GRID * POS_GRID + 7 + FF // D
    first_row = POS_GRID * POS_GRID
    places = jnp.arange(table_count)[:, None]
    gain_rows = (places == first_row + 1) | (places == first_row + 3)
    spread = jnp.where(places < first_row, 0.5, jnp.where(gain_rows, 0.1, 0.2))
    offset = jnp.where(gain_rows, 1.0, 0.0)
    return make_state(key, (table_count, D), spread, offset, 2.0 * grad_size())


def draw_rates(key, part):
    spreads = jnp.array([(3 * BASE * BASE) ** (-0.5), D ** (-0.5), max(D // 64, 1) ** (-0.5), D ** (-0.5), FF ** (-0.5), 0.3], jnp.float32)
    return spreads * jax.random.uniform(key, (6,), jnp.float32, 1.0, 2.0)


def block_levels(stream_key, dims, cuts, smallest, largest):
    gain, own = 1.0, jax.random.fold_in(stream_key, 6)
    for dim, blocks in cuts:
        steps = jnp.exp(jax.random.uniform(jax.random.fold_in(own, dim), (blocks,), jnp.float32, smallest / len(cuts), largest / len(cuts)))
        gain = gain * jnp.repeat(steps, dims[dim] // blocks).reshape([-1 if axis == dim else 1 for axis in range(len(dims))])
    return gain


def scatter_about(rng, dims, deviation, limit, cuts=(), kind=jnp.bfloat16):
    values = jax.random.normal(rng, dims, jnp.float32) * deviation
    if len(cuts) > 0:
        values = block_levels(rng, dims, cuts, -0.22, 0.18) * values
    return jnp.clip(values, min=-limit, max=limit).astype(kind)


def setup_inputs(seed: int = 0) -> dict:
    arg_keys = jax.random.split(jax.random.key(seed), 16)
    kernel_state = draw_kernel_state(jax.random.fold_in(arg_keys[15], 71), 0)
    qkv_state = draw_qkv_state(jax.random.fold_in(arg_keys[15], 71), 0)
    proj_state = draw_proj_state(jax.random.fold_in(arg_keys[15], 71), 0)
    fc1_state = draw_fc1_state(jax.random.fold_in(arg_keys[15], 71), 0)
    fc2_state = draw_fc2_state(jax.random.fold_in(arg_keys[15], 71), 0)
    table_state = draw_table_state(jax.random.fold_in(arg_keys[15], 71), 0)
    patches_s = scatter_about(arg_keys[6], (N_DP * N_MP, GRID_S * GRID_S, 3 * PATCH_S * PATCH_S), 1.0, 6.0, ((0, 16),))
    patches_l = scatter_about(arg_keys[7], (N_DP * N_MP * IMG_L, GRID_L * GRID_L, 3 * PATCH_L * PATCH_L), 1.0, 6.0, ((0, 16),))
    resize_s = scatter_about(arg_keys[8], (PATCH_S * PATCH_S, BASE * BASE), (PATCH_S ** -1), 2.0, ((1, 2),), jnp.float32)
    resize_l = scatter_about(arg_keys[9], (PATCH_L * PATCH_L, BASE * BASE), (PATCH_L ** -1), 0.3125, ((1, 2),), jnp.float32)
    bilin_s = jnp.clip(jax.random.uniform(arg_keys[10], (GRID_S * GRID_S, POS_GRID * POS_GRID), jnp.float32, 0.0, 0.040816326), 0.0, 0.040816326)
    bilin_l = jnp.clip(jax.random.uniform(arg_keys[11], (GRID_L * GRID_L, POS_GRID * POS_GRID), jnp.float32, 0.0, 0.040816326), 0.0, 0.040816326)
    cotangent = scatter_about(arg_keys[12], (NTOKENS, D), 1.0, 6.0, ((0, 32),), jnp.float32)
    rates = draw_rates(jax.random.fold_in(arg_keys[15], 71), 0)
    step = jax.random.randint(arg_keys[14], (1,), 1, 4).astype(jnp.int32)
    return {"kernel_state": kernel_state, "qkv_state": qkv_state, "proj_state": proj_state, "fc1_state": fc1_state, "fc2_state": fc2_state, "table_state": table_state, "patches_s": patches_s, "patches_l": patches_l, "resize_s": resize_s, "resize_l": resize_l, "bilin_s": bilin_s, "bilin_l": bilin_l, "cotangent": cotangent, "rates": rates, "step": step}


@jax.custom_vjp
def low(v):
    return lax.optimization_barrier(v.astype(jnp.bfloat16)).astype(jnp.float32)

@jax.custom_vjp
def low_back(v):
    return v

def low_keep(v):
    return (low(v), None)

def low_pass(kept, grad):
    return (grad,)

def back_keep(v):
    return (v, None)

def back_low(kept, grad):
    return (low(grad),)
low.defvjp(low_keep, low_pass)
low_back.defvjp(back_keep, back_low)
HIGHEST = lax.Precision.HIGHEST
NORM_EPS = 1e-06
BETA_ONE = 0.5
BETA_TWO = 0.5
DECAY = 0.05
ADAM_EPS = 1e-08
MASKED = -1e+30

def layer_norm(inputs, gain_row, shift_row):
    centered = inputs - lax.optimization_barrier(jnp.mean(inputs, axis=-1, keepdims=True))
    variance = lax.optimization_barrier(jnp.mean(centered * centered, axis=-1, keepdims=True))
    return centered * lax.rsqrt(variance + NORM_EPS) * gain_row + shift_row

def gelu_exact(inputs):
    return 0.5 * inputs * (1.0 + lax.erf(inputs * 0.7071067811865476))

def image_ids(row_count):
    places = jnp.arange(row_count, dtype=jnp.int32)
    first_row = GRID_S * GRID_S
    return jnp.where(places < first_row, 0, 1 + (places - first_row) // (GRID_L * GRID_L))

def block_forward(inputs, w_qkv, w_proj, w_fc1, w_fc2, table_rows):
    first_row = POS_GRID * POS_GRID
    row_count = inputs.shape[0]
    normed = low(layer_norm(inputs, table_rows[first_row + 1], table_rows[first_row + 2]))
    projected = low(low_back(jnp.dot(normed, w_qkv, precision=HIGHEST)))
    split_heads = projected.reshape(row_count, 3, HEADS, HEAD_DIM)
    queries = split_heads[:, 0].transpose(1, 0, 2)
    keys_all = split_heads[:, 1].transpose(1, 0, 2)
    values = split_heads[:, 2].transpose(1, 0, 2)
    labels = image_ids(row_count)
    same_image = labels[:, None] == labels[None, :]
    scores = low_back(jnp.einsum('hqd,hkd->hqk', queries, keys_all, precision=HIGHEST) * HEAD_DIM ** (-0.5))
    scores = jnp.where(same_image[None], scores, MASKED)
    weights = low(jax.nn.softmax(scores, axis=-1))
    attended = jnp.einsum('hqk,hkd->hqd', weights, values, precision=HIGHEST)
    attended = low(low_back(attended.transpose(1, 0, 2).reshape(row_count, D)))
    branch = low_back(jnp.dot(attended, w_proj, precision=HIGHEST) + table_rows[first_row + 5])
    middle = inputs + branch
    normed_two = low(layer_norm(middle, table_rows[first_row + 3], table_rows[first_row + 4]))
    hidden = low_back(jnp.dot(normed_two, w_fc1, precision=HIGHEST) + table_rows[first_row + 7:].reshape(FF))
    activated = low(gelu_exact(hidden))
    return middle + low_back(jnp.dot(activated, w_fc2, precision=HIGHEST) + table_rows[first_row + 6])

def forward(base_kernel, w_qkv, w_proj, w_fc1, w_fc2, table_rows, small_patches, large_patches, resize_s, resize_l, bilin_s, bilin_l):
    kern_small = low(jnp.dot(resize_s, base_kernel, precision=HIGHEST).reshape(3 * PATCH_S * PATCH_S, D))
    kern_large = jnp.dot(resize_l, base_kernel, precision=HIGHEST).reshape(3 * PATCH_L * PATCH_L, D)
    low_qkv = low(w_qkv)
    low_proj = low(w_proj)
    low_fc1 = low(w_fc1)
    low_fc2 = low(w_fc2)
    first_row = POS_GRID * POS_GRID
    pos_small = jnp.dot(bilin_s, table_rows[:first_row], precision=HIGHEST)
    pos_large = jnp.dot(bilin_l, table_rows[:first_row], precision=HIGHEST)
    placed = jnp.concatenate([pos_small, jnp.tile(pos_large, (IMG_L, 1))], axis=0) + table_rows[first_row]
    device_count = N_DP * N_MP
    small_rows = small_patches.reshape(device_count, GRID_S * GRID_S, 3 * PATCH_S * PATCH_S)
    large_rows = large_patches.reshape(device_count, IMG_L * GRID_L * GRID_L, 3 * PATCH_L * PATCH_L)

    def one_device(carried, pieces):
        embedded = jnp.concatenate([jnp.dot(pieces[0], kern_small, precision=HIGHEST), jnp.dot(pieces[1], kern_large, precision=HIGHEST)], axis=0)
        result = block_forward(low_back(embedded) + placed, low_qkv, low_proj, low_fc1, low_fc2, table_rows)
        return (carried, result)
    final_carry, outputs = lax.scan(jax.checkpoint(one_device), jnp.zeros((), jnp.float32), (small_rows, large_rows))
    return outputs.reshape(device_count * TOK_DEV, D)

def adam_step(state_stack, gradient, rate_value, factor, fix_one, fix_two):
    clipped = gradient * factor
    first_moment = BETA_ONE * state_stack[1] + (1.0 - BETA_ONE) * clipped
    second = BETA_TWO * state_stack[2] + (1.0 - BETA_TWO) * clipped * clipped
    movement = first_moment / fix_one / (jnp.sqrt(second / fix_two) + ADAM_EPS) + DECAY * state_stack[0]
    return (state_stack[0] - rate_value * movement, jnp.stack([first_moment, second]))

def reference(kernel_state, qkv_state, proj_state, fc1_state, fc2_state, table_state, patches_s, patches_l, resize_s, resize_l, bilin_s, bilin_l, cotangent, rates, step):
    small_float = patches_s.astype(jnp.float32)
    large_float = patches_l.astype(jnp.float32)

    def run_layer(base_kernel, w_qkv, w_proj, w_fc1, w_fc2, table_rows):
        return forward(base_kernel, w_qkv, w_proj, w_fc1, w_fc2, table_rows, small_float, large_float, resize_s, resize_l, bilin_s, bilin_l)
    block_out, pull_back = jax.vjp(run_layer, kernel_state[0], qkv_state[0], proj_state[0], fc1_state[0], fc2_state[0], table_state[0])
    gradients = pull_back(cotangent)
    squares = jnp.zeros((), jnp.float32)
    for gradient in gradients:
        squares = squares + jnp.sum(gradient * gradient)
    grad_norm = jnp.sqrt(squares)
    clip_level = 0.5 * math.sqrt(3 * BASE * BASE * D + 4 * D * D + 2 * D * FF + TROWS * D)
    factor = clip_level / jnp.maximum(grad_norm, clip_level)
    step_count = step[0].astype(jnp.float32)
    fix_one = 1.0 - jnp.power(BETA_ONE, step_count)
    fix_two = 1.0 - jnp.power(BETA_TWO, step_count)
    states = (kernel_state, qkv_state, proj_state, fc1_state, fc2_state, table_state)
    updated = [adam_step(states[position], gradients[position], rates[position], factor, fix_one, fix_two) for position in range(6)]
    return (block_out, grad_norm, updated[0][0], updated[0][1], updated[1][0], updated[1][1], updated[2][0], updated[2][1], updated[3][0], updated[3][1], updated[4][0], updated[4][1], updated[5][0], updated[5][1])
```

```python
import functools
import math

import jax
import jax.numpy as jnp
from jax import lax
from jax.experimental import pallas as pl
from jax.experimental.pallas import tpu as pltpu
from jax.sharding import PartitionSpec as P

D = 768
HEADS = 12
HEAD_DIM = 64
FF = 3072
BASE = 32
POS_GRID = 7
GRID_S = 28
GRID_L = 4
TROWS = 60

NORM_EPS = 1e-06
BETA_ONE = 0.5
BETA_TWO = 0.5
DECAY = 0.05
ADAM_EPS = 1e-08
MASKED = -1e30
LOG2E = 1.4426950408889634
LANES = 128
MIB = 2**20

BF = jnp.bfloat16
F32 = jnp.float32
NN = (((1,), (0,)), ((), ()))
NT = (((1,), (1,)), ((), ()))
TN = (((0,), (0,)), ((), ()))


def shape_of(dims, dtype):
    return jax.ShapeDtypeStruct(dims, dtype)


def params(mib=56):
    return pltpu.CompilerParams(vmem_limit_bytes=mib * MIB)


def cost(flops, moved):
    return pl.CostEstimate(flops=int(flops), bytes_accessed=int(moved), transcendentals=0)


def dot(left, right, dims=NN):
    return lax.dot_general(left, right, dims, preferred_element_type=F32)


def halves(value):
    high = value.astype(BF)
    return high, (value - high.astype(F32)).astype(BF)


def dot_fine(left, right, dims=NN):
    left_high, left_low = halves(left)
    right_high, right_low = halves(right)
    return dot(left_high, right_high, dims) + (
        dot(left_high, right_low, dims) + dot(left_low, right_high, dims)
    )


def norm_forward(inputs):
    centered = inputs - jnp.mean(inputs, axis=-1, keepdims=True)
    inverse = lax.rsqrt(jnp.mean(centered * centered, axis=-1, keepdims=True) + NORM_EPS)
    return centered * inverse, inverse


def norm_backward(upstream, normalized, inverse, gain_row):
    scaled = upstream * gain_row
    inner = jnp.mean(scaled * normalized, axis=-1, keepdims=True)
    result = inverse * (scaled - jnp.mean(scaled, axis=-1, keepdims=True) - normalized * inner)
    return (
        result,
        jnp.sum(upstream * normalized, axis=0, keepdims=True),
        jnp.sum(upstream, axis=0, keepdims=True),
    )


def resize_kernel(
    base_ref, small_ref, large_ref, patch_ref, projected_ref, embed_ref, kern_ref, turned, pixels_ref
):
    rows = embed_ref.shape[0]

    @pl.when(pl.program_id(0) == 0)
    def _():
        embed_ref[...] = jnp.zeros_like(embed_ref)
        kern_ref[...] = jnp.zeros_like(kern_ref)
        count = large_ref.shape[0]
        for start in range(0, rows, LANES):
            size = min(LANES, rows - start)
            patch = patch_ref[start : start + size, :].astype(F32)
            if size < LANES:
                patch = jnp.concatenate(
                    [patch, jnp.zeros((LANES - size, patch.shape[1]), F32)], axis=0
                )
            turned[...] = patch.T
            for channel in range(3):
                pixels_ref[:, channel * rows + start : channel * rows + start + size] = turned[
                    pl.ds(channel, count, stride=3), :
                ][:, :size].astype(BF)

    base = base_ref[0]
    width = base.shape[1] // 3
    large_high, large_low = halves(large_ref[...])
    pixels = pixels_ref[...]
    projected = dot(large_high, pixels, TN) + dot(large_low, pixels, TN)
    projected_ref[...] = projected.astype(BF)
    kern_ref[...] += dot_fine(small_ref[...], base)
    total = embed_ref[...]
    for channel in range(3):
        total += dot_fine(
            projected[:, channel * rows : (channel + 1) * rows],
            base[:, channel * width : (channel + 1) * width],
            TN,
        )
    embed_ref[...] = total


def resize_forward(kernel_state, resize_s, resize_l, patches):
    base_rows, wide = kernel_state.shape[1:]
    count = base_rows // LANES
    rows = patches.shape[0]
    columns = 3 * rows
    return pl.pallas_call(
        resize_kernel,
        grid=(count,),
        in_specs=[
            pl.BlockSpec((1, LANES, wide), lambda i: (0, i, 0)),
            pl.BlockSpec((resize_s.shape[0], LANES), lambda i: (0, i)),
            pl.BlockSpec((resize_l.shape[0], LANES), lambda i: (0, i)),
            pl.BlockSpec(patches.shape, lambda i: (0, 0)),
        ],
        out_specs=[
            pl.BlockSpec((LANES, columns), lambda i: (i, 0)),
            pl.BlockSpec((rows, wide // 3), lambda i: (0, 0)),
            pl.BlockSpec((resize_s.shape[0], wide), lambda i: (0, 0)),
        ],
        out_shape=[
            shape_of((base_rows, columns), BF),
            shape_of((rows, wide // 3), F32),
            shape_of((resize_s.shape[0], wide), F32),
        ],
        scratch_shapes=[
            pltpu.VMEM((patches.shape[1], LANES), F32),
            pltpu.VMEM((resize_l.shape[0], columns), BF),
        ],
        compiler_params=params(),
        cost_estimate=cost(9e9, 0),
        name="resize",
    )(kernel_state, resize_s, resize_l, patches)


def embed_kernel(
    patch_ref, kern_ref, large_ref, bilin_s_ref, bilin_l_ref, table_ref, x_ref, a_ref, woven
):
    table = table_ref[0]
    first = POS_GRID * POS_GRID
    pixels = kern_ref.shape[0]
    width = table.shape[1]
    tiles = width // LANES
    for channel in range(3):
        for tile in range(tiles):
            start = channel * width + tile * LANES
            woven[tile, pl.ds(channel, pixels, stride=3), :] = kern_ref[:, start : start + LANES]
    kern = jnp.concatenate([woven[tile].astype(BF) for tile in range(tiles)], axis=1)
    grid_rows = table[:first]
    bias = table[first : first + 1]
    small = patch_ref.shape[0]
    x_ref[:small, :] = (
        dot(patch_ref[...], kern) + dot_fine(bilin_s_ref[...], grid_rows) + bias
    )
    tokens = bilin_l_ref.shape[0]
    placed = dot_fine(bilin_l_ref[...], grid_rows) + bias
    for image in range(large_ref.shape[0] // tokens):
        part = slice(image * tokens, (image + 1) * tokens)
        x_ref[small + image * tokens : small + (image + 1) * tokens, :] = large_ref[part, :] + placed
    normal, _ = norm_forward(x_ref[...])
    a_ref[...] = (normal * table[first + 1 : first + 2] + table[first + 2 : first + 3]).astype(BF)


def embed(patches, kern, large, bilin_s, bilin_l, table_state):
    rows = patches.shape[0] + large.shape[0]
    width = table_state.shape[2]
    whole = lambda array: pl.BlockSpec(array.shape, lambda i: (0,) * array.ndim)
    return pl.pallas_call(
        embed_kernel,
        grid=(1,),
        in_specs=[
            whole(patches),
            whole(kern),
            whole(large),
            whole(bilin_s),
            whole(bilin_l),
            pl.BlockSpec((1,) + table_state.shape[1:], lambda i: (0, 0, 0)),
        ],
        out_specs=[pl.BlockSpec((rows, width), lambda i: (0, 0))] * 2,
        out_shape=[shape_of((rows, width), F32), shape_of((rows, width), BF)],
        scratch_shapes=[pltpu.VMEM((width // LANES, patches.shape[1], LANES), F32)],
        compiler_params=params(),
        cost_estimate=cost(5e9, 0),
        name="embed",
    )(patches, kern, large, bilin_s, bilin_l, table_state)


def product_kernel(left_ref, right_ref, out_ref):
    out_ref[...] = dot(left_ref[...], right_ref[...]).astype(BF)


def product(left, right, block):
    rows, depth = left.shape
    columns = right.shape[1]
    return pl.pallas_call(
        product_kernel,
        grid=(columns // block,),
        in_specs=[
            pl.BlockSpec((rows, depth), lambda i: (0, 0)),
            pl.BlockSpec((depth, block), lambda i: (0, i)),
        ],
        out_specs=pl.BlockSpec((rows, block), lambda i: (0, i)),
        out_shape=shape_of((rows, columns), BF),
        compiler_params=params(),
        cost_estimate=cost(7e9, 0),
        name="project",
    )(left, right)


def image_features(rows, first_rows, image_rows):
    row = lax.broadcasted_iota(jnp.int32, (rows, LANES), 0)
    lane = lax.broadcasted_iota(jnp.int32, (rows, LANES), 1) % HEAD_DIM
    label = jnp.where(row < first_rows, 0, 1 + (row - first_rows) // image_rows)
    count = 1 + (rows - first_rows) // image_rows
    own = label == lane
    query = jnp.where(own | (lane >= count), 0.0, MASKED).astype(BF)
    return query, jnp.where(own, 1.0, 0.0).astype(BF)


def attend_kernel(first_rows, image_rows, chunks, q_ref, k_ref, v_ref, out_ref, log_ref):
    rows = q_ref.shape[0]
    query_mark, key_mark = image_features(rows, first_rows, image_rows)
    low = lax.broadcasted_iota(jnp.int32, (rows, LANES), 1) < HEAD_DIM
    step = rows // chunks
    queries = q_ref[...] * jnp.asarray(HEAD_DIM**-0.5, BF)
    keys, values = k_ref[...], v_ref[...]
    ones = jnp.ones((rows, LANES), BF)
    results = []
    for head in range(2):
        mine = low if head == 0 else ~low
        query = jnp.where(mine, queries, query_mark)
        key = jnp.where(mine, keys, key_mark)
        value = jnp.where(mine, values, ones)
        outs, logs = [], []
        for chunk in range(chunks):
            scores = dot(query[chunk * step : (chunk + 1) * step], key, NT)
            largest = jnp.max(scores, axis=1, keepdims=True)
            probs = jnp.exp2(scores * LOG2E - largest * LOG2E)
            summed = dot(probs.astype(BF), value)
            rolled = pltpu.roll(summed, HEAD_DIM, 1)
            outs.append(summed / rolled)
            logs.append(largest * LOG2E + jnp.log2(jnp.where(mine[:step], rolled, summed)))
        results.append(jnp.concatenate(outs, axis=0))
        log_ref[0, 8 * head : 8 * head + 8, :] = jnp.concatenate(logs, axis=0).T[:8]
    out_ref[...] = jnp.where(low, results[0], results[1]).astype(BF)


def attend(qkv, first_rows, image_rows):
    rows, wide = qkv.shape
    width = wide // 3
    pairs = width // LANES
    chunks = 3 if rows % 48 == 0 else 1
    part = lambda offset: pl.BlockSpec((rows, LANES), lambda i: (0, offset + i))
    return pl.pallas_call(
        functools.partial(attend_kernel, first_rows, image_rows, chunks),
        grid=(pairs,),
        in_specs=[part(0), part(pairs), part(2 * pairs)],
        out_specs=[part(0), pl.BlockSpec((1, 16, rows), lambda i: (i, 0, 0))],
        out_shape=[shape_of((rows, width), BF), shape_of((pairs, 16, rows), F32)],
        compiler_params=params(),
        cost_estimate=cost(18e9, 0),
        name="attend",
    )(qkv, qkv, qkv)


def merge_kernel(x_ref, attended_ref, w_ref, table_ref, middle_ref, a_ref):
    first = POS_GRID * POS_GRID
    table = table_ref[0]
    middle = x_ref[...] + dot(attended_ref[...], w_ref[...]) + table[first + 5 : first + 6]
    middle_ref[...] = middle
    normal, _ = norm_forward(middle)
    a_ref[...] = (normal * table[first + 3 : first + 4] + table[first + 4 : first + 5]).astype(BF)


def merge(inputs, attended, w_proj, table_state):
    rows, width = inputs.shape
    whole = lambda array: pl.BlockSpec(array.shape, lambda i: (0,) * array.ndim)
    return pl.pallas_call(
        merge_kernel,
        grid=(1,),
        in_specs=[
            whole(inputs),
            whole(attended),
            whole(w_proj),
            pl.BlockSpec((1,) + table_state.shape[1:], lambda i: (0, 0, 0)),
        ],
        out_specs=[whole(inputs)] * 2,
        out_shape=[shape_of((rows, width), F32), shape_of((rows, width), BF)],
        compiler_params=params(),
        cost_estimate=cost(6e9, 0),
        name="merge",
    )(inputs, attended, w_proj, table_state)


def feed_kernel(
    middle_ref,
    a_ref,
    cotangent_ref,
    w_one_ref,
    w_two_ref,
    bias_ref,
    table_ref,
    out_ref,
    grad_ref,
    g_one_ref,
    g_two_ref,
    b_one_ref,
    b_two_ref,
    turned,
    upstream,
):
    @pl.when(pl.program_id(0) == 0)
    def _():
        first = POS_GRID * POS_GRID
        turned[...] = a_ref[...].T
        low = cotangent_ref[...].astype(BF)
        upstream[...] = low
        out_ref[...] = middle_ref[...] + table_ref[0][first + 6 : first + 7]
        grad_ref[...] = jnp.zeros_like(grad_ref)
        b_two_ref[...] = jnp.sum(low.astype(F32), axis=0, keepdims=True)

    w_one, w_two, dz = w_one_ref[...], w_two_ref[...], upstream[...]
    hidden = dot(a_ref[...], w_one) + bias_ref[...]
    phi = 0.5 * (1.0 + lax.erf(hidden * 0.7071067811865476))
    active = (hidden * phi).astype(BF)
    slope = phi + hidden * jnp.exp(-0.5 * hidden * hidden) * 0.3989422804014327
    change = dot(dz, w_two, NT) * slope
    b_one_ref[...] = jnp.sum(change, axis=0, keepdims=True)
    change = change.astype(BF)
    out_ref[...] += dot(active, w_two)
    grad_ref[...] += dot(change, w_one, NT)
    g_one_ref[...] = dot(turned[...], change).astype(BF)
    g_two_ref[...] = dot(active, dz, TN).astype(BF)


def feed(middle, normed, cotangent, w_one, w_two, bias_one, table_state, block):
    rows, width = normed.shape
    hidden = w_one.shape[1]
    full = pl.BlockSpec((rows, width), lambda i: (0, 0))
    across = pl.BlockSpec((width, block), lambda i: (0, i))
    down = pl.BlockSpec((block, width), lambda i: (i, 0))
    line = pl.BlockSpec((1, block), lambda i: (0, i))
    return pl.pallas_call(
        feed_kernel,
        grid=(hidden // block,),
        in_specs=[
            full,
            full,
            full,
            across,
            down,
            line,
            pl.BlockSpec((1,) + table_state.shape[1:], lambda i: (0, 0, 0)),
        ],
        out_specs=[full, full, across, down, line, pl.BlockSpec((1, width), lambda i: (0, 0))],
        out_shape=[
            shape_of((rows, width), F32),
            shape_of((rows, width), F32),
            shape_of((width, hidden), BF),
            shape_of((hidden, width), BF),
            shape_of((1, hidden), F32),
            shape_of((1, width), F32),
        ],
        scratch_shapes=[pltpu.VMEM((width, rows), BF), pltpu.VMEM((rows, width), BF)],
        compiler_params=params(60),
        cost_estimate=cost(34e9, 0),
        name="feed",
    )(middle, normed, cotangent, w_one, w_two, bias_one, table_state)


def merge_back_kernel(
    grad_ref,
    middle_ref,
    cotangent_ref,
    attended_ref,
    w_ref,
    table_ref,
    back_ref,
    heads_ref,
    g_ref,
    rows_ref,
):
    first = POS_GRID * POS_GRID
    normal, inverse = norm_forward(middle_ref[...])
    change, gain, shift = norm_backward(
        grad_ref[...], normal, inverse, table_ref[0][first + 3 : first + 4]
    )
    back = cotangent_ref[...] + change
    back_ref[...] = back
    low = back.astype(BF)
    heads_ref[...] = dot(low, w_ref[...], NT).astype(BF)
    g_ref[...] = dot(attended_ref[...], low, TN).astype(BF)
    rows_ref[0:1, :] = gain
    rows_ref[1:2, :] = shift
    rows_ref[2:3, :] = jnp.sum(low.astype(F32), axis=0, keepdims=True)


def merge_back(grad, middle, cotangent, attended, w_proj, table_state):
    rows, width = middle.shape
    whole = lambda array: pl.BlockSpec(array.shape, lambda i: (0,) * array.ndim)
    return pl.pallas_call(
        merge_back_kernel,
        grid=(1,),
        in_specs=[
            whole(grad),
            whole(middle),
            whole(cotangent),
            whole(attended),
            whole(w_proj),
            pl.BlockSpec((1,) + table_state.shape[1:], lambda i: (0, 0, 0)),
        ],
        out_specs=[
            whole(middle),
            whole(middle),
            whole(w_proj),
            pl.BlockSpec((8, width), lambda i: (0, 0)),
        ],
        out_shape=[
            shape_of((rows, width), F32),
            shape_of((rows, width), BF),
            shape_of(w_proj.shape, BF),
            shape_of((8, width), F32),
        ],
        compiler_params=params(),
        cost_estimate=cost(9e9, 0),
        name="merge_back",
    )(grad, middle, cotangent, attended, w_proj, table_state)


def attend_back_kernel(
    first_rows, image_rows, chunks, q_ref, k_ref, v_ref, out_ref, up_ref, log_ref, grad_ref
):
    rows = q_ref.shape[0]
    query_mark, key_mark = image_features(rows, first_rows, image_rows)
    low = lax.broadcasted_iota(jnp.int32, (rows, LANES), 1) < HEAD_DIM
    step = rows // chunks
    queries = q_ref[...] * jnp.asarray(HEAD_DIM**-0.5, BF)
    keys, values, up = k_ref[...], v_ref[...], up_ref[...]
    overlap = (out_ref[...].astype(F32) * up.astype(F32)).T
    zeros = jnp.zeros((rows, LANES), BF)
    grads = ([], [], [])
    for head in range(2):
        mine = low if head == 0 else ~low
        query = jnp.where(mine, queries, query_mark)
        key = jnp.where(mine, keys, key_mark)
        value = jnp.where(mine, values, zeros)
        inner = jnp.sum(overlap[HEAD_DIM * head : HEAD_DIM * (head + 1)], axis=0, keepdims=True)
        totals = log_ref[0, 8 * head : 8 * head + 1, :]
        query_grad = jnp.zeros((rows, LANES), F32)
        key_grads, value_grads = [], []
        for chunk in range(chunks):
            part = slice(chunk * step, (chunk + 1) * step)
            scores = dot(key[part], query, NT)
            probs = jnp.exp2(scores * LOG2E - totals)
            value_grads.append(dot(probs.astype(BF), up))
            change = (probs * (dot(value[part], up, NT) - inner)).astype(BF)
            key_grads.append(dot(change, queries))
            query_grad = query_grad + dot(change, keys[part], TN)
        grads[0].append(query_grad * HEAD_DIM**-0.5)
        grads[1].append(jnp.concatenate(key_grads, axis=0))
        grads[2].append(jnp.concatenate(value_grads, axis=0))
    for place, pair in enumerate(grads):
        grad_ref[place] = jnp.where(low, pair[0], pair[1]).astype(BF)


def attend_back(qkv, attended, upstream, logs, first_rows, image_rows):
    rows, wide = qkv.shape
    width = wide // 3
    pairs = width // LANES
    part = lambda offset: pl.BlockSpec((rows, LANES), lambda i: (0, offset + i))
    return pl.pallas_call(
        functools.partial(attend_back_kernel, first_rows, image_rows, 1),
        grid=(pairs,),
        in_specs=[
            part(0),
            part(pairs),
            part(2 * pairs),
            part(0),
            part(0),
            pl.BlockSpec((1, 16, rows), lambda i: (i, 0, 0)),
        ],
        out_specs=pl.BlockSpec((3, rows, LANES), lambda i: (0, 0, i)),
        out_shape=shape_of((3, rows, width), BF),
        compiler_params=params(),
        cost_estimate=cost(30e9, 0),
        name="attend_back",
    )(qkv, qkv, qkv, attended, upstream, logs)


def inputs_back_kernel(
    heads_ref,
    a_ref,
    w_ref,
    x_ref,
    back_ref,
    table_ref,
    patch_ref,
    bilin_s_ref,
    bilin_l_ref,
    middle_rows_ref,
    b_one_ref,
    b_two_ref,
    g_ref,
    table_grad_ref,
    large_ref,
    kern_ref,
    turned,
    total,
    woven,
):
    place = pl.program_id(0)

    @pl.when(place == 0)
    def _():
        turned[...] = a_ref[...].T
        total[...] = jnp.zeros_like(total)

    heads = heads_ref[0]
    g_ref[...] = dot(turned[...], heads).astype(BF)
    total[...] += dot(heads, w_ref[...], NT)

    @pl.when(place == pl.num_programs(0) - 1)
    def _():
        first = POS_GRID * POS_GRID
        normal, inverse = norm_forward(x_ref[...])
        change, gain, shift = norm_backward(
            total[...], normal, inverse, table_ref[0][first + 1 : first + 2]
        )
        grad = back_ref[...] + change
        low = grad.astype(BF)
        small = patch_ref.shape[0]
        width = grad.shape[1]
        large_ref[...] = low[small:]
        kern = dot(patch_ref[...], low[:small], TN)
        pixels = kern_ref.shape[0]
        for tile in range(width // LANES):
            woven[tile] = kern[:, tile * LANES : (tile + 1) * LANES]
            for channel in range(3):
                start = channel * width + tile * LANES
                kern_ref[:, start : start + LANES] = woven[tile, pl.ds(channel, pixels, stride=3), :]
        tokens = bilin_l_ref.shape[0]
        large = grad[small : small + tokens]
        for image in range(1, (grad.shape[0] - small) // tokens):
            large = large + grad[small + image * tokens : small + (image + 1) * tokens]
        table_grad_ref[:first, :] = dot_fine(bilin_s_ref[...], grad[:small], TN) + dot_fine(
            bilin_l_ref[...], large, TN
        )
        table_grad_ref[first : first + 1, :] = jnp.sum(grad, axis=0, keepdims=True)
        table_grad_ref[first + 1 : first + 2, :] = gain
        table_grad_ref[first + 2 : first + 3, :] = shift
        table_grad_ref[first + 3 : first + 6, :] = middle_rows_ref[0:3, :]
        table_grad_ref[first + 6 : first + 7, :] = b_two_ref[...]
        for line in range(b_one_ref.shape[1] // width):
            table_grad_ref[first + 7 + line : first + 8 + line, :] = b_one_ref[
                :, line * width : (line + 1) * width
            ]


def inputs_back(
    heads,
    normed,
    w_qkv,
    inputs,
    back,
    table_state,
    patches,
    bilin_s,
    bilin_l,
    middle_rows,
    bias_one,
    bias_two,
    pixels,
):
    rows, width = inputs.shape
    whole = lambda array: pl.BlockSpec(array.shape, lambda i: (0,) * array.ndim)
    large = rows - patches.shape[0]
    return pl.pallas_call(
        inputs_back_kernel,
        grid=(3,),
        in_specs=[
            pl.BlockSpec((1, rows, width), lambda i: (i, 0, 0)),
            whole(normed),
            pl.BlockSpec((width, width), lambda i: (0, i)),
            whole(inputs),
            whole(back),
            pl.BlockSpec((1,) + table_state.shape[1:], lambda i: (0, 0, 0)),
            whole(patches),
            whole(bilin_s),
            whole(bilin_l),
            whole(middle_rows),
            whole(bias_one),
            whole(bias_two),
        ],
        out_specs=[
            pl.BlockSpec((width, width), lambda i: (0, i)),
            pl.BlockSpec(table_state.shape[1:], lambda i: (0, 0)),
            pl.BlockSpec((large, width), lambda i: (0, 0)),
            pl.BlockSpec((pixels, 3 * width), lambda i: (0, 0)),
        ],
        out_shape=[
            shape_of(w_qkv.shape, BF),
            shape_of(table_state.shape[1:], F32),
            shape_of((large, width), BF),
            shape_of((pixels, 3 * width), F32),
        ],
        scratch_shapes=[
            pltpu.VMEM((width, rows), BF),
            pltpu.VMEM((rows, width), F32),
            pltpu.VMEM((width // LANES, 3 * pixels, LANES), F32),
        ],
        compiler_params=params(),
        cost_estimate=cost(16e9, 0),
        name="inputs_back",
    )(
        heads,
        normed,
        w_qkv,
        inputs,
        back,
        table_state,
        patches,
        bilin_s,
        bilin_l,
        middle_rows,
        bias_one,
        bias_two,
    )


def base_back_kernel(projected_ref, large_ref, small_ref, kern_ref, out_ref):
    rows, width = large_ref.shape
    large = large_ref[...]
    out = dot_fine(small_ref[...], kern_ref[...], TN)
    for channel in range(3):
        part = slice(channel * width, (channel + 1) * width)
        out_ref[:, part] = (
            dot(projected_ref[:, channel * rows : (channel + 1) * rows], large) + out[:, part]
        ).astype(BF)


def base_back(projected, large, resize_s, kern):
    whole = lambda array: pl.BlockSpec(array.shape, lambda i: (0,) * array.ndim)
    rows, wide = projected.shape[0], kern.shape[1]
    return pl.pallas_call(
        base_back_kernel,
        grid=(1,),
        in_specs=[whole(projected), whole(large), whole(resize_s), whole(kern)],
        out_specs=pl.BlockSpec((rows, wide), lambda i: (0, 0)),
        out_shape=shape_of((rows, wide), BF),
        compiler_params=params(),
        cost_estimate=cost(5e9, 0),
        name="base_back",
    )(projected, large, resize_s, kern)


def adam_values(state, gradient, rate, scalars):
    clipped = gradient * scalars[0]
    first = BETA_ONE * state[1] + (1.0 - BETA_ONE) * clipped
    second = BETA_TWO * state[2] + (1.0 - BETA_TWO) * clipped * clipped
    movement = (first * scalars[1]) / (jnp.sqrt(second * scalars[2]) + ADAM_EPS)
    return state[0] - rate * (movement + DECAY * state[0]), first, second


def adam_kernel(count, scalars_ref, *refs):
    scalars = [scalars_ref[place] for place in range(3)]
    for place in range(count):
        state_ref, gradient_ref = refs[2 * place], refs[2 * place + 1]
        new_ref, moments_ref = refs[2 * count + 2 * place], refs[2 * count + 2 * place + 1]
        new, first, second = adam_values(
            state_ref[...], gradient_ref[...].astype(F32), scalars_ref[3 + place], scalars
        )
        new_ref[...] = new
        moments_ref[0] = first
        moments_ref[1] = second


def adam(scalars, states, gradients, steps):
    in_specs = [pl.BlockSpec(memory_space=pltpu.SMEM)]
    out_specs, out_shapes, operands = [], [], [scalars]
    for state, gradient in zip(states, gradients):
        rows, columns = state.shape[1:]
        part = rows // steps
        in_specs.append(pl.BlockSpec((3, part, columns), lambda i: (0, i, 0)))
        in_specs.append(pl.BlockSpec((part, columns), lambda i: (i, 0)))
        out_specs.append(pl.BlockSpec((part, columns), lambda i: (i, 0)))
        out_specs.append(pl.BlockSpec((2, part, columns), lambda i: (0, i, 0)))
        out_shapes.append(shape_of((rows, columns), F32))
        out_shapes.append(shape_of((2, rows, columns), F32))
        operands += [state, gradient]
    return pl.pallas_call(
        functools.partial(adam_kernel, len(states)),
        grid=(steps,),
        in_specs=in_specs,
        out_specs=out_specs,
        out_shape=out_shapes,
        compiler_params=params(),
        cost_estimate=cost(9e9, 0),
        name="optimizer",
    )(*operands)


class Place:
    def __init__(self):
        self.dp, self.mp = lax.axis_size("dp"), lax.axis_size("mp")
        self.index, self.column = lax.axis_index("dp"), lax.axis_index("mp")
        self.direct = self.mp == 2 and self.dp % 8 == 0
        self.outer = self.dp // 4
        self.z, self.x, self.core = self.index // 4, (self.index // 2) % 2, self.index % 2

    def over_core(self, value):
        return lax.ppermute(value, "dp", [(i, i ^ 1) for i in range(self.dp)])

    def over_x(self, value):
        return lax.ppermute(value, "dp", [(i, i ^ 2) for i in range(self.dp)])

    def over_y(self, value):
        return lax.ppermute(value, "mp", [(0, 1), (1, 0)])

    def along_z(self, value, shift):
        rank = lambda i: ((i // 4 + shift) % self.outer) * 4 + i % 4
        return lax.ppermute(value, "dp", [(i, rank(i)) for i in range(self.dp)])

    def xor_z(self, value, bit):
        return lax.ppermute(value, "dp", [(i, i ^ (4 * bit)) for i in range(self.dp)])


def pick(value, index, axis):
    return lax.dynamic_index_in_dim(value, index, axis, keepdims=False)


def add_low(left, right):
    return (left.astype(F32) + right.astype(F32)).astype(BF)


def assemble_kernel(outer, widths, where_ref, *refs):
    parts, wholes = refs[:8], refs[8:]
    height = parts[0].shape[1]
    z, x, core, y = where_ref[0], where_ref[1], where_ref[2], where_ref[3]
    for place, part in enumerate(parts):
        far_x, far_y, far_core = place & 1, (place >> 1) & 1, place >> 2
        column = y if far_y == 0 else 1 - y
        pair = x if far_x == 0 else 1 - x
        single = core if far_core == 0 else 1 - core
        for slot in range(outer):
            block = lax.rem(z - slot + outer, outer) * 4 + pair * 2 + single
            start = 0
            for whole, width in zip(wholes, widths):
                whole[
                    pl.ds(pl.multiple_of(block * height, 16), height),
                    pl.ds(pl.multiple_of(column * width, LANES), width),
                ] = part[slot, :, start : start + width]
                start += width


def assemble(place, parts, widths):
    outer, height = parts[0].shape[:2]
    where = jnp.stack([place.z, place.x, place.core, place.column]).astype(jnp.int32)
    size = 2 * place.dp * height * sum(widths)
    return pl.pallas_call(
        functools.partial(assemble_kernel, outer, widths),
        in_specs=[pl.BlockSpec(memory_space=pltpu.SMEM)] + [pl.BlockSpec(memory_space=pltpu.VMEM)] * 8,
        out_specs=[pl.BlockSpec(memory_space=pltpu.VMEM)] * len(widths),
        out_shape=[shape_of((place.dp * height, 2 * width), BF) for width in widths],
        compiler_params=params(),
        cost_estimate=cost(0, 4 * size),
        name="assemble",
    )(where, *parts)


def gather_shards(place, shards):
    if not place.direct:
        return [
            lax.all_gather(lax.all_gather(s, "dp", axis=0, tiled=True), "mp", axis=1, tiled=True)
            for s in shards
        ]
    widths = [s.shape[1] for s in shards]
    own = jnp.concatenate(shards, axis=1) if len(shards) > 1 else shards[0]
    line = jnp.stack([own] + [place.along_z(own, shift) for shift in range(1, place.outer)])
    half = place.outer // 2
    by_x, by_y = place.over_x(line), place.over_y(line)
    corner = jnp.concatenate([place.over_y(by_x[:half]), place.over_x(by_y[half:])], axis=0)
    near = [line, by_x, by_y, corner]
    return assemble(place, near + [place.over_core(part) for part in near], widths)


def scatter_sums(place, grad):
    if not place.direct:
        rows = lax.psum_scatter(grad, "dp", scatter_dimension=0, tiled=True)
        return lax.psum_scatter(rows, "mp", scatter_dimension=1, tiled=True).astype(F32)
    outer, half = place.outer, place.outer // 2
    height, wide = grad.shape[0] // place.dp, grad.shape[1]
    width = wide // 2
    blocks = grad.reshape(outer, 2, 2, height, wide)
    mine = add_low(
        pick(blocks, place.core, 2), place.over_core(pick(blocks, 1 - place.core, 2))
    )
    side = lambda value, column: lax.dynamic_slice_in_dim(
        value, column * width, width, value.ndim - 1
    )
    upper, lower = mine[:half], mine[half:]
    upper = add_low(pick(upper, place.x, 1), place.over_x(pick(upper, 1 - place.x, 1)))
    lower = add_low(side(lower, place.column), place.over_y(side(lower, 1 - place.column)))
    upper = add_low(side(upper, place.column), place.over_y(side(upper, 1 - place.column)))
    lower = add_low(pick(lower, place.x, 1), place.over_x(pick(lower, 1 - place.x, 1)))
    line = jnp.concatenate([upper, lower], axis=0)
    total = pick(line, place.z, 0).astype(F32)
    for shift in range(1, outer):
        total = total + place.along_z(
            pick(line, lax.rem(place.z + shift, outer), 0), shift
        ).astype(F32)
    return total


def sum_everywhere(place, value):
    if not place.direct:
        return lax.psum(value, ("dp", "mp"))
    value = value + place.over_core(value)
    value = value + place.over_x(value)
    value = value + place.over_y(value)
    bit = 1
    while bit < place.outer:
        value = value + place.xor_z(value, bit)
        bit *= 2
    return value


def sum_over_dp(place, partial):
    if not place.direct:
        total = lax.psum(partial, "dp").astype(F32)
        return total, jnp.where(place.index == 0, jnp.sum(total * total), 0.0)
    outer = place.outer
    height, wide = partial.shape[0] // place.dp, partial.shape[1]
    blocks = partial.reshape(outer, 2, 2, height, wide)
    mine = add_low(pick(blocks, place.core, 2), place.over_core(pick(blocks, 1 - place.core, 2)))
    mine = add_low(pick(mine, place.x, 1), place.over_x(pick(mine, 1 - place.x, 1)))
    total = pick(mine, place.z, 0).astype(F32)
    for shift in range(1, outer):
        total = total + place.along_z(
            pick(mine, lax.rem(place.z + shift, outer), 0), shift
        ).astype(F32)
    own = total.astype(BF)
    squares = jnp.sum(total * total)
    line = jnp.zeros((outer, height, wide), BF)
    line = lax.dynamic_update_index_in_dim(line, own, place.z, 0)
    for shift in range(1, outer):
        source = lax.rem(place.z - shift + outer, outer)
        line = lax.dynamic_update_index_in_dim(line, place.along_z(own, shift), source, 0)
    other = place.over_x(line)
    both = jnp.where(
        place.x == 0, jnp.stack([line, other], axis=1), jnp.stack([other, line], axis=1)
    )
    other = place.over_core(both)
    every = jnp.where(
        place.core == 0, jnp.stack([both, other], axis=2), jnp.stack([other, both], axis=2)
    )
    return every.reshape(partial.shape), squares


def body(
    kernel_state,
    qkv_state,
    proj_state,
    fc1_state,
    fc2_state,
    table_state,
    patches_s,
    patches_l,
    resize_s,
    resize_l,
    bilin_s,
    bilin_l,
    cotangent,
    rates,
    step,
):
    place = Place()
    low = lambda state: state[0].astype(BF)
    (w_qkv,) = gather_shards(place, [low(qkv_state)])
    w_proj, w_fc1 = gather_shards(place, [low(proj_state), low(fc1_state)])
    (w_fc2,) = gather_shards(place, [low(fc2_state)])

    images, image_rows = patches_l.shape[0], patches_l.shape[1]
    large_rows = images * image_rows // place.mp
    projected, embed_part, kern_part = resize_forward(
        kernel_state, resize_s, resize_l, patches_l.reshape(images * image_rows, -1)
    )
    if place.direct:
        kern = kern_part + place.over_y(kern_part.astype(BF)).astype(F32)
        parts = embed_part.reshape(place.mp, large_rows, -1)
        embed_large = pick(parts, place.column, 0) + place.over_y(pick(parts, 1 - place.column, 0))
    else:
        kern = lax.psum(kern_part, "mp")
        embed_large = lax.psum_scatter(embed_part, "mp", scatter_dimension=0, tiled=True)
    patches_own = pick(patches_s, place.column, 0)
    first_rows = patches_own.shape[0]

    inputs, normed_one = embed(patches_own, kern, embed_large, bilin_s, bilin_l, table_state)
    qkv_rows = product(normed_one, w_qkv, D)
    attended, logs = attend(qkv_rows, first_rows, image_rows)
    middle, normed_two = merge(inputs, attended, w_proj, table_state)
    bias_one = table_state[0, POS_GRID * POS_GRID + 7 :].reshape(1, -1)
    block_out, feed_grad, grad_fc1, grad_fc2, bias_one_grad, bias_two_grad = feed(
        middle, normed_two, cotangent, w_fc1, w_fc2, bias_one, table_state, D
    )
    own_fc1, own_fc2 = scatter_sums(place, grad_fc1), scatter_sums(place, grad_fc2)
    middle_grad, heads_up, grad_proj, middle_rows = merge_back(
        feed_grad, middle, cotangent, attended, w_proj, table_state
    )
    own_proj = scatter_sums(place, grad_proj)
    head_grads = attend_back(qkv_rows, attended, heads_up, logs, first_rows, image_rows)
    grad_qkv, table_grad, large_grad, kern_grad = inputs_back(
        head_grads,
        normed_one,
        w_qkv,
        inputs,
        middle_grad,
        table_state,
        patches_own,
        bilin_s,
        bilin_l,
        middle_rows,
        bias_one_grad,
        bias_two_grad,
        resize_s.shape[0],
    )
    own_qkv = scatter_sums(place, grad_qkv)
    table_total = sum_everywhere(place, table_grad)
    if place.direct:
        other = place.over_y(large_grad)
        large_all = jnp.where(
            place.column == 0,
            jnp.concatenate([large_grad, other], axis=0),
            jnp.concatenate([other, large_grad], axis=0),
        )
        kern_grad = kern_grad + place.over_y(kern_grad)
    else:
        large_all = lax.all_gather(large_grad, "mp", axis=0, tiled=True)
        kern_grad = lax.psum(kern_grad, "mp")
    base_grad, squares = sum_over_dp(place, base_back(projected, large_all, resize_s, kern_grad))

    owned = (own_qkv, own_proj, own_fc1, own_fc2)
    for piece in owned:
        squares = squares + jnp.sum(piece * piece)
    square_total = sum_everywhere(place, jnp.full((8, LANES), squares, F32))[0, 0]
    grad_norm = jnp.sqrt(square_total + jnp.sum(table_total * table_total))
    clip_level = 0.5 * math.sqrt(3 * BASE * BASE * D + 4 * D * D + 2 * D * FF + TROWS * D)
    factor = clip_level / jnp.maximum(grad_norm, clip_level)
    count = step[0].astype(F32)
    fix_one = 1.0 / (1.0 - jnp.power(BETA_ONE, count))
    fix_two = 1.0 / (1.0 - jnp.power(BETA_TWO, count))
    fixed = jnp.stack([factor, fix_one, fix_two])
    blocks = adam(
        jnp.concatenate([fixed, rates[1:]]),
        (qkv_state, proj_state, fc1_state, fc2_state, table_state),
        owned + (table_total,),
        1,
    )
    kernel_new, kernel_moments = adam(
        jnp.concatenate([fixed, rates[:1]]), (kernel_state,), (base_grad,), kernel_state.shape[1] // 64
    )
    return (block_out, grad_norm, kernel_new, kernel_moments, *blocks)


def solution(mesh):
    placed = (
        P(None, "mp", None),
        P(None, "dp", "mp"),
        P(None, "dp", "mp"),
        P(None, "dp", "mp"),
        P(None, "dp", "mp"),
        P(),
        P("dp", None, None),
        P("dp", None, None),
        P(None, "mp"),
        P(None, "mp"),
        P(),
        P(),
        P(("dp", "mp"), None),
        P(),
        P(),
    )
    return jax.shard_map(
        body,
        mesh=mesh,
        in_specs=placed,
        out_specs=(
            P(("dp", "mp"), None),
            P(),
            P("mp", None),
            P(None, "mp", None),
            P("dp", "mp"),
            P(None, "dp", "mp"),
            P("dp", "mp"),
            P(None, "dp", "mp"),
            P("dp", "mp"),
            P(None, "dp", "mp"),
            P("dp", "mp"),
            P(None, "dp", "mp"),
            P(),
            P(),
        ),
        check_vma=False,
    )
```

```python
import functools
import math

import jax
import jax.numpy as jnp
from jax import lax
from jax.experimental import pallas as pl
from jax.experimental.pallas import tpu as pltpu
from jax.sharding import PartitionSpec as P

D = 768
HEADS = 12
HEAD_DIM = 64
FF = 3072
BASE = 32
POS_GRID = 7
GRID_S = 28
GRID_L = 4
TROWS = 60

NORM_EPS = 1e-06
BETA_ONE = 0.5
BETA_TWO = 0.5
DECAY = 0.05
ADAM_EPS = 1e-08
MASKED = -1e30
LOG2E = 1.4426950408889634
LANES = 128
MIB = 2**20

BF = jnp.bfloat16
F32 = jnp.float32
NN = (((1,), (0,)), ((), ()))
NT = (((1,), (1,)), ((), ()))
TN = (((0,), (0,)), ((), ()))


def shape_of(dims, dtype):
    return jax.ShapeDtypeStruct(dims, dtype)


def params(mib=56):
    return pltpu.CompilerParams(vmem_limit_bytes=mib * MIB)


def cost(flops, moved):
    return pl.CostEstimate(flops=int(flops), bytes_accessed=int(moved), transcendentals=0)


def dot(left, right, dims=NN):
    return lax.dot_general(left, right, dims, preferred_element_type=F32)


def run(kernel, operands, out_shape, deps=(), in_specs=None, name=None, micros=1, mib=56, **rest):
    count, skip = len(operands), len(deps)

    def inner(*refs):
        kernel(*refs[:count], *refs[count + skip :])

    if in_specs is None:
        in_specs = [pl.BlockSpec(memory_space=pltpu.VMEM)] * count
    return pl.pallas_call(
        inner,
        in_specs=list(in_specs) + [pl.BlockSpec(memory_space=pl.ANY)] * skip,
        out_shape=out_shape,
        compiler_params=params(mib),
        cost_estimate=cost(micros * 1e8, 0),
        name=name,
        **rest,
    )(*operands, *deps)


def whole(array):
    return pl.BlockSpec(array.shape, lambda *i: (0,) * len(array.shape))


SCALARS = pl.BlockSpec(memory_space=pltpu.SMEM)
INSIDE = pl.BlockSpec(memory_space=pltpu.VMEM)


def first_state(state):
    return pl.BlockSpec((1,) + state.shape[1:], lambda *i: (0, 0, 0))


def halves(value):
    high = value.astype(BF)
    return high, (value - high.astype(F32)).astype(BF)


def dot_fine(left, right, dims=NN):
    left_high, left_low = halves(left)
    right_high, right_low = halves(right)
    return dot(left_high, right_high, dims) + (
        dot(left_high, right_low, dims) + dot(left_low, right_high, dims)
    )


def norm_forward(inputs):
    centered = inputs - jnp.mean(inputs, axis=-1, keepdims=True)
    inverse = lax.rsqrt(jnp.mean(centered * centered, axis=-1, keepdims=True) + NORM_EPS)
    return centered * inverse, inverse


def norm_backward(upstream, normalized, inverse, gain_row):
    scaled = upstream * gain_row
    inner = jnp.mean(scaled * normalized, axis=-1, keepdims=True)
    result = inverse * (scaled - jnp.mean(scaled, axis=-1, keepdims=True) - normalized * inner)
    return (
        result,
        jnp.sum(upstream * normalized, axis=0, keepdims=True),
        jnp.sum(upstream, axis=0, keepdims=True),
    )


def resize_kernel(
    base_ref, small_ref, large_ref, patch_ref, projected_ref, embed_ref, kern_ref, turned, pixels_ref
):
    rows = embed_ref.shape[0]

    @pl.when(pl.program_id(0) == 0)
    def _():
        embed_ref[...] = jnp.zeros_like(embed_ref)
        kern_ref[...] = jnp.zeros_like(kern_ref)
        count = large_ref.shape[0]
        for start in range(0, rows, LANES):
            size = min(LANES, rows - start)
            patch = patch_ref[start : start + size, :].astype(F32)
            if size < LANES:
                patch = jnp.concatenate(
                    [patch, jnp.zeros((LANES - size, patch.shape[1]), F32)], axis=0
                )
            turned[...] = patch.T
            for channel in range(3):
                across = turned[pl.ds(channel, count, stride=3), :].T
                pixels_ref[channel * rows + start : channel * rows + start + size, :] = across[
                    :size
                ].astype(BF)

    base = base_ref[0]
    width = base.shape[1] // 3
    large_high, large_low = halves(large_ref[...])
    pixels = pixels_ref[...]
    projected = dot(pixels, large_high) + dot(pixels, large_low)
    kern_ref[...] += dot_fine(small_ref[...], base)
    total = embed_ref[...]
    for channel in range(3):
        part = projected[channel * rows : (channel + 1) * rows]
        projected_ref[channel] = part.astype(BF)
        total += dot_fine(part, base[:, channel * width : (channel + 1) * width])
    embed_ref[...] = total


def resize_forward(kernel_state, resize_s, resize_l, patches):
    base_rows, wide = kernel_state.shape[1:]
    count = base_rows // LANES
    rows = patches.shape[0]
    columns = 3 * rows
    return pl.pallas_call(
        resize_kernel,
        grid=(count,),
        in_specs=[
            pl.BlockSpec((1, LANES, wide), lambda i: (0, i, 0)),
            pl.BlockSpec((resize_s.shape[0], LANES), lambda i: (0, i)),
            pl.BlockSpec((resize_l.shape[0], LANES), lambda i: (0, i)),
            pl.BlockSpec(patches.shape, lambda i: (0, 0)),
        ],
        out_specs=[
            pl.BlockSpec((3, rows, LANES), lambda i: (0, 0, i)),
            pl.BlockSpec((rows, wide // 3), lambda i: (0, 0)),
            pl.BlockSpec((resize_s.shape[0], wide), lambda i: (0, 0)),
        ],
        out_shape=[
            shape_of((3, rows, base_rows), BF),
            shape_of((rows, wide // 3), F32),
            shape_of((resize_s.shape[0], wide), F32),
        ],
        scratch_shapes=[
            pltpu.VMEM((patches.shape[1], LANES), F32),
            pltpu.VMEM((columns, resize_l.shape[0]), BF),
        ],
        compiler_params=params(),
        cost_estimate=cost(9e8, 0),
        name="resize",
    )(kernel_state, resize_s, resize_l, patches)


def embed_kernel(
    patch_ref, kern_ref, large_ref, bilin_s_ref, bilin_l_ref, table_ref, x_ref, a_ref, woven
):
    table = table_ref[0]
    first = POS_GRID * POS_GRID
    pixels = kern_ref.shape[0]
    width = table.shape[1]
    tiles = width // LANES
    for channel in range(3):
        for tile in range(tiles):
            start = channel * width + tile * LANES
            woven[tile, pl.ds(channel, pixels, stride=3), :] = kern_ref[:, start : start + LANES]
    kern = jnp.concatenate([woven[tile].astype(BF) for tile in range(tiles)], axis=1)
    grid_rows = table[:first]
    bias = table[first : first + 1]
    small = patch_ref.shape[0]
    x_ref[:small, :] = (
        dot(patch_ref[...], kern) + dot_fine(bilin_s_ref[...], grid_rows) + bias
    )
    tokens = bilin_l_ref.shape[0]
    placed = dot_fine(bilin_l_ref[...], grid_rows) + bias
    for image in range(large_ref.shape[0] // tokens):
        part = slice(image * tokens, (image + 1) * tokens)
        x_ref[small + image * tokens : small + (image + 1) * tokens, :] = large_ref[part, :] + placed
    normal, _ = norm_forward(x_ref[...])
    a_ref[...] = (normal * table[first + 1 : first + 2] + table[first + 2 : first + 3]).astype(BF)


def embed(patches, kern, large, bilin_s, bilin_l, table_state):
    rows = patches.shape[0] + large.shape[0]
    width = table_state.shape[2]
    return run(
        embed_kernel,
        (patches, kern, large, bilin_s, bilin_l, table_state),
        [shape_of((rows, width), F32), shape_of((rows, width), BF)],
        (),
        [INSIDE] * 5 + [first_state(table_state)],
        grid=(1,),
        out_specs=[INSIDE] * 2,
        scratch_shapes=[pltpu.VMEM((width // LANES, patches.shape[1], LANES), F32)],
        name="embed",
        micros=5,
    )


def product_kernel(left_ref, right_ref, out_ref):
    out_ref[...] = dot(left_ref[...], right_ref[...]).astype(BF)


def product(left, right, block):
    rows, depth = left.shape
    columns = right.shape[1]
    return pl.pallas_call(
        product_kernel,
        grid=(columns // block,),
        in_specs=[
            pl.BlockSpec((rows, depth), lambda i: (0, 0)),
            pl.BlockSpec((depth, block), lambda i: (0, i)),
        ],
        out_specs=pl.BlockSpec((rows, block), lambda i: (0, i)),
        out_shape=shape_of((rows, columns), BF),
        compiler_params=params(),
        cost_estimate=cost(7e8, 0),
        name="project",
    )(left, right)


def image_features(rows, first_rows, image_rows):
    row = lax.broadcasted_iota(jnp.int32, (rows, LANES), 0)
    lane = lax.broadcasted_iota(jnp.int32, (rows, LANES), 1) % HEAD_DIM
    label = jnp.where(row < first_rows, 0, 1 + (row - first_rows) // image_rows)
    count = 1 + (rows - first_rows) // image_rows
    own = label == lane
    query = jnp.where(own | (lane >= count), 0.0, MASKED).astype(BF)
    return query, jnp.where(own, 1.0, 0.0).astype(BF)


def attend_kernel(first_rows, image_rows, chunks, q_ref, k_ref, v_ref, out_ref, log_ref):
    rows = q_ref.shape[0]
    query_mark, key_mark = image_features(rows, first_rows, image_rows)
    low = lax.broadcasted_iota(jnp.int32, (rows, LANES), 1) < HEAD_DIM
    step = rows // chunks
    queries = q_ref[...] * jnp.asarray(HEAD_DIM**-0.5, BF)
    keys, values = k_ref[...], v_ref[...]
    ones = jnp.ones((rows, LANES), BF)
    results = []
    for head in range(2):
        mine = low if head == 0 else ~low
        query = jnp.where(mine, queries, query_mark)
        key = jnp.where(mine, keys, key_mark)
        value = jnp.where(mine, values, ones)
        outs, logs = [], []
        for chunk in range(chunks):
            scores = dot(query[chunk * step : (chunk + 1) * step], key, NT)
            largest = jnp.max(scores, axis=1, keepdims=True)
            probs = jnp.exp2(scores * LOG2E - largest * LOG2E)
            summed = dot(probs.astype(BF), value)
            rolled = pltpu.roll(summed, HEAD_DIM, 1)
            outs.append(summed / rolled)
            logs.append(largest * LOG2E + jnp.log2(jnp.where(mine[:step], rolled, summed)))
        results.append(jnp.concatenate(outs, axis=0))
        log_ref[0, 8 * head : 8 * head + 8, :] = jnp.concatenate(logs, axis=0).T[:8]
    out_ref[...] = jnp.where(low, results[0], results[1]).astype(BF)


def attend(qkv, first_rows, image_rows, start, count, deps=()):
    rows, wide = qkv.shape
    pairs = wide // 3 // LANES
    chunks = 3 if rows % 48 == 0 else 1
    part = lambda offset: pl.BlockSpec((rows, LANES), lambda i: (0, offset + i))
    return run(
        functools.partial(attend_kernel, first_rows, image_rows, chunks),
        (qkv, qkv, qkv),
        [shape_of((rows, count * LANES), BF), shape_of((count, 16, rows), F32)],
        deps,
        [part(start), part(pairs + start), part(2 * pairs + start)],
        grid=(count,),
        out_specs=[part(0), pl.BlockSpec((1, 16, rows), lambda i: (i, 0, 0))],
        name="attend",
        micros=3 * count,
    )


def merge_kernel(x_ref, w_ref, table_ref, *refs):
    attended, (middle_ref, a_ref) = refs[:-2], refs[-2:]
    first = POS_GRID * POS_GRID
    table = table_ref[0]
    middle = x_ref[...] + table[first + 5 : first + 6]
    start = 0
    for part in attended:
        size = part.shape[1]
        middle = middle + dot(part[...], w_ref[start : start + size, :])
        start += size
    middle_ref[...] = middle
    normal, _ = norm_forward(middle)
    a_ref[...] = (normal * table[first + 3 : first + 4] + table[first + 4 : first + 5]).astype(BF)


def merge(inputs, attended, w_proj, table_state, deps=()):
    rows, width = inputs.shape
    return run(
        merge_kernel,
        (inputs, w_proj, table_state, *attended),
        [shape_of((rows, width), F32), shape_of((rows, width), BF)],
        deps,
        [INSIDE, INSIDE, first_state(table_state)] + [INSIDE] * len(attended),
        grid=(1,),
        out_specs=[INSIDE] * 2,
        name="merge",
        micros=6,
    )


def feed_kernel(
    middle_ref,
    cotangent_ref,
    a_ref,
    w_one_ref,
    w_two_ref,
    bias_ref,
    table_ref,
    out_ref,
    grad_ref,
    g_one_ref,
    g_two_ref,
    b_one_ref,
    b_two_ref,
    turned,
    upstream,
):
    place = pl.program_id(0)

    @pl.when(place == 0)
    def _():
        first = POS_GRID * POS_GRID
        turned[...] = a_ref[...].T
        low = cotangent_ref[...].astype(BF)
        upstream[...] = low
        out_ref[...] = middle_ref[...] + table_ref[0][first + 6 : first + 7]
        grad_ref[...] = jnp.zeros_like(grad_ref)
        b_two_ref[...] = jnp.sum(low.astype(F32), axis=0, keepdims=True)

    w_one, w_two, dz = w_one_ref[...], w_two_ref[...], upstream[...]
    hidden = dot(a_ref[...], w_one) + bias_ref[...]
    phi = 0.5 * (1.0 + lax.erf(hidden * 0.7071067811865476))
    active = (hidden * phi).astype(BF)
    slope = phi + hidden * jnp.exp(-0.5 * hidden * hidden) * 0.3989422804014327
    change = dot(dz, w_two, NT) * slope
    b_one_ref[...] = jnp.sum(change, axis=0, keepdims=True)
    change = change.astype(BF)
    out_ref[...] += dot(active, w_two)
    grad_ref[...] += dot(change, w_one, NT)
    g_one_ref[...] = dot(turned[...], change).astype(BF)
    g_two_ref[...] = dot(active, dz, TN).astype(BF)


def feed(middle, cotangent, normed, w_one, w_two, bias_one, table_state):
    rows, width = normed.shape
    hidden = w_one.shape[1]
    block = D
    across = pl.BlockSpec((width, block), lambda i: (0, i))
    down = pl.BlockSpec((block, width), lambda i: (i, 0))
    line = pl.BlockSpec((1, block), lambda i: (0, i))
    return run(
        feed_kernel,
        (middle, cotangent, normed, w_one, w_two, bias_one, table_state),
        [
            shape_of((rows, width), F32),
            shape_of((rows, width), F32),
            shape_of((width, hidden), BF),
            shape_of((hidden, width), BF),
            shape_of((1, hidden), F32),
            shape_of((1, width), F32),
        ],
        (),
        [INSIDE, INSIDE, INSIDE, across, down, line, first_state(table_state)],
        grid=(hidden // block,),
        out_specs=[INSIDE, INSIDE, across, down, line, INSIDE],
        scratch_shapes=[pltpu.VMEM((width, rows), BF), pltpu.VMEM((rows, width), BF)],
        name="feed",
        micros=9 * (hidden // block),
        mib=60,
    )


def merge_back_kernel(count, grad_ref, middle_ref, cotangent_ref, w_ref, table_ref, *refs):
    attended = refs[:count]
    back_ref, heads_ref, rows_ref, g_ref = refs[count:]
    first = POS_GRID * POS_GRID
    normal, inverse = norm_forward(middle_ref[...])
    change, gain, shift = norm_backward(
        grad_ref[...], normal, inverse, table_ref[0][first + 3 : first + 4]
    )
    back = cotangent_ref[...] + change
    back_ref[...] = back
    low = back.astype(BF)
    heads_ref[...] = dot(low, w_ref[...], NT).astype(BF)
    start = 0
    for part in attended:
        size = part.shape[1]
        g_ref[start : start + size, :] = dot(part[...], low, TN).astype(BF)
        start += size
    rows_ref[0:1, :] = gain
    rows_ref[1:2, :] = shift
    rows_ref[2:3, :] = jnp.sum(low.astype(F32), axis=0, keepdims=True)


def merge_back(grad, middle, cotangent, attended, w_proj, table_state):
    rows, width = middle.shape
    return run(
        functools.partial(merge_back_kernel, len(attended)),
        (grad, middle, cotangent, w_proj, table_state, *attended),
        [
            shape_of((rows, width), F32),
            shape_of((rows, width), BF),
            shape_of((8, width), F32),
            shape_of(w_proj.shape, BF),
        ],
        (),
        [INSIDE, INSIDE, INSIDE, INSIDE, first_state(table_state)] + [INSIDE] * len(attended),
        grid=(1,),
        out_specs=[INSIDE] * 4,
        name="merge_back",
        micros=9,
    )


def attend_back_kernel(
    first_rows, image_rows, chunks, q_ref, k_ref, v_ref, out_ref, up_ref, log_ref, grad_ref
):
    rows = q_ref.shape[0]
    query_mark, key_mark = image_features(rows, first_rows, image_rows)
    low = lax.broadcasted_iota(jnp.int32, (rows, LANES), 1) < HEAD_DIM
    step = rows // chunks
    queries = q_ref[...] * jnp.asarray(HEAD_DIM**-0.5, BF)
    keys, values, up = k_ref[...], v_ref[...], up_ref[...]
    overlap = (out_ref[...].astype(F32) * up.astype(F32)).T
    zeros = jnp.zeros((rows, LANES), BF)
    grads = ([], [], [])
    for head in range(2):
        mine = low if head == 0 else ~low
        query = jnp.where(mine, queries, query_mark)
        key = jnp.where(mine, keys, key_mark)
        value = jnp.where(mine, values, zeros)
        inner = jnp.sum(overlap[HEAD_DIM * head : HEAD_DIM * (head + 1)], axis=0, keepdims=True)
        totals = log_ref[0, 8 * head : 8 * head + 1, :]
        query_grad = jnp.zeros((rows, LANES), F32)
        key_grads, value_grads = [], []
        for chunk in range(chunks):
            part = slice(chunk * step, (chunk + 1) * step)
            scores = dot(key[part], query, NT)
            probs = jnp.exp2(scores * LOG2E - totals)
            value_grads.append(dot(probs.astype(BF), up))
            change = (probs * (dot(value[part], up, NT) - inner)).astype(BF)
            key_grads.append(dot(change, queries))
            query_grad = query_grad + dot(change, keys[part], TN)
        grads[0].append(query_grad * HEAD_DIM**-0.5)
        grads[1].append(jnp.concatenate(key_grads, axis=0))
        grads[2].append(jnp.concatenate(value_grads, axis=0))
    for place, pair in enumerate(grads):
        grad_ref[place] = jnp.where(low, pair[0], pair[1]).astype(BF)


def attend_back(qkv, attended, upstream, logs, first_rows, image_rows, start, deps=()):
    rows, wide = qkv.shape
    pairs, count = wide // 3 // LANES, attended.shape[1] // LANES
    part = lambda offset: pl.BlockSpec((rows, LANES), lambda i: (0, offset + i))
    return run(
        functools.partial(attend_back_kernel, first_rows, image_rows, 1),
        (qkv, qkv, qkv, attended, upstream, logs),
        shape_of((3, rows, count * LANES), BF),
        deps,
        [
            part(start),
            part(pairs + start),
            part(2 * pairs + start),
            part(0),
            part(start),
            pl.BlockSpec((1, 16, rows), lambda i: (i, 0, 0)),
        ],
        grid=(count,),
        out_specs=pl.BlockSpec((3, rows, LANES), lambda i: (0, 0, i)),
        name="attend_back",
        micros=5 * count,
    )


def qkv_grad_kernel(a_ref, *refs):
    turned = a_ref[...].T
    heads, out = refs[:-1], refs[-1]
    start = 0
    for kind in range(3):
        for part in heads:
            size = part.shape[2]
            out[:, start : start + size] = dot(turned, part[kind]).astype(BF)
            start += size


def qkv_grad(normed, heads, deps=()):
    width = normed.shape[1]
    return run(
        qkv_grad_kernel,
        (normed, *heads),
        shape_of((width, 3 * width), BF),
        deps,
        out_specs=INSIDE,
        name="qkv_grad",
        micros=6,
    )


def inputs_back_kernel(
    w_ref,
    x_ref,
    back_ref,
    table_ref,
    patch_ref,
    bilin_s_ref,
    bilin_l_ref,
    middle_rows_ref,
    b_one_ref,
    b_two_ref,
    *refs,
):
    heads, (large_ref, small_ref, woven, small_grad) = refs[:-4], refs[-4:]
    width = x_ref.shape[1]
    total, start = None, 0
    for kind in range(3):
        for part in heads:
            size = part.shape[2]
            value = dot(part[kind], w_ref[:, start : start + size], NT)
            total = value if total is None else total + value
            start += size
    first = POS_GRID * POS_GRID
    normal, inverse = norm_forward(x_ref[...])
    change, gain, shift = norm_backward(total, normal, inverse, table_ref[0][first + 1 : first + 2])
    grad = back_ref[...] + change
    low = grad.astype(BF)
    small = patch_ref.shape[0]
    large_ref[...] = low[small:]
    kern = dot(patch_ref[...], low[:small], TN)
    pixels = kern.shape[0] // 3
    for tile in range(width // LANES):
        woven[tile] = kern[:, tile * LANES : (tile + 1) * LANES]
        for channel in range(3):
            small_grad[
                channel * pixels : (channel + 1) * pixels, tile * LANES : (tile + 1) * LANES
            ] = woven[tile, pl.ds(channel, pixels, stride=3), :]
    table_grad_ref = small_grad.at[3 * pixels :]
    table_grad_ref[...] = jnp.zeros_like(table_grad_ref)
    tokens = bilin_l_ref.shape[0]
    large = grad[small : small + tokens]
    for image in range(1, (grad.shape[0] - small) // tokens):
        large = large + grad[small + image * tokens : small + (image + 1) * tokens]
    table_grad_ref[:first, :] = dot_fine(bilin_s_ref[...], grad[:small], TN) + dot_fine(
        bilin_l_ref[...], large, TN
    )
    table_grad_ref[first : first + 1, :] = jnp.sum(grad, axis=0, keepdims=True)
    table_grad_ref[first + 1 : first + 2, :] = gain
    table_grad_ref[first + 2 : first + 3, :] = shift
    table_grad_ref[first + 3 : first + 6, :] = middle_rows_ref[0:3, :]
    table_grad_ref[first + 6 : first + 7, :] = b_two_ref[...]
    for line in range(b_one_ref.shape[1] // width):
        table_grad_ref[first + 7 + line : first + 8 + line, :] = b_one_ref[
            :, line * width : (line + 1) * width
        ]
    rows = small_grad.shape[0]
    count = width // LANES // 2
    for tile in range(2 * count):
        side, level = divmod(tile, count)
        small_ref[level * rows : (level + 1) * rows, side * LANES : (side + 1) * LANES] = small_grad[
            :, tile * LANES : (tile + 1) * LANES
        ].astype(small_ref.dtype)


def inputs_back(
    heads, w_qkv, inputs, back, table_state, patches, bilin_s, bilin_l, rows_grads, bias_one, bias_two, kind
):
    rows, width = inputs.shape
    large = rows - patches.shape[0]
    operands = (
        w_qkv, inputs, back, table_state, patches, bilin_s, bilin_l, rows_grads, bias_one, bias_two, *heads
    )
    specs = [INSIDE] * len(operands)
    specs[3] = first_state(table_state)
    small = small_rows(patches.shape[1])
    return run(
        inputs_back_kernel,
        operands,
        [shape_of((large, width), BF), shape_of((small * width // LANES // 2, 2 * LANES), kind)],
        (),
        specs,
        grid=(1,),
        out_specs=[INSIDE] * 2,
        scratch_shapes=[
            pltpu.VMEM((width // LANES, patches.shape[1], LANES), F32),
            pltpu.VMEM((small, width), F32),
        ],
        name="inputs_back",
        micros=13,
    )


def small_rows(pixels):
    return -(-(pixels + TROWS) // 256) * 256


def base_back_kernel(projected_ref, large_ref, out_ref):
    width = large_ref.shape[1]
    large = large_ref[...]
    for channel in range(3):
        out_ref[:, channel * width : (channel + 1) * width] = dot(projected_ref[channel], large, TN)


def base_back(projected, large):
    rows, wide = projected.shape[2], 3 * large.shape[1]
    return run(
        base_back_kernel,
        (projected, large),
        shape_of((rows, wide), F32),
        out_specs=INSIDE,
        name="base_back",
        micros=8,
    )


def base_total_kernel(outer, where_ref, part_ref, small_ref, line_ref, out_ref, table_ref, squares_ref, sums):
    pixels = small_ref.shape[0]
    width = part_ref.shape[1] // 3
    count = width // LANES // 2
    height = sums.shape[1] * sums.shape[0] // line_ref.shape[0]
    rows = sums.shape[1] // count
    z, x, core, y = where_ref[0], where_ref[1], where_ref[2], where_ref[3]
    squares = jnp.zeros((1, LANES), F32)
    for place in range(line_ref.shape[0]):
        flip, pair, side, single = z ^ (place % outer), place // outer % 2, place // outer // 2 % 2, place // outer // 4
        block = flip * 4 + (x ^ pair) * 2 + (core ^ single)
        sums[y ^ side, pl.ds(pl.multiple_of(block * height, 8), height), :] = line_ref[place, :height]
    for block in range(line_ref.shape[0]):
        flip, pair, single, side = (block // 8) ^ z, (block // 4 % 2) ^ x, (block // 2 % 2) ^ core, (block % 2) ^ y
        squares = squares + line_ref[((single * 2 + side) * 2 + pair) * outer + flip, height : height + 1]
    squares_ref[1:2, :] = squares
    small = jnp.concatenate(
        [
            sums[tile // count, tile % count * rows : (tile % count + 1) * rows, :]
            for tile in range(2 * count)
        ],
        axis=1,
    )
    table_ref[...] = small[3 * pixels : 3 * pixels + table_ref.shape[0]]
    squares = jnp.zeros((1, LANES), F32)
    for channel in range(3):
        across = slice(channel * width, (channel + 1) * width)
        value = part_ref[:, across] + dot_fine(
            small_ref[...], small[channel * pixels : (channel + 1) * pixels], TN
        )
        out_ref[:, across] = value
        lines = jnp.sum(value * value, axis=0, keepdims=True)
        for start in range(0, width, LANES):
            squares = squares + lines[:, start : start + LANES]
    squares_ref[0:1, :] = squares


def base_total(place, part, resize_s, line, sums_rows):
    return run(
        functools.partial(base_total_kernel, place.outer),
        (place.where, part, resize_s, line),
        [shape_of(part.shape, F32), shape_of((TROWS, part.shape[1] // 3), F32), shape_of((2, LANES), F32)],
        (),
        [SCALARS] + [INSIDE] * 3,
        out_specs=[INSIDE] * 3,
        scratch_shapes=[pltpu.VMEM((2, sums_rows, LANES), F32)],
        name="base_total",
        micros=5,
    )


def adam_values(state, gradient, rate, scalars):
    clipped = gradient * scalars[0]
    first = BETA_ONE * state[1] + (1.0 - BETA_ONE) * clipped
    second = BETA_TWO * state[2] + (1.0 - BETA_TWO) * clipped * clipped
    movement = (first * scalars[1]) / (jnp.sqrt(second * scalars[2]) + ADAM_EPS)
    return state[0] - rate * (movement + DECAY * state[0]), first, second


def adam_kernel(count, scalars_ref, *refs):
    scalars = [scalars_ref[place] for place in range(3)]
    for place in range(count):
        state_ref, gradient_ref = refs[2 * place], refs[2 * place + 1]
        new_ref, moments_ref = refs[2 * count + 2 * place], refs[2 * count + 2 * place + 1]
        new, first, second = adam_values(
            state_ref[...], gradient_ref[...].astype(F32), scalars_ref[3 + place], scalars
        )
        new_ref[...] = new
        moments_ref[0] = first
        moments_ref[1] = second


def adam(scalars, states, gradients, steps):
    in_specs = [pl.BlockSpec(memory_space=pltpu.SMEM)]
    out_specs, out_shapes, operands = [], [], [scalars]
    for state, gradient in zip(states, gradients):
        rows, columns = state.shape[1:]
        part = rows // steps
        in_specs.append(pl.BlockSpec((3, part, columns), lambda i: (0, i, 0)))
        in_specs.append(pl.BlockSpec((part, columns), lambda i: (i, 0)))
        out_specs.append(pl.BlockSpec((part, columns), lambda i: (i, 0)))
        out_specs.append(pl.BlockSpec((2, part, columns), lambda i: (0, i, 0)))
        out_shapes.append(shape_of((rows, columns), F32))
        out_shapes.append(shape_of((2, rows, columns), F32))
        operands += [state, gradient]
    return pl.pallas_call(
        functools.partial(adam_kernel, len(states)),
        grid=(steps,),
        in_specs=in_specs,
        out_specs=out_specs,
        out_shape=out_shapes,
        compiler_params=params(),
        cost_estimate=cost(9e8, 0),
        name="optimizer",
    )(*operands)


class Place:
    def __init__(self):
        self.dp, self.mp = lax.axis_size("dp"), lax.axis_size("mp")
        self.index, self.column = lax.axis_index("dp"), lax.axis_index("mp")
        self.direct = self.mp == 2 and self.dp in (8, 16, 32, 64)
        self.outer = self.dp // 4
        self.z, self.x, self.core = self.index // 4, (self.index // 2) % 2, self.index % 2
        core = self.core if self.direct else jnp.zeros_like(self.core)
        self.where = jnp.stack([self.z, self.x, core, self.column]).astype(jnp.int32)

    def over_core(self, value):
        return lax.ppermute(value, "dp", [(i, i ^ 1) for i in range(self.dp)])

    def over_x(self, value):
        return lax.ppermute(value, "dp", [(i, i ^ 2) for i in range(self.dp)])

    def over_y(self, value):
        return lax.ppermute(value, "mp", [(0, 1), (1, 0)])

    def over_corner(self, value):
        return lax.ppermute(value, ("dp", "mp"), [(i, i ^ 5) for i in range(2 * self.dp)])

    def along_z(self, value, flip):
        return lax.ppermute(value, "dp", [(i, i ^ (4 * flip)) for i in range(self.dp)])


def pick(value, index, axis):
    return lax.dynamic_index_in_dim(value, index, axis, keepdims=False)


def assemble_kernel(outer, plan, where_ref, *refs):
    parts, wholes = refs[:8], refs[8:]
    height = parts[0].shape[1]
    z, x, core, y = where_ref[0], where_ref[1], where_ref[2], where_ref[3]
    for place, part in enumerate(parts):
        far_x, far_y, far_core = place & 1, (place >> 1) & 1, place >> 2
        column = y if far_y == 0 else 1 - y
        pair = x if far_x == 0 else 1 - x
        single = core if far_core == 0 else 1 - core
        for slot in range(outer):
            block = (z ^ slot) * 4 + pair * 2 + single
            for array, start, width, rows, offset in plan:
                wholes[array][
                    pl.ds(pl.multiple_of(block * rows + offset, 16), height),
                    pl.ds(pl.multiple_of(column * width, LANES), width),
                ] = part[slot, :, start : start + width]


def assemble(place, parts, plan, deps=()):
    outer, height = parts[0].shape[:2]
    sizes = {array: (place.dp * rows, 2 * width) for array, _, width, rows, _ in plan}
    return run(
        functools.partial(assemble_kernel, outer, plan),
        (place.where, *parts),
        [shape_of(sizes[array], BF) for array in sorted(sizes)],
        deps,
        [SCALARS] + [INSIDE] * 8,
        out_specs=[INSIDE] * len(sizes),
        name="assemble",
        micros=4,
    )


def assemble_rows_kernel(outer, where_ref, line_ref, out):
    height = line_ref.shape[1]
    z, x, core, y = where_ref[0], where_ref[1], where_ref[2], where_ref[3]
    for place in range(line_ref.shape[0]):
        flip, rest = place % outer, place // outer
        block = (z ^ flip) * 4 + (x ^ (rest & 1)) * 2 + (core ^ (rest >> 2))
        row = pl.multiple_of((block * 2 + (y ^ ((rest >> 1) & 1))) * height, 16)
        out[pl.ds(row, height), :] = line_ref[place]


def assemble_rows(place, line):
    count, height, width = line.shape
    return run(
        functools.partial(assemble_rows_kernel, place.outer),
        (place.where, line),
        shape_of((count * height, width), BF),
        (),
        [SCALARS, INSIDE],
        out_specs=INSIDE,
        name="assemble",
        micros=2,
    )


def behind(value, after):
    return lax.optimization_barrier((value, after))[0]


class Gather:
    def __init__(self, place, own):
        self.place = place
        self.first = [own] + [place.along_z(own, flip) for flip in range(1, place.outer)]

    def sides(self, after=()):
        place = self.place
        self.line = jnp.stack(behind(self.first, after))
        self.by_x, self.by_y = place.over_x(self.line), place.over_y(self.line)

    def corner(self, after=()):
        place, half = self.place, self.place.outer // 2
        by_x, by_y = behind((self.by_x, self.by_y), after)
        self.far = (place.over_y(by_x[:half]), place.over_x(by_y[half:]))
        near = [self.line, self.by_x, self.by_y, jnp.concatenate(self.far, axis=0)]
        self.parts = near + [place.over_core(part) for part in near]


def add_low(left, right):
    return left + right


def first_sum_kernel(plan, where_ref, *refs):
    count = len(plan)
    keeps, comes, outs = refs[:count], refs[count : 2 * count], refs[2 * count :]
    x, core, y = where_ref[1], where_ref[2], where_ref[3]
    height = outs[0].shape[2]
    half = keeps[0].shape[0] // 4
    for keep, come, (width, start) in zip(keeps, comes, plan):
        for piece in range(keep.shape[2] // height):
            down = slice(piece * height, (piece + 1) * height)
            into = slice(start + piece * width, start + (piece + 1) * width)
            for column in range(2):
                across = slice(column * width, (column + 1) * width)
                for level in range(half):
                    for out, value in ((outs[0], x), (outs[1], 1 - x)):
                        at = 2 * level + value
                        out[column, level, :, into] = add_low(
                            keep[at, core, down, across], come[at, down, across]
                        )
            for place in range(2 * half):
                at = 2 * half + place
                for out, value in ((outs[2], y), (outs[3], 1 - y)):
                    across = pl.ds(pl.multiple_of(value * width, LANES), width)
                    out[place, :, into] = add_low(keep[at, core, down, across], come[at, down, across])


def second_sum_kernel(where_ref, *refs):
    x, y = where_ref[1], where_ref[3]
    keep, come, keep_low, come_low, *outs = refs
    for level in range(keep.shape[1]):
        for out, value in ((outs[0], y), (outs[1], 1 - y)):
            out[level] = add_low(keep[value, level], come[value, level])
    for level in range(keep_low.shape[0] // 2):
        for out, value in ((outs[2], x), (outs[3], 1 - x)):
            at = 2 * level + value
            out[level] = add_low(keep_low[at], come_low[at])


def third_sum_kernel(where_ref, *refs):
    line = refs[-1]
    z, outer = where_ref[0], line.shape[0]
    operands, outs = refs[: -1 - outer], refs[-1 - outer : -1]
    start = 0
    for keep, come in zip(operands[0::2], operands[1::2]):
        for level in range(keep.shape[0]):
            line[start + level] = add_low(keep[level], come[level])
        start += keep.shape[0]
    for shift, out in enumerate(outs):
        out[...] = line[z ^ shift]


def last_sum_kernel(wide, more, *refs):
    parts, outs = refs[: len(refs) - 2 - more], refs[len(refs) - 2 - more :]
    total_ref, share_ref = outs[-2:]
    total = parts[0][...].astype(F32)
    for part in parts[1:]:
        total = total + part[...].astype(F32)
    total_ref[...] = total[:, :wide]
    lines = jnp.sum(total[:, :wide] * total[:, :wide], axis=0, keepdims=True)
    squares = lines[:, :LANES]
    for start in range(LANES, wide, LANES):
        squares = squares + lines[:, start : start + LANES]
    if more:
        height = total.shape[0]
        share_ref[:height, :] = total[:, wide:]
        share_ref[height:, :] = jnp.zeros((8, LANES), F32)
        share_ref[height : height + 1, :] = squares + outs[0][...]
    else:
        share_ref[...] = squares


class Scatter:
    def __init__(self, place, grads, height, deps=()):
        self.place = place
        half = place.outer // 2
        keeps = [g.reshape(2 * place.outer, 2, g.shape[0] // place.dp, g.shape[1]) for g in grads]
        comes = [place.over_core(pick(keep, 1 - place.core, 1)) for keep in keeps]
        plan, total = [], 0
        for keep in keeps:
            plan.append((keep.shape[3] // 2, total))
            total += keep.shape[2] // height * keep.shape[3] // 2
        shapes = [shape_of((2, half, height, total), BF)] * 2
        shapes += [shape_of((2 * half, height, total), BF)] * 2
        self.first = self.call(functools.partial(first_sum_kernel, plan), (*keeps, *comes), shapes, deps)
        self.came_first = (place.over_x(self.first[1]), place.over_y(self.first[3]))
        self.size = (height, total)

    def call(self, kernel, operands, shapes, deps=(), name="sum", **rest):
        return run(
            kernel,
            (self.place.where, *operands),
            shapes,
            deps,
            [SCALARS] + [INSIDE] * len(operands),
            out_specs=[INSIDE] * len(shapes),
            name=name,
            micros=2,
            **rest,
        )

    def second(self, deps=()):
        place = self.place
        operands = [v for pair in zip(self.first[0::2], self.came_first) for v in pair]
        shapes = [shape_of((place.outer // 2,) + self.size, BF)] * 4
        self.next = self.call(second_sum_kernel, operands, shapes, deps)
        self.came_second = (place.over_y(self.next[1]), place.over_x(self.next[3]))
        return self.next[1::2]

    def third(self, deps=()):
        place, outer = self.place, self.place.outer
        operands = [v for pair in zip(self.next[0::2], self.came_second) for v in pair]
        lines = self.call(
            third_sum_kernel,
            operands,
            [shape_of(self.size, BF)] * outer,
            deps,
            scratch_shapes=[pltpu.VMEM((outer,) + self.size, BF)],
        )
        self.sent = lines[1:]
        self.lines = [lines[0]] + [
            place.along_z(line, shift) for shift, line in enumerate(lines[1:], start=1)
        ]
        return self.lines

    def last(self, squares=None, deps=()):
        height, wide = self.size
        if squares is None:
            share, more = shape_of((1, LANES), F32), ()
        else:
            wide -= LANES
            share, more = shape_of((height + 8, LANES), F32), (squares,)
        return run(
            functools.partial(last_sum_kernel, wide, len(more)),
            tuple(self.lines) + more,
            [shape_of((height, wide), F32), share],
            deps,
            out_specs=[INSIDE] * 2,
            name="total",
            micros=1,
        )


def spread_share(place, share, after_line=(), after_near=()):
    line = [share] + [place.along_z(share, flip) for flip in range(1, place.outer)]
    line = jnp.stack(behind(line, after_line))
    near = [line, place.over_x(line), place.over_y(line), place.over_corner(line)]
    near = jnp.concatenate(behind(near, after_near), axis=0)
    return jnp.concatenate([near, place.over_core(near)], axis=0)


def scatter_plain(grad):
    rows = lax.psum_scatter(grad, "dp", scatter_dimension=0, tiled=True)
    return lax.psum_scatter(rows, "mp", scatter_dimension=1, tiled=True).astype(F32)


def gather_plain(shard):
    rows = lax.all_gather(shard.astype(BF), "dp", axis=0, tiled=True)
    return lax.all_gather(rows, "mp", axis=1, tiled=True)


def body(
    kernel_state,
    qkv_state,
    proj_state,
    fc1_state,
    fc2_state,
    table_state,
    patches_s,
    patches_l,
    resize_s,
    resize_l,
    bilin_s,
    bilin_l,
    cotangent,
    rates,
    step,
):
    place = Place()
    where, direct = place.where, place.direct
    first = POS_GRID * POS_GRID
    bias_one = table_state[0, first + 7 :].reshape(1, -1)
    low = lambda state: state[0].astype(BF)
    height, wide = qkv_state.shape[1:]
    hidden = fc1_state.shape[2]
    units = fc2_state.shape[1]
    side = proj_state.shape[2]
    if direct:
        pieces = units // height
        first_gather = Gather(place, low(qkv_state))
        first_gather.sides()
        shard = [low(fc1_state)] + list(low(fc2_state).reshape(pieces, height, side)) + [low(proj_state)]
        second_gather = Gather(place, jnp.concatenate(shard, axis=1))
        plan = [(0, 0, hidden, height, 0)]
        plan += [(1, hidden + piece * side, side, units, piece * height) for piece in range(pieces)]
        plan += [(2, hidden + pieces * side, side, height, 0)]

    images, image_rows = patches_l.shape[0], patches_l.shape[1]
    large_rows = images * image_rows // place.mp
    projected, embed_part, kern_part = resize_forward(
        kernel_state, resize_s, resize_l, patches_l.reshape(images * image_rows, -1)
    )
    if direct:
        kern = kern_part + place.over_y(kern_part.astype(BF)).astype(F32)
        parts = embed_part.reshape(place.mp, large_rows, -1)
        embed_large = pick(parts, place.column, 0) + place.over_y(pick(parts, 1 - place.column, 0))
    else:
        kern = lax.psum(kern_part, "mp")
        embed_large = lax.psum_scatter(embed_part, "mp", scatter_dimension=0, tiled=True)
    patches_own = pick(patches_s, place.column, 0)
    first_rows = patches_own.shape[0]
    inputs, normed_one = embed(patches_own, kern, embed_large, bilin_s, bilin_l, table_state)

    if direct:
        first_gather.corner((normed_one, second_gather.first))
        second_gather.sides(first_gather.far)
        (w_qkv,) = assemble(place, first_gather.parts, [(0, 0, wide, height, 0)])
    else:
        w_qkv = gather_plain(qkv_state[0])
    qkv_rows = product(normed_one, w_qkv, D)
    pairs = D // LANES // 2
    attention = []
    for call in range(2):
        waits = (second_gather.line,) if direct and call == 0 else ()
        attention.append(attend(qkv_rows, first_rows, image_rows, call * pairs, pairs, waits))
    attended = [call[0] for call in attention]

    if direct:
        second_gather.corner(attended)
        w_fc1, w_fc2, w_proj = assemble(place, second_gather.parts, plan)
    else:
        w_proj, w_fc1, w_fc2 = [gather_plain(a[0]) for a in (proj_state, fc1_state, fc2_state)]
    middle, normed_two = merge(inputs, attended, w_proj, table_state)
    block_out, back, grad_fc1, grad_fc2, bias_one_grad, bias_two_grad = feed(
        middle, cotangent, normed_two, w_fc1, w_fc2, bias_one, table_state
    )
    middle_grad, heads_up, middle_rows, grad_proj = merge_back(
        back, middle, cotangent, attended, w_proj, table_state
    )
    waits = ()
    if direct:
        scatter_f = Scatter(place, (grad_fc1, grad_fc2, grad_proj), height)
        waits = tuple(scatter_f.first[1::2])
    heads = [
        attend_back(
            qkv_rows, attended[call], heads_up, attention[call][1], first_rows, image_rows,
            call * pairs, waits,
        )
        for call in range(2)
    ]
    large_grad, small_grad = inputs_back(
        heads,
        w_qkv,
        inputs,
        middle_grad,
        table_state,
        patches_own,
        bilin_s,
        bilin_l,
        middle_rows,
        bias_one_grad,
        bias_two_grad,
        BF if direct else F32,
    )
    waits = tuple(scatter_f.second()) if direct else ()
    grad_qkv = qkv_grad(normed_one, heads, waits)
    kern_rows = patches_s.shape[2]
    if direct:
        projected = behind(projected, second_gather.far)
        projected = lax.all_gather(projected, "dp", axis=1, tiled=True)
        scatter_f.third()
        scatter_q = Scatter(place, (grad_qkv, small_grad), height, tuple(scatter_f.sent))
        scatter_q.second()
        large_all = assemble_rows(
            place, spread_share(place, large_grad, scatter_q.first[1::2], scatter_q.next[1::2])
        )
        scatter_q.third()
        own_rest, squares_f = scatter_f.last(None, tuple(scatter_q.sent))
        part = base_back(projected, large_all)
        own_qkv, share = scatter_q.last(squares_f, (part,))
        base_grad, table_total, squares = base_total(
            place, part, resize_s, spread_share(place, share), small_grad.shape[0]
        )
        own_fc2 = jnp.concatenate(
            [own_rest[:, hidden + piece * side : hidden + (piece + 1) * side] for piece in range(pieces)],
            axis=0,
        )
        owned = (own_qkv, own_rest[:, hidden + pieces * side :], own_rest[:, :hidden], own_fc2)
        square_total = jnp.sum(squares[1] + (squares[0] + place.over_y(squares[:1])[0]))
    else:
        large_all = lax.all_gather(large_grad, "mp", axis=0, tiled=True)
        sums = lax.psum(small_grad, ("dp", "mp"))
        sums = sums.reshape(D // LANES // 2, -1, 2, LANES).transpose(1, 2, 0, 3).reshape(-1, D)
        table_total = sums[kern_rows : kern_rows + TROWS]
        part = lax.dot_general(
            resize_s,
            sums[:kern_rows].reshape(3, -1, D).transpose(1, 0, 2).reshape(-1, 3 * D),
            TN,
            precision=lax.Precision.HIGHEST,
            preferred_element_type=F32,
        )
        base_grad = lax.psum(base_back(projected, large_all), "dp") + part
        owned = tuple(scatter_plain(g) for g in (grad_qkv, grad_proj, grad_fc1, grad_fc2))
        squares = sum(jnp.sum(piece * piece) for piece in owned)
        square_total = lax.psum(squares, ("dp", "mp")) + lax.psum(
            jnp.sum(base_grad * base_grad), "mp"
        )
    grad_norm = jnp.sqrt(square_total + jnp.sum(table_total * table_total))
    clip_level = 0.5 * math.sqrt(3 * BASE * BASE * D + 4 * D * D + 2 * D * FF + TROWS * D)
    factor = clip_level / jnp.maximum(grad_norm, clip_level)
    count = step[0].astype(F32)
    fix_one = 1.0 / (1.0 - jnp.power(BETA_ONE, count))
    fix_two = 1.0 / (1.0 - jnp.power(BETA_TWO, count))
    fixed = jnp.stack([factor, fix_one, fix_two])
    blocks = adam(
        jnp.concatenate([fixed, rates[1:]]),
        (qkv_state, proj_state, fc1_state, fc2_state, table_state),
        owned + (table_total,),
        1,
    )
    kernel_new, kernel_moments = adam(
        jnp.concatenate([fixed, rates[:1]]), (kernel_state,), (base_grad,), kernel_state.shape[1] // 64
    )
    return (block_out, grad_norm, kernel_new, kernel_moments, *blocks)


def solution(mesh):
    placed = (
        P(None, "mp", None),
        P(None, "dp", "mp"),
        P(None, "dp", "mp"),
        P(None, "dp", "mp"),
        P(None, "dp", "mp"),
        P(),
        P("dp", None, None),
        P("dp", None, None),
        P(None, "mp"),
        P(None, "mp"),
        P(),
        P(),
        P(("dp", "mp"), None),
        P(),
        P(),
    )
    return jax.shard_map(
        body,
        mesh=mesh,
        in_specs=placed,
        out_specs=(
            P(("dp", "mp"), None),
            P(),
            P("mp", None),
            P(None, "mp", None),
            P("dp", "mp"),
            P(None, "dp", "mp"),
            P("dp", "mp"),
            P(None, "dp", "mp"),
            P("dp", "mp"),
            P(None, "dp", "mp"),
            P("dp", "mp"),
            P(None, "dp", "mp"),
            P(),
            P(),
        ),
        check_vma=False,
    )
```

```python
import functools
import math

import jax
import jax.numpy as jnp
from jax import lax
from jax.experimental import pallas as pl
from jax.experimental.pallas import tpu as pltpu
from jax.sharding import PartitionSpec as P

D = 768
HEADS = 12
HEAD_DIM = 64
FF = 3072
BASE = 32
POS_GRID = 7
GRID_S = 28
GRID_L = 4
TROWS = 60

NORM_EPS = 1e-06
BETA_ONE = 0.5
BETA_TWO = 0.5
DECAY = 0.05
ADAM_EPS = 1e-08
MASKED = -1e30
LOG2E = 1.4426950408889634
LANES = 128
MIB = 2**20

BF = jnp.bfloat16
F32 = jnp.float32
NN = (((1,), (0,)), ((), ()))
NT = (((1,), (1,)), ((), ()))
TN = (((0,), (0,)), ((), ()))


def shape_of(dims, dtype):
    return jax.ShapeDtypeStruct(dims, dtype)


def params(mib=56):
    return pltpu.CompilerParams(vmem_limit_bytes=mib * MIB)


def cost(flops, moved):
    return pl.CostEstimate(flops=int(flops), bytes_accessed=int(moved), transcendentals=0)


def dot(left, right, dims=NN):
    return lax.dot_general(left, right, dims, preferred_element_type=F32)


def run(kernel, operands, out_shape, deps=(), in_specs=None, name=None, micros=1, mib=56, **rest):
    count, skip = len(operands), len(deps)

    def inner(*refs):
        kernel(*refs[:count], *refs[count + skip :])

    if in_specs is None:
        in_specs = [pl.BlockSpec(memory_space=pltpu.VMEM)] * count
    return pl.pallas_call(
        inner,
        in_specs=list(in_specs) + [pl.BlockSpec(memory_space=pl.ANY)] * skip,
        out_shape=out_shape,
        compiler_params=params(mib),
        cost_estimate=cost(micros * 1e7, 0),
        name=name,
        **rest,
    )(*operands, *deps)


def whole(array):
    return pl.BlockSpec(array.shape, lambda *i: (0,) * len(array.shape))


SCALARS = pl.BlockSpec(memory_space=pltpu.SMEM)
INSIDE = pl.BlockSpec(memory_space=pltpu.VMEM)


def first_state(state):
    return pl.BlockSpec((1,) + state.shape[1:], lambda *i: (0, 0, 0))


def halves(value):
    high = value.astype(BF)
    return high, (value - high.astype(F32)).astype(BF)


def dot_fine(left, right, dims=NN):
    left_high, left_low = halves(left)
    right_high, right_low = halves(right)
    return dot(left_high, right_high, dims) + (
        dot(left_high, right_low, dims) + dot(left_low, right_high, dims)
    )


def norm_forward(inputs):
    centered = inputs - jnp.mean(inputs, axis=-1, keepdims=True)
    inverse = lax.rsqrt(jnp.mean(centered * centered, axis=-1, keepdims=True) + NORM_EPS)
    return centered * inverse, inverse


def norm_backward(upstream, normalized, inverse, gain_row):
    scaled = upstream * gain_row
    inner = jnp.mean(scaled * normalized, axis=-1, keepdims=True)
    result = inverse * (scaled - jnp.mean(scaled, axis=-1, keepdims=True) - normalized * inner)
    return (
        result,
        jnp.sum(upstream * normalized, axis=0, keepdims=True),
        jnp.sum(upstream, axis=0, keepdims=True),
    )


def resize_kernel(
    base_ref, small_ref, large_ref, patch_ref, projected_ref, embed_ref, kern_ref, turned, pixels_ref
):
    rows = embed_ref.shape[0]

    @pl.when(pl.program_id(0) == 0)
    def _():
        embed_ref[...] = jnp.zeros_like(embed_ref)
        kern_ref[...] = jnp.zeros_like(kern_ref)
        count = large_ref.shape[0]
        for start in range(0, rows, LANES):
            size = min(LANES, rows - start)
            patch = patch_ref[start : start + size, :].astype(F32)
            if size < LANES:
                patch = jnp.concatenate(
                    [patch, jnp.zeros((LANES - size, patch.shape[1]), F32)], axis=0
                )
            turned[...] = patch.T
            for channel in range(3):
                across = turned[pl.ds(channel, count, stride=3), :].T
                pixels_ref[channel * rows + start : channel * rows + start + size, :] = across[
                    :size
                ].astype(BF)

    base = base_ref[0]
    width = base.shape[1] // 3
    large_high, large_low = halves(large_ref[...])
    pixels = pixels_ref[...]
    projected = dot(pixels, large_high) + dot(pixels, large_low)
    kern_ref[...] += dot_fine(small_ref[...], base)
    total = embed_ref[...]
    for channel in range(3):
        part = projected[channel * rows : (channel + 1) * rows]
        projected_ref[channel] = part.astype(BF)
        total += dot_fine(part, base[:, channel * width : (channel + 1) * width])
    embed_ref[...] = total


def resize_forward(kernel_state, resize_s, resize_l, patches):
    base_rows, wide = kernel_state.shape[1:]
    count = base_rows // LANES
    rows = patches.shape[0]
    columns = 3 * rows
    return pl.pallas_call(
        resize_kernel,
        grid=(count,),
        in_specs=[
            pl.BlockSpec((1, LANES, wide), lambda i: (0, i, 0)),
            pl.BlockSpec((resize_s.shape[0], LANES), lambda i: (0, i)),
            pl.BlockSpec((resize_l.shape[0], LANES), lambda i: (0, i)),
            pl.BlockSpec(patches.shape, lambda i: (0, 0)),
        ],
        out_specs=[
            pl.BlockSpec((3, rows, LANES), lambda i: (0, 0, i)),
            pl.BlockSpec((rows, wide // 3), lambda i: (0, 0)),
            pl.BlockSpec((resize_s.shape[0], wide), lambda i: (0, 0)),
        ],
        out_shape=[
            shape_of((3, rows, base_rows), BF),
            shape_of((rows, wide // 3), F32),
            shape_of((resize_s.shape[0], wide), F32),
        ],
        scratch_shapes=[
            pltpu.VMEM((patches.shape[1], LANES), F32),
            pltpu.VMEM((columns, resize_l.shape[0]), BF),
        ],
        compiler_params=params(),
        cost_estimate=cost(9e7, 0),
        name="resize",
    )(kernel_state, resize_s, resize_l, patches)


def embed_kernel(
    patch_ref, kern_ref, large_ref, bilin_s_ref, bilin_l_ref, table_ref, x_ref, a_ref, woven
):
    table = table_ref[0]
    first = POS_GRID * POS_GRID
    pixels = kern_ref.shape[0]
    width = table.shape[1]
    tiles = width // LANES
    for channel in range(3):
        for tile in range(tiles):
            start = channel * width + tile * LANES
            woven[tile, pl.ds(channel, pixels, stride=3), :] = kern_ref[:, start : start + LANES]
    kern = jnp.concatenate([woven[tile].astype(BF) for tile in range(tiles)], axis=1)
    grid_rows = table[:first]
    bias = table[first : first + 1]
    small = patch_ref.shape[0]
    x_ref[:small, :] = (
        dot(patch_ref[...], kern) + dot_fine(bilin_s_ref[...], grid_rows) + bias
    )
    tokens = bilin_l_ref.shape[0]
    placed = dot_fine(bilin_l_ref[...], grid_rows) + bias
    for image in range(large_ref.shape[0] // tokens):
        part = slice(image * tokens, (image + 1) * tokens)
        x_ref[small + image * tokens : small + (image + 1) * tokens, :] = large_ref[part, :] + placed
    normal, _ = norm_forward(x_ref[...])
    a_ref[...] = (normal * table[first + 1 : first + 2] + table[first + 2 : first + 3]).astype(BF)


def embed(patches, kern, large, bilin_s, bilin_l, table_state):
    rows = patches.shape[0] + large.shape[0]
    width = table_state.shape[2]
    return run(
        embed_kernel,
        (patches, kern, large, bilin_s, bilin_l, table_state),
        [shape_of((rows, width), F32), shape_of((rows, width), BF)],
        (),
        [INSIDE] * 5 + [first_state(table_state)],
        grid=(1,),
        out_specs=[INSIDE] * 2,
        scratch_shapes=[pltpu.VMEM((width // LANES, patches.shape[1], LANES), F32)],
        name="embed",
        mib=20,
        micros=5,
    )


def product_kernel(left_ref, right_ref, out_ref):
    out_ref[...] = dot(left_ref[...], right_ref[...]).astype(BF)


def product(left, right, block):
    rows, depth = left.shape
    columns = right.shape[1]
    return pl.pallas_call(
        product_kernel,
        grid=(columns // block,),
        in_specs=[
            pl.BlockSpec((rows, depth), lambda i: (0, 0)),
            pl.BlockSpec((depth, block), lambda i: (0, i)),
        ],
        out_specs=pl.BlockSpec((rows, block), lambda i: (0, i)),
        out_shape=shape_of((rows, columns), BF),
        compiler_params=params(),
        cost_estimate=cost(7e7, 0),
        name="project",
    )(left, right)


def image_features(rows, first_rows, image_rows):
    row = lax.broadcasted_iota(jnp.int32, (rows, LANES), 0)
    lane = lax.broadcasted_iota(jnp.int32, (rows, LANES), 1) % HEAD_DIM
    label = jnp.where(row < first_rows, 0, 1 + (row - first_rows) // image_rows)
    count = 1 + (rows - first_rows) // image_rows
    own = label == lane
    query = jnp.where(own | (lane >= count), 0.0, MASKED).astype(BF)
    return query, jnp.where(own, 1.0, 0.0).astype(BF)


def attend_kernel(first_rows, image_rows, chunks, q_ref, k_ref, v_ref, out_ref, log_ref):
    rows = q_ref.shape[0]
    query_mark, key_mark = image_features(rows, first_rows, image_rows)
    low = lax.broadcasted_iota(jnp.int32, (rows, LANES), 1) < HEAD_DIM
    step = rows // chunks
    queries = q_ref[...] * jnp.asarray(HEAD_DIM**-0.5, BF)
    keys, values = k_ref[...], v_ref[...]
    ones = jnp.ones((rows, LANES), BF)
    results = []
    for head in range(2):
        mine = low if head == 0 else ~low
        query = jnp.where(mine, queries, query_mark)
        key = jnp.where(mine, keys, key_mark)
        value = jnp.where(mine, values, ones)
        outs, logs = [], []
        for chunk in range(chunks):
            scores = dot(query[chunk * step : (chunk + 1) * step], key, NT)
            largest = jnp.max(scores, axis=1, keepdims=True)
            probs = jnp.exp2(scores * LOG2E - largest * LOG2E)
            summed = dot(probs.astype(BF), value)
            rolled = pltpu.roll(summed, HEAD_DIM, 1)
            outs.append(summed / rolled)
            logs.append(largest * LOG2E + jnp.log2(jnp.where(mine[:step], rolled, summed)))
        results.append(jnp.concatenate(outs, axis=0))
        log_ref[0, 8 * head : 8 * head + 8, :] = jnp.concatenate(logs, axis=0).T[:8]
    out_ref[...] = jnp.where(low, results[0], results[1]).astype(BF)


def attend(qkv, first_rows, image_rows, start, count, deps=()):
    rows, wide = qkv.shape
    pairs = wide // 3 // LANES
    chunks = 3 if rows % 48 == 0 else 1
    part = lambda offset: pl.BlockSpec((rows, LANES), lambda i: (0, offset + i))
    return run(
        functools.partial(attend_kernel, first_rows, image_rows, chunks),
        (qkv, qkv, qkv),
        [shape_of((rows, count * LANES), BF), shape_of((count, 16, rows), F32)],
        deps,
        [part(start), part(pairs + start), part(2 * pairs + start)],
        grid=(count,),
        out_specs=[part(0), pl.BlockSpec((1, 16, rows), lambda i: (i, 0, 0))],
        name="attend",
        mib=20,
        micros=3 * count,
    )


def merge_kernel(x_ref, w_ref, table_ref, *refs):
    attended, (middle_ref, a_ref) = refs[:-2], refs[-2:]
    first = POS_GRID * POS_GRID
    table = table_ref[0]
    middle = x_ref[...] + table[first + 5 : first + 6]
    start = 0
    for part in attended:
        size = part.shape[1]
        middle = middle + dot(part[...], w_ref[start : start + size, :])
        start += size
    middle_ref[...] = middle
    normal, _ = norm_forward(middle)
    a_ref[...] = (normal * table[first + 3 : first + 4] + table[first + 4 : first + 5]).astype(BF)


def merge(inputs, attended, w_proj, table_state, deps=()):
    rows, width = inputs.shape
    return run(
        merge_kernel,
        (inputs, w_proj, table_state, *attended),
        [shape_of((rows, width), F32), shape_of((rows, width), BF)],
        deps,
        [INSIDE, INSIDE, first_state(table_state)] + [INSIDE] * len(attended),
        grid=(1,),
        out_specs=[INSIDE] * 2,
        name="merge",
        mib=20,
        micros=6,
    )


def feed_kernel(
    middle_ref,
    cotangent_ref,
    a_ref,
    w_one_ref,
    w_two_ref,
    bias_ref,
    table_ref,
    out_ref,
    grad_ref,
    g_one_ref,
    g_two_ref,
    b_one_ref,
    b_two_ref,
    turned,
    upstream,
):
    place = pl.program_id(0)

    @pl.when(place == 0)
    def _():
        first = POS_GRID * POS_GRID
        turned[...] = a_ref[...].T
        low = cotangent_ref[...].astype(BF)
        upstream[...] = low
        out_ref[...] = middle_ref[...] + table_ref[0][first + 6 : first + 7]
        grad_ref[...] = jnp.zeros_like(grad_ref)
        b_two_ref[...] = jnp.sum(low.astype(F32), axis=0, keepdims=True)

    w_one, w_two, dz = w_one_ref[...], w_two_ref[...], upstream[...]
    hidden = dot(a_ref[...], w_one) + bias_ref[...]
    phi = 0.5 * (1.0 + lax.erf(hidden * 0.7071067811865476))
    active = (hidden * phi).astype(BF)
    slope = phi + hidden * jnp.exp(-0.5 * hidden * hidden) * 0.3989422804014327
    change = dot(dz, w_two, NT) * slope
    b_one_ref[...] = jnp.sum(change, axis=0, keepdims=True)
    change = change.astype(BF)
    out_ref[...] += dot(active, w_two)
    grad_ref[...] += dot(change, w_one, NT)
    g_one_ref[...] = dot(turned[...], change).astype(BF)
    g_two_ref[...] = dot(active, dz, TN).astype(BF)


def feed(middle, cotangent, normed, w_one, w_two, bias_one, table_state):
    rows, width = normed.shape
    hidden = w_one.shape[1]
    block = D
    across = pl.BlockSpec((width, block), lambda i: (0, i))
    down = pl.BlockSpec((block, width), lambda i: (i, 0))
    line = pl.BlockSpec((1, block), lambda i: (0, i))
    return run(
        feed_kernel,
        (middle, cotangent, normed, w_one, w_two, bias_one, table_state),
        [
            shape_of((rows, width), F32),
            shape_of((rows, width), F32),
            shape_of((width, hidden), BF),
            shape_of((hidden, width), BF),
            shape_of((1, hidden), F32),
            shape_of((1, width), F32),
        ],
        (),
        [INSIDE, INSIDE, INSIDE, across, down, line, first_state(table_state)],
        grid=(hidden // block,),
        out_specs=[INSIDE, INSIDE, across, down, line, INSIDE],
        scratch_shapes=[pltpu.VMEM((width, rows), BF), pltpu.VMEM((rows, width), BF)],
        name="feed",
        mib=44,
        micros=9 * (hidden // block),
    )


def merge_back_kernel(count, grad_ref, middle_ref, cotangent_ref, w_ref, table_ref, *refs):
    attended = refs[:count]
    back_ref, heads_ref, rows_ref, g_ref = refs[count:]
    first = POS_GRID * POS_GRID
    normal, inverse = norm_forward(middle_ref[...])
    change, gain, shift = norm_backward(
        grad_ref[...], normal, inverse, table_ref[0][first + 3 : first + 4]
    )
    back = cotangent_ref[...] + change
    back_ref[...] = back
    low = back.astype(BF)
    heads_ref[...] = dot(low, w_ref[...], NT).astype(BF)
    start = 0
    for part in attended:
        size = part.shape[1]
        g_ref[start : start + size, :] = dot(part[...], low, TN).astype(BF)
        start += size
    rows_ref[0:1, :] = gain
    rows_ref[1:2, :] = shift
    rows_ref[2:3, :] = jnp.sum(low.astype(F32), axis=0, keepdims=True)


def merge_back(grad, middle, cotangent, attended, w_proj, table_state, deps=()):
    rows, width = middle.shape
    return run(
        functools.partial(merge_back_kernel, len(attended)),
        (grad, middle, cotangent, w_proj, table_state, *attended),
        [
            shape_of((rows, width), F32),
            shape_of((rows, width), BF),
            shape_of((8, width), F32),
            shape_of(w_proj.shape, BF),
        ],
        deps,
        [INSIDE, INSIDE, INSIDE, INSIDE, first_state(table_state)] + [INSIDE] * len(attended),
        grid=(1,),
        out_specs=[INSIDE] * 4,
        name="merge_back",
        mib=36,
        micros=9,
    )


def attend_back_kernel(
    first_rows, image_rows, chunks, q_ref, k_ref, v_ref, out_ref, up_ref, log_ref, grad_ref
):
    rows = q_ref.shape[0]
    query_mark, key_mark = image_features(rows, first_rows, image_rows)
    low = lax.broadcasted_iota(jnp.int32, (rows, LANES), 1) < HEAD_DIM
    step = rows // chunks
    queries = q_ref[...] * jnp.asarray(HEAD_DIM**-0.5, BF)
    keys, values, up = k_ref[...], v_ref[...], up_ref[...]
    overlap = (out_ref[...].astype(F32) * up.astype(F32)).T
    zeros = jnp.zeros((rows, LANES), BF)
    grads = ([], [], [])
    for head in range(2):
        mine = low if head == 0 else ~low
        query = jnp.where(mine, queries, query_mark)
        key = jnp.where(mine, keys, key_mark)
        value = jnp.where(mine, values, zeros)
        inner = jnp.sum(overlap[HEAD_DIM * head : HEAD_DIM * (head + 1)], axis=0, keepdims=True)
        totals = log_ref[0, 8 * head : 8 * head + 1, :]
        query_grad = jnp.zeros((rows, LANES), F32)
        key_grads, value_grads = [], []
        for chunk in range(chunks):
            part = slice(chunk * step, (chunk + 1) * step)
            scores = dot(key[part], query, NT)
            probs = jnp.exp2(scores * LOG2E - totals)
            value_grads.append(dot(probs.astype(BF), up))
            change = (probs * (dot(value[part], up, NT) - inner)).astype(BF)
            key_grads.append(dot(change, queries))
            query_grad = query_grad + dot(change, keys[part], TN)
        grads[0].append(query_grad * HEAD_DIM**-0.5)
        grads[1].append(jnp.concatenate(key_grads, axis=0))
        grads[2].append(jnp.concatenate(value_grads, axis=0))
    for place, pair in enumerate(grads):
        grad_ref[place] = jnp.where(low, pair[0], pair[1]).astype(BF)


def attend_back(qkv, attended, upstream, logs, first_rows, image_rows, start, deps=()):
    rows, wide = qkv.shape
    pairs, count = wide // 3 // LANES, attended.shape[1] // LANES
    part = lambda offset: pl.BlockSpec((rows, LANES), lambda i: (0, offset + i))
    return run(
        functools.partial(attend_back_kernel, first_rows, image_rows, 1),
        (qkv, qkv, qkv, attended, upstream, logs),
        shape_of((3, rows, count * LANES), BF),
        deps,
        [
            part(start),
            part(pairs + start),
            part(2 * pairs + start),
            part(0),
            part(start),
            pl.BlockSpec((1, 16, rows), lambda i: (i, 0, 0)),
        ],
        grid=(count,),
        out_specs=pl.BlockSpec((3, rows, LANES), lambda i: (0, 0, i)),
        name="attend_back",
        mib=32,
        micros=5 * count,
    )


def qkv_grad_kernel(a_ref, *refs):
    turned = a_ref[...].T
    heads, out = refs[:-1], refs[-1]
    start = 0
    for kind in range(3):
        for part in heads:
            size = part.shape[2]
            out[:, start : start + size] = dot(turned, part[kind]).astype(BF)
            start += size


def qkv_grad(normed, heads, deps=()):
    width = normed.shape[1]
    return run(
        qkv_grad_kernel,
        (normed, *heads),
        shape_of((width, 3 * width), BF),
        deps,
        out_specs=INSIDE,
        name="qkv_grad",
        mib=20,
        micros=6,
    )


def inputs_back_kernel(
    w_ref,
    x_ref,
    back_ref,
    table_ref,
    patch_ref,
    bilin_s_ref,
    bilin_l_ref,
    middle_rows_ref,
    b_one_ref,
    b_two_ref,
    *refs,
):
    heads, (large_ref, small_ref, woven, small_grad) = refs[:-4], refs[-4:]
    width = x_ref.shape[1]
    total, start = None, 0
    for kind in range(3):
        for part in heads:
            size = part.shape[2]
            value = dot(part[kind], w_ref[:, start : start + size], NT)
            total = value if total is None else total + value
            start += size
    first = POS_GRID * POS_GRID
    normal, inverse = norm_forward(x_ref[...])
    change, gain, shift = norm_backward(total, normal, inverse, table_ref[0][first + 1 : first + 2])
    grad = back_ref[...] + change
    low = grad.astype(BF)
    small = patch_ref.shape[0]
    large_ref[...] = low[small:]
    kern = dot(patch_ref[...], low[:small], TN)
    pixels = kern.shape[0] // 3
    for tile in range(width // LANES):
        woven[tile] = kern[:, tile * LANES : (tile + 1) * LANES]
        for channel in range(3):
            small_grad[
                channel * pixels : (channel + 1) * pixels, tile * LANES : (tile + 1) * LANES
            ] = woven[tile, pl.ds(channel, pixels, stride=3), :]
    table_grad_ref = small_grad.at[3 * pixels :]
    table_grad_ref[...] = jnp.zeros_like(table_grad_ref)
    tokens = bilin_l_ref.shape[0]
    large = grad[small : small + tokens]
    for image in range(1, (grad.shape[0] - small) // tokens):
        large = large + grad[small + image * tokens : small + (image + 1) * tokens]
    table_grad_ref[:first, :] = dot_fine(bilin_s_ref[...], grad[:small], TN) + dot_fine(
        bilin_l_ref[...], large, TN
    )
    table_grad_ref[first : first + 1, :] = jnp.sum(grad, axis=0, keepdims=True)
    table_grad_ref[first + 1 : first + 2, :] = gain
    table_grad_ref[first + 2 : first + 3, :] = shift
    table_grad_ref[first + 3 : first + 6, :] = middle_rows_ref[0:3, :]
    table_grad_ref[first + 6 : first + 7, :] = b_two_ref[...]
    for line in range(b_one_ref.shape[1] // width):
        table_grad_ref[first + 7 + line : first + 8 + line, :] = b_one_ref[
            :, line * width : (line + 1) * width
        ]
    rows = small_grad.shape[0]
    count = width // LANES // 2
    for tile in range(2 * count):
        side, level = divmod(tile, count)
        small_ref[level * rows : (level + 1) * rows, side * LANES : (side + 1) * LANES] = small_grad[
            :, tile * LANES : (tile + 1) * LANES
        ].astype(small_ref.dtype)


def inputs_back(
    heads, w_qkv, inputs, back, table_state, patches, bilin_s, bilin_l, rows_grads, bias_one, bias_two, kind
):
    rows, width = inputs.shape
    large = rows - patches.shape[0]
    operands = (
        w_qkv, inputs, back, table_state, patches, bilin_s, bilin_l, rows_grads, bias_one, bias_two, *heads
    )
    specs = [INSIDE] * len(operands)
    specs[3] = first_state(table_state)
    small = small_rows(patches.shape[1])
    return run(
        inputs_back_kernel,
        operands,
        [shape_of((large, width), BF), shape_of((small * width // LANES // 2, 2 * LANES), kind)],
        (),
        specs,
        grid=(1,),
        out_specs=[INSIDE] * 2,
        scratch_shapes=[
            pltpu.VMEM((width // LANES, patches.shape[1], LANES), F32),
            pltpu.VMEM((small, width), F32),
        ],
        name="inputs_back",
        mib=40,
        micros=13,
    )


def small_rows(pixels):
    return -(-(pixels + TROWS) // 256) * 256


def base_back_kernel(projected_ref, large_ref, out_ref):
    width = large_ref.shape[1]
    large = large_ref[...]
    for channel in range(3):
        out_ref[:, channel * width : (channel + 1) * width] = dot(projected_ref[channel], large, TN)


def base_back(projected, large):
    rows, wide = projected.shape[2], 3 * large.shape[1]
    return run(
        base_back_kernel,
        (projected, large),
        shape_of((rows, wide), F32),
        out_specs=INSIDE,
        name="base_back",
        mib=24,
        micros=8,
    )


def base_all_kernel(outer, where_ref, *refs):
    parts, line_ref, out_ref, projected, large = refs[:4], *refs[4:]
    height = line_ref.shape[1]
    z, x, core, y = where_ref[0], where_ref[1], where_ref[2], where_ref[3]
    for place in range(line_ref.shape[0]):
        flip, pair = z ^ (place % outer), x ^ (place // outer % 2)
        block = flip * 4 + pair * 2 + (core ^ (place // outer // 4))
        row = pl.multiple_of((block * 2 + (y ^ (place // outer // 2 % 2))) * height, 16)
        large[pl.ds(row, height), :] = line_ref[place]
    rows = parts[0].shape[2]
    for place, part in enumerate(parts):
        for flip in range(outer):
            block = (z ^ flip) * 4 + (x ^ (place % 2)) * 2 + (core ^ (place // 2))
            for channel in range(3):
                projected[channel, pl.ds(pl.multiple_of(block * rows, 16), rows), :] = part[flip, channel]
    base_back_kernel(projected, large, out_ref)


def base_all(place, parts, line):
    outer, _, rows, columns = parts[0].shape
    count, height, width = line.shape
    return run(
        functools.partial(base_all_kernel, outer),
        (place.where, *parts, line),
        shape_of((columns, 3 * width), F32),
        (),
        [SCALARS] + [INSIDE] * 5,
        out_specs=INSIDE,
        scratch_shapes=[
            pltpu.VMEM((3, place.dp * rows, columns), BF),
            pltpu.VMEM((count * height, width), BF),
        ],
        name="base_back",
        mib=24,
        micros=8,
    )


def base_total_kernel(outer, where_ref, part_ref, small_ref, line_ref, out_ref, table_ref, squares_ref, sums):
    pixels = small_ref.shape[0]
    width = part_ref.shape[1] // 3
    count = width // LANES // 2
    height = sums.shape[1] * sums.shape[0] // line_ref.shape[0]
    rows = sums.shape[1] // count
    z, x, core, y = where_ref[0], where_ref[1], where_ref[2], where_ref[3]
    squares = jnp.zeros((1, LANES), F32)
    for place in range(line_ref.shape[0]):
        flip, pair, side, single = z ^ (place % outer), place // outer % 2, place // outer // 2 % 2, place // outer // 4
        block = flip * 4 + (x ^ pair) * 2 + (core ^ single)
        sums[y ^ side, pl.ds(pl.multiple_of(block * height, 8), height), :] = line_ref[place, :height]
    for block in range(line_ref.shape[0]):
        flip, pair, single, side = (block // 8) ^ z, (block // 4 % 2) ^ x, (block // 2 % 2) ^ core, (block % 2) ^ y
        squares = squares + line_ref[((single * 2 + side) * 2 + pair) * outer + flip, height : height + 1]
    squares_all = squares
    small = jnp.concatenate(
        [
            sums[tile // count, tile % count * rows : (tile % count + 1) * rows, :]
            for tile in range(2 * count)
        ],
        axis=1,
    )
    table = small[3 * pixels : 3 * pixels + table_ref.shape[0]]
    table_ref[...] = table
    lines = jnp.sum(table * table, axis=0, keepdims=True)
    for start in range(0, width, LANES):
        squares_all = squares_all + lines[:, start : start + LANES]
    squares_ref[1:2, :] = squares_all
    squares = jnp.zeros((1, LANES), F32)
    for channel in range(3):
        across = slice(channel * width, (channel + 1) * width)
        value = part_ref[:, across] + dot_fine(
            small_ref[...], small[channel * pixels : (channel + 1) * pixels], TN
        )
        out_ref[:, across] = value
        lines = jnp.sum(value * value, axis=0, keepdims=True)
        for start in range(0, width, LANES):
            squares = squares + lines[:, start : start + LANES]
    squares_ref[0:1, :] = squares


def base_total(place, part, resize_s, line, sums_rows):
    return run(
        functools.partial(base_total_kernel, place.outer),
        (place.where, part, resize_s, line),
        [shape_of(part.shape, F32), shape_of((TROWS, part.shape[1] // 3), F32), shape_of((2, LANES), F32)],
        (),
        [SCALARS] + [INSIDE] * 3,
        out_specs=[INSIDE] * 3,
        scratch_shapes=[pltpu.VMEM((2, sums_rows, LANES), F32)],
        name="base_total",
        mib=20,
        micros=5,
    )


def adam_kernel(count, squares_count, scalars_ref, *refs):
    squares, refs = refs[:squares_count], refs[squares_count:]
    states, gradients, outs = refs[:count], refs[count : 2 * count], refs[2 * count :]
    norm_ref, outs = outs[0], outs[1:]
    total = sum(jnp.sum(part[...], axis=0, keepdims=True) for part in squares)
    norm = jnp.sqrt(jnp.sum(total, axis=1, keepdims=True))
    clip_level = 0.5 * math.sqrt(3 * BASE * BASE * D + 4 * D * D + 2 * D * FF + TROWS * D)
    factor = clip_level / jnp.maximum(norm, clip_level)
    fix_one, fix_two = scalars_ref[0], scalars_ref[1]

    def update(place, rows):
        state_ref = states[place]
        master, old_first, old_second = [state_ref[entry, rows, :] for entry in range(3)]
        clipped = gradients[place][rows, :] * factor
        first = BETA_ONE * old_first + (1.0 - BETA_ONE) * clipped
        second = BETA_TWO * old_second + (1.0 - BETA_TWO) * clipped * clipped
        movement = (first * fix_one) / (jnp.sqrt(second * fix_two) + ADAM_EPS)
        return master - scalars_ref[2 + place] * (movement + DECAY * master), first, second

    step = pl.program_id(0)
    outs[0][...], outs[1][0], outs[1][1] = update(0, slice(None))

    @pl.when(step == 0)
    def _():
        norm_ref[...] = jnp.broadcast_to(norm, norm_ref.shape)
        for place in range(1, count - 1):
            new, first, second = update(place, slice(None))
            outs[2 * place][...] = new
            outs[2 * place + 1][0] = first
            outs[2 * place + 1][1] = second
        outs[-3][...], outs[-2][...], outs[-1][...] = update(count - 1, slice(None))


def adam(scalars, squares, states, gradients):
    rows, columns = states[0].shape[1:]
    part = min(rows, 64)
    out_specs = [
        INSIDE,
        pl.BlockSpec((part, columns), lambda i: (i, 0)),
        pl.BlockSpec((2, part, columns), lambda i: (0, i, 0)),
    ]
    out_shapes = [shape_of((1, LANES), F32), shape_of((rows, columns), F32), shape_of((2, rows, columns), F32)]
    for state in states[1:-1]:
        out_shapes += [shape_of(state.shape[1:], F32), shape_of((2,) + state.shape[1:], F32)]
    out_shapes += [shape_of(states[-1].shape[1:], F32)] * 3
    out_specs += [INSIDE] * (len(out_shapes) - 3)
    return run(
        functools.partial(adam_kernel, len(states), len(squares)),
        (scalars, *squares, *states, *gradients),
        out_shapes,
        (),
        [SCALARS]
        + [INSIDE] * len(squares)
        + [pl.BlockSpec((3, part, columns), lambda i: (0, i, 0))]
        + [INSIDE] * (len(states) - 1)
        + [pl.BlockSpec((part, columns), lambda i: (i, 0))]
        + [INSIDE] * (len(states) - 1),
        grid=(rows // part,),
        out_specs=out_specs,
        name="optimizer",
        mib=26,
        micros=15,
    )


class Place:
    def __init__(self):
        self.dp, self.mp = lax.axis_size("dp"), lax.axis_size("mp")
        self.index, self.column = lax.axis_index("dp"), lax.axis_index("mp")
        self.direct = self.mp == 2 and self.dp in (8, 16, 32, 64)
        self.outer = self.dp // 4
        self.z, self.x, self.core = self.index // 4, (self.index // 2) % 2, self.index % 2
        core = self.core if self.direct else jnp.zeros_like(self.core)
        self.where = jnp.stack([self.z, self.x, core, self.column]).astype(jnp.int32)

    def over_core(self, value):
        return lax.ppermute(value, "dp", [(i, i ^ 1) for i in range(self.dp)])

    def over_x(self, value):
        return lax.ppermute(value, "dp", [(i, i ^ 2) for i in range(self.dp)])

    def over_y(self, value):
        return lax.ppermute(value, "mp", [(0, 1), (1, 0)])

    def over_corner(self, value):
        return lax.ppermute(value, ("dp", "mp"), [(i, i ^ 5) for i in range(2 * self.dp)])

    def along_z(self, value, flip):
        return lax.ppermute(value, "dp", [(i, i ^ (4 * flip)) for i in range(self.dp)])


def pick(value, index, axis):
    return lax.dynamic_index_in_dim(value, index, axis, keepdims=False)


def assemble_kernel(outer, plan, where_ref, *refs):
    parts, wholes = refs[:8], refs[8:]
    height = parts[0].shape[1]
    z, x, core, y = where_ref[0], where_ref[1], where_ref[2], where_ref[3]
    for place, part in enumerate(parts):
        far_x, far_y, far_core = place & 1, (place >> 1) & 1, place >> 2
        column = y if far_y == 0 else 1 - y
        pair = x if far_x == 0 else 1 - x
        single = core if far_core == 0 else 1 - core
        for slot in range(outer):
            block = (z ^ slot) * 4 + pair * 2 + single
            for array, start, width, rows, offset in plan:
                wholes[array][
                    pl.ds(pl.multiple_of(block * rows + offset, 16), height),
                    pl.ds(pl.multiple_of(column * width, LANES), width),
                ] = part[slot, :, start : start + width]


def assemble(place, parts, plan, deps=()):
    outer, height = parts[0].shape[:2]
    sizes = {array: (place.dp * rows, 2 * width) for array, _, width, rows, _ in plan}
    return run(
        functools.partial(assemble_kernel, outer, plan),
        (place.where, *parts),
        [shape_of(sizes[array], BF) for array in sorted(sizes)],
        deps,
        [SCALARS] + [INSIDE] * 8,
        out_specs=[INSIDE] * len(sizes),
        name="assemble",
        mib=26,
        micros=4,
    )


def behind(value, after):
    return lax.optimization_barrier((value, after))[0]


class Gather:
    def __init__(self, place, own):
        self.place = place
        self.first = [own] + [place.along_z(own, flip) for flip in range(1, place.outer)]

    def sides(self, after=()):
        place = self.place
        self.line = jnp.stack(behind(self.first, after))
        self.by_x, self.by_y = place.over_x(self.line), place.over_y(self.line)

    def corner(self, after=()):
        place, half = self.place, self.place.outer // 2
        by_x, by_y = behind((self.by_x, self.by_y), after)
        self.far = (place.over_y(by_x[:half]), place.over_x(by_y[half:]))
        near = [self.line, self.by_x, self.by_y, jnp.concatenate(self.far, axis=0)]
        self.parts = near + [place.over_core(part) for part in near]


def add_low(left, right):
    return left + right


def first_sum_kernel(plan, where_ref, *refs):
    count = len(plan)
    keeps, comes, outs = refs[:count], refs[count : 2 * count], refs[2 * count :]
    x, core, y = where_ref[1], where_ref[2], where_ref[3]
    height = outs[0].shape[2]
    half = keeps[0].shape[0] // 4
    for keep, come, (width, start) in zip(keeps, comes, plan):
        for piece in range(keep.shape[2] // height):
            down = slice(piece * height, (piece + 1) * height)
            into = slice(start + piece * width, start + (piece + 1) * width)
            for column in range(2):
                across = slice(column * width, (column + 1) * width)
                for level in range(half):
                    for out, value in ((outs[0], x), (outs[1], 1 - x)):
                        at = 2 * level + value
                        out[column, level, :, into] = add_low(
                            keep[at, core, down, across], come[at, down, across]
                        )
            for place in range(2 * half):
                at = 2 * half + place
                for out, value in ((outs[2], y), (outs[3], 1 - y)):
                    across = pl.ds(pl.multiple_of(value * width, LANES), width)
                    out[place, :, into] = add_low(keep[at, core, down, across], come[at, down, across])


def second_sum_kernel(where_ref, *refs):
    x, y = where_ref[1], where_ref[3]
    keep, come, keep_low, come_low, *outs = refs
    for level in range(keep.shape[1]):
        for out, value in ((outs[0], y), (outs[1], 1 - y)):
            out[level] = add_low(keep[value, level], come[value, level])
    for level in range(keep_low.shape[0] // 2):
        for out, value in ((outs[2], x), (outs[3], 1 - x)):
            at = 2 * level + value
            out[level] = add_low(keep_low[at], come_low[at])


def third_sum_kernel(where_ref, *refs):
    line = refs[-1]
    z, outer = where_ref[0], line.shape[0]
    operands, outs = refs[: -1 - outer], refs[-1 - outer : -1]
    start = 0
    for keep, come in zip(operands[0::2], operands[1::2]):
        for level in range(keep.shape[0]):
            line[start + level] = add_low(keep[level], come[level])
        start += keep.shape[0]
    for shift, out in enumerate(outs):
        out[...] = line[z ^ shift]


def last_sum_kernel(wide, more, *refs):
    parts, outs = refs[: len(refs) - 2 - more], refs[len(refs) - 2 - more :]
    total_ref, share_ref = outs[-2:]
    total = parts[0][...].astype(F32)
    for part in parts[1:]:
        total = total + part[...].astype(F32)
    total_ref[...] = total[:, :wide]
    lines = jnp.sum(total[:, :wide] * total[:, :wide], axis=0, keepdims=True)
    squares = lines[:, :LANES]
    for start in range(LANES, wide, LANES):
        squares = squares + lines[:, start : start + LANES]
    if more:
        height = total.shape[0]
        share_ref[:height, :] = total[:, wide:]
        share_ref[height:, :] = jnp.zeros((8, LANES), F32)
        share_ref[height : height + 1, :] = squares + outs[0][...]
    else:
        share_ref[...] = squares


class Scatter:
    def __init__(self, place, grads, height, deps=()):
        self.place = place
        half = place.outer // 2
        keeps = [g.reshape(2 * place.outer, 2, g.shape[0] // place.dp, g.shape[1]) for g in grads]
        comes = [place.over_core(pick(keep, 1 - place.core, 1)) for keep in keeps]
        plan, total = [], 0
        for keep in keeps:
            plan.append((keep.shape[3] // 2, total))
            total += keep.shape[2] // height * keep.shape[3] // 2
        shapes = [shape_of((2, half, height, total), BF)] * 2
        shapes += [shape_of((2 * half, height, total), BF)] * 2
        self.first = self.call(functools.partial(first_sum_kernel, plan), (*keeps, *comes), shapes, deps)
        self.came_first = (place.over_x(self.first[1]), place.over_y(self.first[3]))
        self.size = (height, total)

    def call(self, kernel, operands, shapes, deps=(), name="sum", **rest):
        return run(
            kernel,
            (self.place.where, *operands),
            shapes,
            deps,
            [SCALARS] + [INSIDE] * len(operands),
            out_specs=[INSIDE] * len(shapes),
            name=name,
            micros=2,
            mib=26,
            **rest,
        )

    def second(self, deps=()):
        place = self.place
        operands = [v for pair in zip(self.first[0::2], self.came_first) for v in pair]
        shapes = [shape_of((place.outer // 2,) + self.size, BF)] * 4
        self.next = self.call(second_sum_kernel, operands, shapes, deps)
        self.came_second = (place.over_y(self.next[1]), place.over_x(self.next[3]))
        return self.next[1::2]

    def third(self, deps=()):
        place, outer = self.place, self.place.outer
        operands = [v for pair in zip(self.next[0::2], self.came_second) for v in pair]
        lines = self.call(
            third_sum_kernel,
            operands,
            [shape_of(self.size, BF)] * outer,
            deps,
            scratch_shapes=[pltpu.VMEM((outer,) + self.size, BF)],
        )
        self.sent = lines[1:]
        self.lines = [lines[0]] + [
            place.along_z(line, shift) for shift, line in enumerate(lines[1:], start=1)
        ]
        return self.lines

    def last(self, squares=None, deps=()):
        height, wide = self.size
        if squares is None:
            share, more = shape_of((1, LANES), F32), ()
        else:
            wide -= LANES
            share, more = shape_of((height + 8, LANES), F32), (squares,)
        return run(
            functools.partial(last_sum_kernel, wide, len(more)),
            tuple(self.lines) + more,
            [shape_of((height, wide), F32), share],
            deps,
            out_specs=[INSIDE] * 2,
            name="total",
        mib=8,
            micros=1,
        )


def spread_share(place, share, after_line=(), after_near=()):
    line = [share] + [place.along_z(share, flip) for flip in range(1, place.outer)]
    line = jnp.stack(behind(line, after_line))
    near = [line, place.over_x(line), place.over_y(line), place.over_corner(line)]
    near = jnp.concatenate(behind(near, after_near), axis=0)
    return jnp.concatenate([near, place.over_core(near)], axis=0)


def scatter_plain(grad):
    rows = lax.psum_scatter(grad, "dp", scatter_dimension=0, tiled=True)
    return lax.psum_scatter(rows, "mp", scatter_dimension=1, tiled=True).astype(F32)


def gather_plain(shard):
    rows = lax.all_gather(shard.astype(BF), "dp", axis=0, tiled=True)
    return lax.all_gather(rows, "mp", axis=1, tiled=True)


def body(
    kernel_state,
    qkv_state,
    proj_state,
    fc1_state,
    fc2_state,
    table_state,
    patches_s,
    patches_l,
    resize_s,
    resize_l,
    bilin_s,
    bilin_l,
    cotangent,
    rates,
    step,
):
    place = Place()
    where, direct = place.where, place.direct
    first = POS_GRID * POS_GRID
    bias_one = table_state[0, first + 7 :].reshape(1, -1)
    low = lambda state: state[0].astype(BF)
    height, wide = qkv_state.shape[1:]
    hidden = fc1_state.shape[2]
    units = fc2_state.shape[1]
    side = proj_state.shape[2]
    if direct:
        pieces = units // height
        first_gather = Gather(place, low(qkv_state))
        first_gather.sides()
        shard = [low(fc1_state)] + list(low(fc2_state).reshape(pieces, height, side)) + [low(proj_state)]
        second_gather = Gather(place, jnp.concatenate(shard, axis=1))
        plan = [(0, 0, hidden, height, 0)]
        plan += [(1, hidden + piece * side, side, units, piece * height) for piece in range(pieces)]
        plan += [(2, hidden + pieces * side, side, height, 0)]

    images, image_rows = patches_l.shape[0], patches_l.shape[1]
    large_rows = images * image_rows // place.mp
    projected, embed_part, kern_part = resize_forward(
        kernel_state, resize_s, resize_l, patches_l.reshape(images * image_rows, -1)
    )
    if direct:
        kern = kern_part + place.over_y(kern_part.astype(BF)).astype(F32)
        parts = embed_part.reshape(place.mp, large_rows, -1)
        embed_large = pick(parts, place.column, 0) + place.over_y(pick(parts, 1 - place.column, 0))
    else:
        kern = lax.psum(kern_part, "mp")
        embed_large = lax.psum_scatter(embed_part, "mp", scatter_dimension=0, tiled=True)
    patches_own = pick(patches_s, place.column, 0)
    first_rows = patches_own.shape[0]
    inputs, normed_one = embed(patches_own, kern, embed_large, bilin_s, bilin_l, table_state)

    if direct:
        first_gather.corner((normed_one, second_gather.first))
        second_gather.sides(first_gather.far)
        factors = behind(projected, first_gather.far)
        factors = [factors] + [place.along_z(factors, flip) for flip in range(1, place.outer)]
        (w_qkv,) = assemble(place, first_gather.parts, [(0, 0, wide, height, 0)])
    else:
        w_qkv = gather_plain(qkv_state[0])
    qkv_rows = product(normed_one, w_qkv, D)
    pairs = D // LANES
    attention = []
    for call in range(1):
        waits = (second_gather.line,) if direct and call == 0 else ()
        attention.append(attend(qkv_rows, first_rows, image_rows, call * pairs, pairs, waits))
    attended = [call[0] for call in attention]

    if direct:
        factors = [jnp.stack(behind(factors, attended))]
        second_gather.corner((attended, factors[0]))
        w_fc1, w_fc2, w_proj = assemble(place, second_gather.parts, plan)
    else:
        w_proj, w_fc1, w_fc2 = [gather_plain(a[0]) for a in (proj_state, fc1_state, fc2_state)]
    middle, normed_two = merge(inputs, attended, w_proj, table_state)
    if direct:
        factors.append(place.over_x(behind(factors[0], w_proj)))
    block_out, back, grad_fc1, grad_fc2, bias_one_grad, bias_two_grad = feed(
        middle, cotangent, normed_two, w_fc1, w_fc2, bias_one, table_state
    )
    middle_grad, heads_up, middle_rows, grad_proj = merge_back(
        back, middle, cotangent, attended, w_proj, table_state, ()
    )
    waits = ()
    if direct:
        grads = behind((grad_fc1, grad_fc2), factors[1])
        scatter_f = Scatter(place, (*grads, grad_proj), height)
        factors += [place.over_core(part) for part in behind(factors, back)]
        waits = tuple(scatter_f.first[1::2]) + tuple(factors[2:])
    heads = [
        attend_back(
            qkv_rows, attended[call], heads_up, attention[call][1], first_rows, image_rows,
            call * pairs, waits,
        )
        for call in range(1)
    ]
    large_grad, small_grad = inputs_back(
        heads,
        w_qkv,
        inputs,
        middle_grad,
        table_state,
        patches_own,
        bilin_s,
        bilin_l,
        middle_rows,
        bias_one_grad,
        bias_two_grad,
        BF if direct else F32,
    )
    waits = tuple(scatter_f.second()) if direct else ()
    grad_qkv = qkv_grad(normed_one, heads, waits)
    kern_rows = patches_s.shape[2]
    if direct:
        scatter_f.third()
        scatter_q = Scatter(place, (grad_qkv, small_grad), height, tuple(scatter_f.sent))
        scatter_q.second((scatter_f.lines[1],))
        own_rest, squares_f = scatter_f.last()
        scatter_q.third(tuple(scatter_f.lines[2:]))
        line = spread_share(place, large_grad, scatter_q.first[1::2], scatter_q.sent)
        part = base_all(place, factors, line)
        own_qkv, share = scatter_q.last(squares_f, (part,))
        base_grad, table_total, squares = base_total(
            place, part, resize_s, spread_share(place, share), small_grad.shape[0]
        )
        own_fc2 = jnp.concatenate(
            [own_rest[:, hidden + piece * side : hidden + (piece + 1) * side] for piece in range(pieces)],
            axis=0,
        )
        owned = (own_qkv, own_rest[:, hidden + pieces * side :], own_rest[:, :hidden], own_fc2)
        squares = (squares, place.over_y(squares[:1]))
    else:
        large_all = lax.all_gather(large_grad, "mp", axis=0, tiled=True)
        sums = lax.psum(small_grad, ("dp", "mp"))
        sums = sums.reshape(D // LANES // 2, -1, 2, LANES).transpose(1, 2, 0, 3).reshape(-1, D)
        table_total = sums[kern_rows : kern_rows + TROWS]
        part = lax.dot_general(
            resize_s,
            sums[:kern_rows].reshape(3, -1, D).transpose(1, 0, 2).reshape(-1, 3 * D),
            TN,
            precision=lax.Precision.HIGHEST,
            preferred_element_type=F32,
        )
        base_grad = lax.psum(base_back(projected, large_all), "dp") + part
        owned = tuple(scatter_plain(g) for g in (grad_qkv, grad_proj, grad_fc1, grad_fc2))
        squares = sum(jnp.sum(piece * piece) for piece in owned)
        squares = lax.psum(squares, ("dp", "mp")) + jnp.sum(table_total * table_total)
        squares = squares + lax.psum(jnp.sum(base_grad * base_grad), "mp")
        squares = (jnp.pad(squares.reshape(1, 1), ((0, 0), (0, LANES - 1))),)
    count = step[0].astype(F32)
    fix_one = 1.0 / (1.0 - jnp.power(BETA_ONE, count))
    fix_two = 1.0 / (1.0 - jnp.power(BETA_TWO, count))
    grad_norm, kernel_new, kernel_moments, *blocks = adam(
        jnp.concatenate([jnp.stack([fix_one, fix_two]), rates]),
        squares,
        (kernel_state, qkv_state, proj_state, fc1_state, fc2_state, table_state),
        (base_grad, *owned, table_total),
    )
    grad_norm = grad_norm[0, 0]
    blocks = blocks[:-2] + [jnp.stack(blocks[-2:])]
    return (block_out, grad_norm, kernel_new, kernel_moments, *blocks)


def solution(mesh):
    placed = (
        P(None, "mp", None),
        P(None, "dp", "mp"),
        P(None, "dp", "mp"),
        P(None, "dp", "mp"),
        P(None, "dp", "mp"),
        P(),
        P("dp", None, None),
        P("dp", None, None),
        P(None, "mp"),
        P(None, "mp"),
        P(),
        P(),
        P(("dp", "mp"), None),
        P(),
        P(),
    )
    return jax.shard_map(
        body,
        mesh=mesh,
        in_specs=placed,
        out_specs=(
            P(("dp", "mp"), None),
            P(),
            P("mp", None),
            P(None, "mp", None),
            P("dp", "mp"),
            P(None, "dp", "mp"),
            P("dp", "mp"),
            P(None, "dp", "mp"),
            P("dp", "mp"),
            P(None, "dp", "mp"),
            P("dp", "mp"),
            P(None, "dp", "mp"),
            P(),
            P(),
        ),
        check_vma=False,
    )
```

```python
import functools
import math

import jax
import jax.numpy as jnp
from jax import lax
from jax.experimental import pallas as pl
from jax.experimental.pallas import tpu as pltpu
from jax.sharding import PartitionSpec as P

D = 768
HEADS = 12
HEAD_DIM = 64
FF = 3072
BASE = 32
POS_GRID = 7
GRID_S = 28
GRID_L = 4
TROWS = 60

NORM_EPS = 1e-06
BETA_ONE = 0.5
BETA_TWO = 0.5
DECAY = 0.05
ADAM_EPS = 1e-08
TINY = 1e-37
MASKED = -1e30
LOG2E = 1.4426950408889634
LANES = 128
MIB = 2**20

BF = jnp.bfloat16
F32 = jnp.float32
NN = (((1,), (0,)), ((), ()))
NT = (((1,), (1,)), ((), ()))
TN = (((0,), (0,)), ((), ()))


def shape_of(dims, dtype):
    return jax.ShapeDtypeStruct(dims, dtype)


def params(mib=56):
    return pltpu.CompilerParams(vmem_limit_bytes=mib * MIB)


def cost(flops, moved):
    return pl.CostEstimate(flops=int(flops), bytes_accessed=int(moved), transcendentals=0)


def dot(left, right, dims=NN):
    return lax.dot_general(left, right, dims, preferred_element_type=F32)


def run(kernel, operands, out_shape, deps=(), in_specs=None, name=None, micros=1, mib=56, **rest):
    count, skip = len(operands), len(deps)

    def inner(*refs):
        kernel(*refs[:count], *refs[count + skip :])

    if in_specs is None:
        in_specs = [pl.BlockSpec(memory_space=pltpu.VMEM)] * count
    return pl.pallas_call(
        inner,
        in_specs=list(in_specs) + [pl.BlockSpec(memory_space=pl.ANY)] * skip,
        out_shape=out_shape,
        compiler_params=params(mib),
        cost_estimate=cost(micros * 1e7, 0),
        name=name,
        **rest,
    )(*operands, *deps)


def whole(array):
    return pl.BlockSpec(array.shape, lambda *i: (0,) * len(array.shape))


SCALARS = pl.BlockSpec(memory_space=pltpu.SMEM)
INSIDE = pl.BlockSpec(memory_space=pltpu.VMEM)


def first_state(state):
    return pl.BlockSpec((1,) + state.shape[1:], lambda *i: (0, 0, 0))


def halves(value):
    high = value.astype(BF)
    return high, (value - high.astype(F32)).astype(BF)


def dot_fine(left, right, dims=NN):
    left_high, left_low = halves(left)
    right_high, right_low = halves(right)
    return dot(left_high, right_high, dims) + (
        dot(left_high, right_low, dims) + dot(left_low, right_high, dims)
    )


def norm_forward(inputs):
    centered = inputs - jnp.mean(inputs, axis=-1, keepdims=True)
    inverse = lax.rsqrt(jnp.mean(centered * centered, axis=-1, keepdims=True) + NORM_EPS)
    return centered * inverse, inverse


def norm_backward(upstream, normalized, inverse, gain_row):
    scaled = upstream * gain_row
    inner = jnp.mean(scaled * normalized, axis=-1, keepdims=True)
    result = inverse * (scaled - jnp.mean(scaled, axis=-1, keepdims=True) - normalized * inner)
    return (
        result,
        jnp.sum(upstream * normalized, axis=0, keepdims=True),
        jnp.sum(upstream, axis=0, keepdims=True),
    )


def resize_kernel(
    where_ref,
    base_ref,
    small_ref,
    large_ref,
    patch_ref,
    projected_ref,
    embed_ref,
    kern_ref,
    mine_ref,
    send_ref,
    turned,
    pixels_ref,
):
    rows = embed_ref.shape[0]

    @pl.when(pl.program_id(0) == 0)
    def _():
        embed_ref[...] = jnp.zeros_like(embed_ref)
        kern_ref[...] = jnp.zeros_like(kern_ref)
        count = large_ref.shape[0]
        for start in range(0, rows, LANES):
            size = min(LANES, rows - start)
            patch = patch_ref[start : start + size, :].astype(F32)
            if size < LANES:
                patch = jnp.concatenate(
                    [patch, jnp.zeros((LANES - size, patch.shape[1]), F32)], axis=0
                )
            turned[...] = patch.T
            for channel in range(3):
                across = turned[pl.ds(channel, count, stride=3), :].T
                pixels_ref[channel * rows + start : channel * rows + start + size, :] = across[
                    :size
                ].astype(BF)

    base = base_ref[0]
    width = base.shape[1] // 3
    large_high, large_low = halves(large_ref[...])
    pixels = pixels_ref[...]
    projected = dot(pixels, large_high) + dot(pixels, large_low)
    kern_ref[...] += dot_fine(small_ref[...], base)
    total = embed_ref[...]
    for channel in range(3):
        part = projected[channel * rows : (channel + 1) * rows]
        projected_ref[channel] = part.astype(BF)
        total += dot_fine(part, base[:, channel * width : (channel + 1) * width])
    embed_ref[...] = total

    @pl.when(pl.program_id(0) == pl.num_programs(0) - 1)
    def _():
        part, y = mine_ref.shape[0], where_ref[3]
        mine_ref[...] = embed_ref[pl.ds(pl.multiple_of(y * part, 8), part), :]
        other = embed_ref[pl.ds(pl.multiple_of((1 - y) * part, 8), part), :]
        send_ref[:, : 3 * width] = kern_ref[...].astype(BF)
        if 2 * part == send_ref.shape[0]:
            high, low = halves(other)
            send_ref[:part, 3 * width :] = high
            send_ref[part:, 3 * width :] = low


def resize_forward(where, kernel_state, resize_s, resize_l, patches, parts):
    base_rows, wide = kernel_state.shape[1:]
    count = base_rows // LANES
    rows = patches.shape[0]
    columns = 3 * rows
    shapes = [
        shape_of((3, rows, base_rows), BF),
        shape_of((rows, wide // 3), F32),
        shape_of((resize_s.shape[0], wide), F32),
        shape_of((rows // parts, wide // 3), F32),
        shape_of((resize_s.shape[0], wide + wide // 3), BF),
    ]
    return run(
        resize_kernel,
        (where, kernel_state, resize_s, resize_l, patches),
        shapes,
        (),
        [
            SCALARS,
            pl.BlockSpec((1, LANES, wide), lambda i: (0, i, 0)),
            pl.BlockSpec((resize_s.shape[0], LANES), lambda i: (0, i)),
            pl.BlockSpec((resize_l.shape[0], LANES), lambda i: (0, i)),
            whole(patches),
        ],
        grid=(count,),
        out_specs=[pl.BlockSpec((3, rows, LANES), lambda i: (0, 0, i))]
        + [whole(shape) for shape in shapes[1:]],
        scratch_shapes=[
            pltpu.VMEM((patches.shape[1], LANES), F32),
            pltpu.VMEM((columns, resize_l.shape[0]), BF),
        ],
        name="resize",
        micros=9,
        mib=22,
    )


def embed_kernel(
    patch_ref, kern_ref, large_ref, bilin_s_ref, bilin_l_ref, table_ref, *refs
):
    table = table_ref[0]
    first = POS_GRID * POS_GRID
    pixels = kern_ref.shape[0]
    width = table.shape[1]
    x_ref, a_ref, woven = refs[-3:]
    part = large_ref.shape[0]
    if len(refs) == 4:
        come_ref = refs[0]
        come = come_ref[:, 3 * width :].astype(F32)
        large_part = large_ref[...] + (come[:part] + come[part:])
    else:
        come_ref, large_part = None, large_ref[...]
    tiles = width // LANES
    for channel in range(3):
        for tile in range(tiles):
            start = channel * width + tile * LANES
            value = kern_ref[:, start : start + LANES]
            if come_ref is not None:
                value = value + come_ref[:, start : start + LANES].astype(F32)
            woven[tile, pl.ds(channel, pixels, stride=3), :] = value
    kern = jnp.concatenate([woven[tile].astype(BF) for tile in range(tiles)], axis=1)
    grid_rows = table[:first]
    bias = table[first : first + 1]
    small = patch_ref.shape[0]
    x_ref[:small, :] = (
        dot(patch_ref[...], kern) + dot_fine(bilin_s_ref[...], grid_rows) + bias
    )
    tokens = bilin_l_ref.shape[0]
    placed = dot_fine(bilin_l_ref[...], grid_rows) + bias
    for image in range(large_ref.shape[0] // tokens):
        part = slice(image * tokens, (image + 1) * tokens)
        x_ref[small + image * tokens : small + (image + 1) * tokens, :] = large_part[part] + placed
    normal, _ = norm_forward(x_ref[...])
    a_ref[...] = (normal * table[first + 1 : first + 2] + table[first + 2 : first + 3]).astype(BF)


def embed(patches, kern, large, bilin_s, bilin_l, table_state, come=(), deps=()):
    rows = patches.shape[0] + large.shape[0]
    width = table_state.shape[2]
    return run(
        embed_kernel,
        (patches, kern, large, bilin_s, bilin_l, table_state, *come),
        [shape_of((rows, width), F32), shape_of((rows, width), BF)],
        deps,
        [INSIDE] * 5 + [first_state(table_state)] + [INSIDE] * len(come),
        grid=(1,),
        out_specs=[INSIDE] * 2,
        scratch_shapes=[pltpu.VMEM((width // LANES, patches.shape[1], LANES), F32)],
        name="embed",
        mib=12,
        micros=5,
    )


def product_kernel(left_ref, right_ref, out_ref):
    columns = out_ref.shape[1]
    block = min(columns, D)
    for start in range(0, columns, block):
        across = slice(start, start + block)
        out_ref[:, across] = dot(left_ref[...], right_ref[:, across]).astype(BF)


def product(left, right):
    return run(
        product_kernel,
        (left, right),
        shape_of((left.shape[0], right.shape[1]), BF),
        out_specs=INSIDE,
        name="project",
        micros=7,
        mib=14,
    )


def assemble_product_kernel(outer, plan, where_ref, left_ref, *refs):
    assemble_kernel(outer, plan, where_ref, *refs[:-1])
    product_kernel(left_ref, refs[-2], refs[-1])


def assemble_product(place, left, parts, plan):
    outer, height = parts[0].shape[:2]
    (_, _, width, rows, _) = plan[0]
    shape = (place.dp * rows, 2 * width)
    return run(
        functools.partial(assemble_product_kernel, outer, plan),
        (place.where, left, *parts),
        [shape_of(shape, BF), shape_of((left.shape[0], shape[1]), BF)],
        (),
        [SCALARS] + [INSIDE] * 9,
        out_specs=[INSIDE] * 2,
        name="project",
        micros=8,
        mib=14,
    )


def image_features(rows, first_rows, image_rows):
    row = lax.broadcasted_iota(jnp.int32, (rows, LANES), 0)
    lane = lax.broadcasted_iota(jnp.int32, (rows, LANES), 1) % HEAD_DIM
    label = jnp.where(row < first_rows, 0, 1 + (row - first_rows) // image_rows)
    count = 1 + (rows - first_rows) // image_rows
    own = label == lane
    query = jnp.where(own | (lane >= count), 0.0, MASKED).astype(BF)
    return query, jnp.where(own, 1.0, 0.0).astype(BF)


def attend_kernel(first_rows, image_rows, chunks, q_ref, k_ref, v_ref, out_ref, log_ref):
    rows = q_ref.shape[0]
    query_mark, key_mark = image_features(rows, first_rows, image_rows)
    low = lax.broadcasted_iota(jnp.int32, (rows, LANES), 1) < HEAD_DIM
    step = rows // chunks
    queries = q_ref[...] * jnp.asarray(HEAD_DIM**-0.5, BF)
    keys, values = k_ref[...], v_ref[...]
    ones = jnp.ones((rows, LANES), BF)
    results = []
    for head in range(2):
        mine = low if head == 0 else ~low
        query = jnp.where(mine, queries, query_mark)
        key = jnp.where(mine, keys, key_mark)
        value = jnp.where(mine, values, ones)
        outs, logs = [], []
        for chunk in range(chunks):
            scores = dot(query[chunk * step : (chunk + 1) * step], key, NT)
            largest = jnp.max(scores, axis=1, keepdims=True)
            probs = jnp.exp2(scores * LOG2E - largest * LOG2E)
            summed = dot(probs.astype(BF), value)
            rolled = pltpu.roll(summed, HEAD_DIM, 1)
            outs.append(summed / rolled)
            logs.append(largest * LOG2E + jnp.log2(jnp.where(mine[:step], rolled, summed)))
        results.append(jnp.concatenate(outs, axis=0))
        log_ref[0, 8 * head : 8 * head + 8, :] = jnp.concatenate(logs, axis=0).T[:8]
    out_ref[...] = jnp.where(low, results[0], results[1]).astype(BF)


def attend(qkv, first_rows, image_rows, start, count, deps=()):
    rows, wide = qkv.shape
    pairs = wide // 3 // LANES
    chunks = 3 if rows % 48 == 0 else 1
    part = lambda offset: pl.BlockSpec((rows, LANES), lambda i: (0, offset + i))
    return run(
        functools.partial(attend_kernel, first_rows, image_rows, chunks),
        (qkv, qkv, qkv),
        [shape_of((rows, count * LANES), BF), shape_of((count, 16, rows), F32)],
        deps,
        [part(start), part(pairs + start), part(2 * pairs + start)],
        grid=(count,),
        out_specs=[part(0), pl.BlockSpec((1, 16, rows), lambda i: (i, 0, 0))],
        name="attend",
        mib=12,
        micros=3 * count,
    )


def merge_kernel(x_ref, w_ref, table_ref, *refs):
    attended, (middle_ref, a_ref) = refs[:-2], refs[-2:]
    first = POS_GRID * POS_GRID
    table = table_ref[0]
    middle = x_ref[...] + table[first + 5 : first + 6]
    start = 0
    for part in attended:
        size = part.shape[1]
        middle = middle + dot(part[...], w_ref[start : start + size, :])
        start += size
    middle_ref[...] = middle
    normal, _ = norm_forward(middle)
    a_ref[...] = (normal * table[first + 3 : first + 4] + table[first + 4 : first + 5]).astype(BF)


def merge(inputs, attended, w_proj, table_state, deps=()):
    rows, width = inputs.shape
    return run(
        merge_kernel,
        (inputs, w_proj, table_state, *attended),
        [shape_of((rows, width), F32), shape_of((rows, width), BF)],
        deps,
        [INSIDE, INSIDE, first_state(table_state)] + [INSIDE] * len(attended),
        grid=(1,),
        out_specs=[INSIDE] * 2,
        name="merge",
        mib=12,
        micros=6,
    )


def feed_kernel(
    middle_ref,
    cotangent_ref,
    a_ref,
    w_one_ref,
    w_two_ref,
    bias_ref,
    table_ref,
    out_ref,
    grad_ref,
    g_one_ref,
    g_two_ref,
    b_one_ref,
    b_two_ref,
    turned,
    upstream,
):
    place = pl.program_id(0)

    @pl.when(place == 0)
    def _():
        first = POS_GRID * POS_GRID
        turned[...] = a_ref[...].T
        low = cotangent_ref[...].astype(BF)
        upstream[...] = low
        out_ref[...] = middle_ref[...] + table_ref[0][first + 6 : first + 7]
        grad_ref[...] = jnp.zeros_like(grad_ref)
        b_two_ref[...] = jnp.sum(low.astype(F32), axis=0, keepdims=True)

    w_one, w_two, dz = w_one_ref[...], w_two_ref[...], upstream[...]
    hidden = dot(a_ref[...], w_one) + bias_ref[...]
    phi = 0.5 * (1.0 + lax.erf(hidden * 0.7071067811865476))
    active = (hidden * phi).astype(BF)
    slope = phi + hidden * jnp.exp(-0.5 * hidden * hidden) * 0.3989422804014327
    change = dot(dz, w_two, NT) * slope
    b_one_ref[...] = jnp.sum(change, axis=0, keepdims=True)
    change = change.astype(BF)
    out_ref[...] += dot(active, w_two)
    grad_ref[...] += dot(change, w_one, NT)
    g_one_ref[...] = dot(turned[...], change).astype(BF)
    g_two_ref[...] = dot(active, dz, TN).astype(BF)


def feed(middle, cotangent, normed, w_one, w_two, bias_one, table_state):
    rows, width = normed.shape
    hidden = w_one.shape[1]
    block = D
    across = pl.BlockSpec((width, block), lambda i: (0, i))
    down = pl.BlockSpec((block, width), lambda i: (i, 0))
    line = pl.BlockSpec((1, block), lambda i: (0, i))
    return run(
        feed_kernel,
        (middle, cotangent, normed, w_one, w_two, bias_one, table_state),
        [
            shape_of((rows, width), F32),
            shape_of((rows, width), F32),
            shape_of((width, hidden), BF),
            shape_of((hidden, width), BF),
            shape_of((1, hidden), F32),
            shape_of((1, width), F32),
        ],
        (),
        [INSIDE, INSIDE, INSIDE, across, down, line, first_state(table_state)],
        grid=(hidden // block,),
        out_specs=[INSIDE, INSIDE, across, down, line, INSIDE],
        scratch_shapes=[pltpu.VMEM((width, rows), BF), pltpu.VMEM((rows, width), BF)],
        name="feed",
        mib=28,
        micros=9 * (hidden // block),
    )


def merge_back_kernel(count, grad_ref, middle_ref, cotangent_ref, w_ref, table_ref, *refs):
    attended = refs[:count]
    back_ref, heads_ref, rows_ref, g_ref = refs[count:]
    first = POS_GRID * POS_GRID
    normal, inverse = norm_forward(middle_ref[...])
    change, gain, shift = norm_backward(
        grad_ref[...], normal, inverse, table_ref[0][first + 3 : first + 4]
    )
    back = cotangent_ref[...] + change
    back_ref[...] = back
    low = back.astype(BF)
    heads_ref[...] = dot(low, w_ref[...], NT).astype(BF)
    start = 0
    for part in attended:
        size = part.shape[1]
        g_ref[start : start + size, :] = dot(part[...], low, TN).astype(BF)
        start += size
    rows_ref[0:1, :] = gain
    rows_ref[1:2, :] = shift
    rows_ref[2:3, :] = jnp.sum(low.astype(F32), axis=0, keepdims=True)


def merge_back(grad, middle, cotangent, attended, w_proj, table_state, deps=()):
    rows, width = middle.shape
    return run(
        functools.partial(merge_back_kernel, len(attended)),
        (grad, middle, cotangent, w_proj, table_state, *attended),
        [
            shape_of((rows, width), F32),
            shape_of((rows, width), BF),
            shape_of((8, width), F32),
            shape_of(w_proj.shape, BF),
        ],
        deps,
        [INSIDE, INSIDE, INSIDE, INSIDE, first_state(table_state)] + [INSIDE] * len(attended),
        grid=(1,),
        out_specs=[INSIDE] * 4,
        name="merge_back",
        mib=20,
        micros=9,
    )


def attend_back_kernel(
    first_rows, image_rows, chunks, q_ref, k_ref, v_ref, out_ref, up_ref, log_ref, grad_ref
):
    rows = q_ref.shape[0]
    query_mark, key_mark = image_features(rows, first_rows, image_rows)
    low = lax.broadcasted_iota(jnp.int32, (rows, LANES), 1) < HEAD_DIM
    step = rows // chunks
    queries = q_ref[...] * jnp.asarray(HEAD_DIM**-0.5, BF)
    keys, values, up = k_ref[...], v_ref[...], up_ref[...]
    overlap = (out_ref[...].astype(F32) * up.astype(F32)).T
    zeros = jnp.zeros((rows, LANES), BF)
    grads = ([], [], [])
    for head in range(2):
        mine = low if head == 0 else ~low
        query = jnp.where(mine, queries, query_mark)
        key = jnp.where(mine, keys, key_mark)
        value = jnp.where(mine, values, zeros)
        inner = jnp.sum(overlap[HEAD_DIM * head : HEAD_DIM * (head + 1)], axis=0, keepdims=True)
        totals = log_ref[0, 8 * head : 8 * head + 1, :]
        query_grad = jnp.zeros((rows, LANES), F32)
        key_grads, value_grads = [], []
        for chunk in range(chunks):
            part = slice(chunk * step, (chunk + 1) * step)
            scores = dot(key[part], query, NT)
            probs = jnp.exp2(scores * LOG2E - totals)
            value_grads.append(dot(probs.astype(BF), up))
            change = (probs * (dot(value[part], up, NT) - inner)).astype(BF)
            key_grads.append(dot(change, queries))
            query_grad = query_grad + dot(change, keys[part], TN)
        grads[0].append(query_grad * HEAD_DIM**-0.5)
        grads[1].append(jnp.concatenate(key_grads, axis=0))
        grads[2].append(jnp.concatenate(value_grads, axis=0))
    for place, pair in enumerate(grads):
        grad_ref[place] = jnp.where(low, pair[0], pair[1]).astype(BF)


def attend_back(qkv, attended, upstream, logs, first_rows, image_rows, start, deps=()):
    rows, wide = qkv.shape
    pairs, count = wide // 3 // LANES, attended.shape[1] // LANES
    part = lambda offset: pl.BlockSpec((rows, LANES), lambda i: (0, offset + i))
    return run(
        functools.partial(attend_back_kernel, first_rows, image_rows, 1),
        (qkv, qkv, qkv, attended, upstream, logs),
        shape_of((3, rows, count * LANES), BF),
        deps,
        [
            part(start),
            part(pairs + start),
            part(2 * pairs + start),
            part(0),
            part(start),
            pl.BlockSpec((1, 16, rows), lambda i: (i, 0, 0)),
        ],
        grid=(count,),
        out_specs=pl.BlockSpec((3, rows, LANES), lambda i: (0, 0, i)),
        name="attend_back",
        mib=18,
        micros=5 * count,
    )


def qkv_grad_kernel(a_ref, *refs):
    turned = a_ref[...].T
    heads, out = refs[:-1], refs[-1]
    start = 0
    for kind in range(3):
        for part in heads:
            size = part.shape[2]
            out[:, start : start + size] = dot(turned, part[kind]).astype(BF)
            start += size


def qkv_grad(normed, heads, deps=()):
    width = normed.shape[1]
    return run(
        qkv_grad_kernel,
        (normed, *heads),
        shape_of((width, 3 * width), BF),
        deps,
        out_specs=INSIDE,
        name="qkv_grad",
        mib=12,
        micros=6,
    )


def inputs_back_kernel(
    w_ref,
    x_ref,
    back_ref,
    table_ref,
    patch_ref,
    bilin_s_ref,
    bilin_l_ref,
    middle_rows_ref,
    b_one_ref,
    b_two_ref,
    *refs,
):
    heads, (large_ref, small_ref, woven, small_grad) = refs[:-4], refs[-4:]
    width = x_ref.shape[1]
    total, start = None, 0
    for kind in range(3):
        for part in heads:
            size = part.shape[2]
            value = dot(part[kind], w_ref[:, start : start + size], NT)
            total = value if total is None else total + value
            start += size
    first = POS_GRID * POS_GRID
    normal, inverse = norm_forward(x_ref[...])
    change, gain, shift = norm_backward(total, normal, inverse, table_ref[0][first + 1 : first + 2])
    grad = back_ref[...] + change
    low = grad.astype(BF)
    small = patch_ref.shape[0]
    large_ref[...] = low[small:]
    kern = dot(patch_ref[...], low[:small], TN)
    pixels = kern.shape[0] // 3
    for tile in range(width // LANES):
        woven[tile] = kern[:, tile * LANES : (tile + 1) * LANES]
        for channel in range(3):
            small_grad[
                channel * pixels : (channel + 1) * pixels, tile * LANES : (tile + 1) * LANES
            ] = woven[tile, pl.ds(channel, pixels, stride=3), :]
    table_grad_ref = small_grad.at[3 * pixels :]
    table_grad_ref[...] = jnp.zeros_like(table_grad_ref)
    tokens = bilin_l_ref.shape[0]
    large = grad[small : small + tokens]
    for image in range(1, (grad.shape[0] - small) // tokens):
        large = large + grad[small + image * tokens : small + (image + 1) * tokens]
    table_grad_ref[:first, :] = dot_fine(bilin_s_ref[...], grad[:small], TN) + dot_fine(
        bilin_l_ref[...], large, TN
    )
    table_grad_ref[first : first + 1, :] = jnp.sum(grad, axis=0, keepdims=True)
    table_grad_ref[first + 1 : first + 2, :] = gain
    table_grad_ref[first + 2 : first + 3, :] = shift
    table_grad_ref[first + 3 : first + 6, :] = middle_rows_ref[0:3, :]
    table_grad_ref[first + 6 : first + 7, :] = b_two_ref[...]
    for line in range(b_one_ref.shape[1] // width):
        table_grad_ref[first + 7 + line : first + 8 + line, :] = b_one_ref[
            :, line * width : (line + 1) * width
        ]
    rows = small_grad.shape[0]
    count = width // LANES // 2
    for tile in range(2 * count):
        side, level = divmod(tile, count)
        small_ref[level * rows : (level + 1) * rows, side * LANES : (side + 1) * LANES] = small_grad[
            :, tile * LANES : (tile + 1) * LANES
        ].astype(small_ref.dtype)


def inputs_back(
    heads, w_qkv, inputs, back, table_state, patches, bilin_s, bilin_l, rows_grads, bias_one, bias_two, kind
):
    rows, width = inputs.shape
    large = rows - patches.shape[0]
    operands = (
        w_qkv, inputs, back, table_state, patches, bilin_s, bilin_l, rows_grads, bias_one, bias_two, *heads
    )
    specs = [INSIDE] * len(operands)
    specs[3] = first_state(table_state)
    small = small_rows(patches.shape[1])
    return run(
        inputs_back_kernel,
        operands,
        [shape_of((large, width), BF), shape_of((small * width // LANES // 2, 2 * LANES), kind)],
        (),
        specs,
        grid=(1,),
        out_specs=[INSIDE] * 2,
        scratch_shapes=[
            pltpu.VMEM((width // LANES, patches.shape[1], LANES), F32),
            pltpu.VMEM((small, width), F32),
        ],
        name="inputs_back",
        mib=20,
        micros=13,
    )


def small_rows(pixels):
    return -(-(pixels + TROWS) // 256) * 256


def base_back_kernel(projected_ref, large_ref, out_ref):
    width = large_ref.shape[1]
    large = large_ref[...]
    for channel in range(3):
        out_ref[:, channel * width : (channel + 1) * width] = dot(projected_ref[channel], large, TN)


def base_back(projected, large):
    rows, wide = projected.shape[2], 3 * large.shape[1]
    return run(
        base_back_kernel,
        (projected, large),
        shape_of((rows, wide), F32),
        out_specs=INSIDE,
        name="base_back",
        mib=16,
        micros=8,
    )


def base_all_kernel(outer, where_ref, *refs):
    parts, line_ref, out_ref, projected, large = refs[:4], *refs[4:]
    height = line_ref.shape[1]
    z, x, core, y = where_ref[0], where_ref[1], where_ref[2], where_ref[3]
    for place in range(line_ref.shape[0]):
        flip, pair = z ^ (place % outer), x ^ (place // outer % 2)
        block = flip * 4 + pair * 2 + (core ^ (place // outer // 4))
        row = pl.multiple_of((block * 2 + (y ^ (place // outer // 2 % 2))) * height, 16)
        large[pl.ds(row, height), :] = line_ref[place]
    rows = parts[0].shape[2]
    for place, part in enumerate(parts):
        for flip in range(outer):
            block = (z ^ flip) * 4 + (x ^ (place % 2)) * 2 + (core ^ (place // 2))
            for channel in range(3):
                projected[channel, pl.ds(pl.multiple_of(block * rows, 16), rows), :] = part[flip, channel]
    base_back_kernel(projected, large, out_ref)


def base_all(place, parts, line):
    outer, _, rows, columns = parts[0].shape
    count, height, width = line.shape
    return run(
        functools.partial(base_all_kernel, outer),
        (place.where, *parts, line),
        shape_of((columns, 3 * width), F32),
        (),
        [SCALARS] + [INSIDE] * 5,
        out_specs=INSIDE,
        scratch_shapes=[
            pltpu.VMEM((3, place.dp * rows, columns), BF),
            pltpu.VMEM((count * height, width), BF),
        ],
        name="base_back",
        mib=16,
        micros=8,
    )


def base_total_kernel(outer, where_ref, part_ref, small_ref, line_ref, out_ref, table_ref, squares_ref, sums):
    pixels = small_ref.shape[0]
    width = part_ref.shape[1] // 3
    count = width // LANES // 2
    height = sums.shape[1] * sums.shape[0] // line_ref.shape[0]
    rows = sums.shape[1] // count
    z, x, core, y = where_ref[0], where_ref[1], where_ref[2], where_ref[3]
    squares = jnp.zeros((1, LANES), F32)
    for place in range(line_ref.shape[0]):
        flip, pair, side, single = z ^ (place % outer), place // outer % 2, place // outer // 2 % 2, place // outer // 4
        block = flip * 4 + (x ^ pair) * 2 + (core ^ single)
        sums[y ^ side, pl.ds(pl.multiple_of(block * height, 8), height), :] = line_ref[place, :height]
    for block in range(line_ref.shape[0]):
        flip, pair, single, side = (block // 8) ^ z, (block // 4 % 2) ^ x, (block // 2 % 2) ^ core, (block % 2) ^ y
        squares = squares + line_ref[((single * 2 + side) * 2 + pair) * outer + flip, height : height + 1]
    squares_all = squares
    small = jnp.concatenate(
        [
            sums[tile // count, tile % count * rows : (tile % count + 1) * rows, :]
            for tile in range(2 * count)
        ],
        axis=1,
    )
    table = small[3 * pixels : 3 * pixels + table_ref.shape[0]]
    table_ref[...] = table
    lines = jnp.sum(table * table, axis=0, keepdims=True)
    for start in range(0, width, LANES):
        squares_all = squares_all + lines[:, start : start + LANES]
    squares_ref[1:2, :] = squares_all
    squares = jnp.zeros((1, LANES), F32)
    for channel in range(3):
        across = slice(channel * width, (channel + 1) * width)
        value = part_ref[:, across] + dot_fine(
            small_ref[...], small[channel * pixels : (channel + 1) * pixels], TN
        )
        out_ref[:, across] = value
        lines = jnp.sum(value * value, axis=0, keepdims=True)
        for start in range(0, width, LANES):
            squares = squares + lines[:, start : start + LANES]
    squares_ref[0:1, :] = squares


def base_total(place, part, resize_s, line, sums_rows):
    return run(
        functools.partial(base_total_kernel, place.outer),
        (place.where, part, resize_s, line),
        [shape_of(part.shape, F32), shape_of((TROWS, part.shape[1] // 3), F32), shape_of((2, LANES), F32)],
        (),
        [SCALARS] + [INSIDE] * 3,
        out_specs=[INSIDE] * 3,
        scratch_shapes=[pltpu.VMEM((2, sums_rows, LANES), F32)],
        name="base_total",
        mib=12,
        micros=5,
    )


def adam_kernel(count, squares_count, scalars_ref, *refs):
    squares, refs = refs[:squares_count], refs[squares_count:]
    states, gradients, outs = refs[:count], refs[count : 2 * count], refs[2 * count :]
    norm_ref, outs = outs[0], outs[1:]
    total = sum(jnp.sum(part[...], axis=0, keepdims=True) for part in squares)
    norm = jnp.sqrt(jnp.sum(total, axis=1, keepdims=True))
    clip_level = 0.5 * math.sqrt(3 * BASE * BASE * D + 4 * D * D + 2 * D * FF + TROWS * D)
    factor = clip_level / jnp.maximum(norm, clip_level)
    fix_one, fix_two = scalars_ref[0], scalars_ref[1]

    def update(place, rows):
        state_ref = states[place]
        master, old_first, old_second = [state_ref[entry, rows, :] for entry in range(3)]
        clipped = gradients[place][rows, :] * factor
        first = BETA_ONE * (old_first + clipped)
        second = BETA_TWO * (old_second + clipped * clipped)
        square = second * fix_two
        below = square * lax.rsqrt(jnp.maximum(square, TINY)) + ADAM_EPS
        guess = pl.reciprocal(below, approx=True)
        guess = guess * (2.0 - below * guess)
        rate = scalars_ref[2 + place]
        new = master * (1.0 - rate * DECAY) - (first * guess) * (rate * fix_one)
        return new, first, second

    step = pl.program_id(0)
    outs[0][...], outs[1][0], outs[1][1] = update(0, slice(None))

    @pl.when(step == 0)
    def _():
        norm_ref[...] = jnp.broadcast_to(norm, norm_ref.shape)
        for place in range(1, count - 1):
            new, first, second = update(place, slice(None))
            outs[2 * place][...] = new
            outs[2 * place + 1][0] = first
            outs[2 * place + 1][1] = second
        outs[-3][...], outs[-2][...], outs[-1][...] = update(count - 1, slice(None))


def adam(scalars, squares, states, gradients):
    rows, columns = states[0].shape[1:]
    part = min(rows, 64)
    out_specs = [
        INSIDE,
        pl.BlockSpec((part, columns), lambda i: (i, 0)),
        pl.BlockSpec((2, part, columns), lambda i: (0, i, 0)),
    ]
    out_shapes = [shape_of((1, LANES), F32), shape_of((rows, columns), F32), shape_of((2, rows, columns), F32)]
    for state in states[1:-1]:
        out_shapes += [shape_of(state.shape[1:], F32), shape_of((2,) + state.shape[1:], F32)]
    out_shapes += [shape_of(states[-1].shape[1:], F32)] * 3
    out_specs += [INSIDE] * (len(out_shapes) - 3)
    return run(
        functools.partial(adam_kernel, len(states), len(squares)),
        (scalars, *squares, *states, *gradients),
        out_shapes,
        (),
        [SCALARS]
        + [INSIDE] * len(squares)
        + [pl.BlockSpec((3, part, columns), lambda i: (0, i, 0))]
        + [INSIDE] * (len(states) - 1)
        + [pl.BlockSpec((part, columns), lambda i: (i, 0))]
        + [INSIDE] * (len(states) - 1),
        grid=(rows // part,),
        out_specs=out_specs,
        name="optimizer",
        mib=18,
        micros=15,
    )


class Place:
    def __init__(self):
        self.dp, self.mp = lax.axis_size("dp"), lax.axis_size("mp")
        self.index, self.column = lax.axis_index("dp"), lax.axis_index("mp")
        self.direct = self.mp == 2 and self.dp in (8, 16, 32, 64)
        self.outer = self.dp // 4
        self.z, self.x, self.core = self.index // 4, (self.index // 2) % 2, self.index % 2
        core = self.core if self.direct else jnp.zeros_like(self.core)
        self.where = jnp.stack([self.z, self.x, core, self.column]).astype(jnp.int32)

    def over_core(self, value):
        return lax.ppermute(value, "dp", [(i, i ^ 1) for i in range(self.dp)])

    def over_x(self, value):
        return lax.ppermute(value, "dp", [(i, i ^ 2) for i in range(self.dp)])

    def over_y(self, value):
        return lax.ppermute(value, "mp", [(0, 1), (1, 0)])

    def over_corner(self, value):
        return lax.ppermute(value, ("dp", "mp"), [(i, i ^ 5) for i in range(2 * self.dp)])

    def along_z(self, value, flip):
        return lax.ppermute(value, "dp", [(i, i ^ (4 * flip)) for i in range(self.dp)])


def pick(value, index, axis):
    return lax.dynamic_index_in_dim(value, index, axis, keepdims=False)


def assemble_kernel(outer, plan, where_ref, *refs):
    parts, wholes = refs[:8], refs[8:]
    height = parts[0].shape[1]
    z, x, core, y = where_ref[0], where_ref[1], where_ref[2], where_ref[3]
    for place, part in enumerate(parts):
        far_x, far_y, far_core = place & 1, (place >> 1) & 1, place >> 2
        column = y if far_y == 0 else 1 - y
        pair = x if far_x == 0 else 1 - x
        single = core if far_core == 0 else 1 - core
        for slot in range(outer):
            block = (z ^ slot) * 4 + pair * 2 + single
            for array, start, width, rows, offset in plan:
                wholes[array][
                    pl.ds(pl.multiple_of(block * rows + offset, 16), height),
                    pl.ds(pl.multiple_of(column * width, LANES), width),
                ] = part[slot, :, start : start + width]


def assemble(place, parts, plan, deps=()):
    outer, height = parts[0].shape[:2]
    sizes = {array: (place.dp * rows, 2 * width) for array, _, width, rows, _ in plan}
    return run(
        functools.partial(assemble_kernel, outer, plan),
        (place.where, *parts),
        [shape_of(sizes[array], BF) for array in sorted(sizes)],
        deps,
        [SCALARS] + [INSIDE] * 8,
        out_specs=[INSIDE] * len(sizes),
        name="assemble",
        mib=14,
        micros=4,
    )


def behind(value, after):
    return lax.optimization_barrier((value, after))[0]


class Gather:
    def __init__(self, place, own):
        self.place = place
        self.first = [own] + [place.along_z(own, flip) for flip in range(1, place.outer)]

    def sides(self, after=()):
        place = self.place
        self.line = jnp.stack(behind(self.first, after))
        self.by_x, self.by_y = place.over_x(self.line), place.over_y(self.line)

    def corner(self, after=()):
        place, half = self.place, self.place.outer // 2
        by_x, by_y = behind((self.by_x, self.by_y), after)
        self.far = (place.over_y(by_x[:half]), place.over_x(by_y[half:]))
        near = [self.line, self.by_x, self.by_y, jnp.concatenate(self.far, axis=0)]
        self.parts = near + [place.over_core(part) for part in near]


def add_low(left, right):
    return left + right


def first_sum_kernel(plan, where_ref, *refs):
    count = len(plan)
    keeps, comes, outs = refs[:count], refs[count : 2 * count], refs[2 * count :]
    x, core, y = where_ref[1], where_ref[2], where_ref[3]
    height = outs[0].shape[2]
    half = keeps[0].shape[0] // 4
    for keep, come, (width, start) in zip(keeps, comes, plan):
        for piece in range(keep.shape[2] // height):
            down = slice(piece * height, (piece + 1) * height)
            into = slice(start + piece * width, start + (piece + 1) * width)
            for column in range(2):
                across = slice(column * width, (column + 1) * width)
                for level in range(half):
                    for out, value in ((outs[0], x), (outs[1], 1 - x)):
                        at = 2 * level + value
                        out[column, level, :, into] = add_low(
                            keep[at, core, down, across], come[at, down, across]
                        )
            for place in range(2 * half):
                at = 2 * half + place
                for out, value in ((outs[2], y), (outs[3], 1 - y)):
                    across = pl.ds(pl.multiple_of(value * width, LANES), width)
                    out[place, :, into] = add_low(keep[at, core, down, across], come[at, down, across])


def second_sum_kernel(where_ref, *refs):
    x, y = where_ref[1], where_ref[3]
    keep, come, keep_low, come_low, *outs = refs
    for level in range(keep.shape[1]):
        for out, value in ((outs[0], y), (outs[1], 1 - y)):
            out[level] = add_low(keep[value, level], come[value, level])
    for level in range(keep_low.shape[0] // 2):
        for out, value in ((outs[2], x), (outs[3], 1 - x)):
            at = 2 * level + value
            out[level] = add_low(keep_low[at], come_low[at])


def third_sum_kernel(where_ref, *refs):
    line = refs[-1]
    z, outer = where_ref[0], line.shape[0]
    operands, outs = refs[: -1 - outer], refs[-1 - outer : -1]
    start = 0
    for keep, come in zip(operands[0::2], operands[1::2]):
        for level in range(keep.shape[0]):
            line[start + level] = add_low(keep[level], come[level])
        start += keep.shape[0]
    for shift, out in enumerate(outs):
        out[...] = line[z ^ shift]


def last_sum_kernel(wide, more, *refs):
    parts, outs = refs[: len(refs) - 2 - more], refs[len(refs) - 2 - more :]
    total_ref, share_ref = outs[-2:]
    total = parts[0][...].astype(F32)
    for part in parts[1:]:
        total = total + part[...].astype(F32)
    total_ref[...] = total[:, :wide]
    lines = jnp.sum(total[:, :wide] * total[:, :wide], axis=0, keepdims=True)
    squares = lines[:, :LANES]
    for start in range(LANES, wide, LANES):
        squares = squares + lines[:, start : start + LANES]
    if more:
        height = total.shape[0]
        share_ref[:height, :] = total[:, wide:]
        share_ref[height:, :] = jnp.zeros((8, LANES), F32)
        share_ref[height : height + 1, :] = squares + outs[0][...]
    else:
        share_ref[...] = squares


class Scatter:
    def __init__(self, place, grads, height, deps=()):
        self.place = place
        half = place.outer // 2
        keeps = [g.reshape(2 * place.outer, 2, g.shape[0] // place.dp, g.shape[1]) for g in grads]
        comes = [place.over_core(pick(keep, 1 - place.core, 1)) for keep in keeps]
        plan, total = [], 0
        for keep in keeps:
            plan.append((keep.shape[3] // 2, total))
            total += keep.shape[2] // height * keep.shape[3] // 2
        shapes = [shape_of((2, half, height, total), BF)] * 2
        shapes += [shape_of((2 * half, height, total), BF)] * 2
        self.first = self.call(functools.partial(first_sum_kernel, plan), (*keeps, *comes), shapes, deps)
        self.came_first = (place.over_x(self.first[1]), place.over_y(self.first[3]))
        self.size = (height, total)

    def call(self, kernel, operands, shapes, deps=(), name="sum", **rest):
        return run(
            kernel,
            (self.place.where, *operands),
            shapes,
            deps,
            [SCALARS] + [INSIDE] * len(operands),
            out_specs=[INSIDE] * len(shapes),
            name=name,
            micros=2,
            mib=14,
            **rest,
        )

    def second(self, deps=()):
        place = self.place
        operands = [v for pair in zip(self.first[0::2], self.came_first) for v in pair]
        shapes = [shape_of((place.outer // 2,) + self.size, BF)] * 4
        self.next = self.call(second_sum_kernel, operands, shapes, deps)
        self.came_second = (place.over_y(self.next[1]), place.over_x(self.next[3]))
        return self.next[1::2]

    def third(self, deps=()):
        place, outer = self.place, self.place.outer
        operands = [v for pair in zip(self.next[0::2], self.came_second) for v in pair]
        lines = self.call(
            third_sum_kernel,
            operands,
            [shape_of(self.size, BF)] * outer,
            deps,
            scratch_shapes=[pltpu.VMEM((outer,) + self.size, BF)],
        )
        self.sent = lines[1:]
        self.lines = [lines[0]] + [
            place.along_z(line, shift) for shift, line in enumerate(lines[1:], start=1)
        ]
        return self.lines

    def last(self, squares=None, deps=()):
        height, wide = self.size
        if squares is None:
            share, more = shape_of((1, LANES), F32), ()
        else:
            wide -= LANES
            share, more = shape_of((height + 8, LANES), F32), (squares,)
        return run(
            functools.partial(last_sum_kernel, wide, len(more)),
            tuple(self.lines) + more,
            [shape_of((height, wide), F32), share],
            deps,
            out_specs=[INSIDE] * 2,
            name="total",
        mib=8,
            micros=1,
        )


def spread_line(place, share):
    return jnp.stack([share] + [place.along_z(share, flip) for flip in range(1, place.outer)])


def spread_rest(place, line, after=()):
    near = [line, place.over_x(line), place.over_y(line), place.over_corner(line)]
    near = jnp.concatenate(behind(near, after), axis=0)
    return jnp.concatenate([near, place.over_core(near)], axis=0)


def scatter_plain(grad):
    rows = lax.psum_scatter(grad, "dp", scatter_dimension=0, tiled=True)
    return lax.psum_scatter(rows, "mp", scatter_dimension=1, tiled=True).astype(F32)


def gather_plain(shard):
    rows = lax.all_gather(shard.astype(BF), "dp", axis=0, tiled=True)
    return lax.all_gather(rows, "mp", axis=1, tiled=True)


def body(
    kernel_state,
    qkv_state,
    proj_state,
    fc1_state,
    fc2_state,
    table_state,
    patches_s,
    patches_l,
    resize_s,
    resize_l,
    bilin_s,
    bilin_l,
    cotangent,
    rates,
    step,
):
    place = Place()
    where, direct = place.where, place.direct
    first = POS_GRID * POS_GRID
    bias_one = table_state[0, first + 7 :].reshape(1, -1)
    low = lambda state: state[0].astype(BF)
    height, wide = qkv_state.shape[1:]
    hidden = fc1_state.shape[2]
    units = fc2_state.shape[1]
    side = proj_state.shape[2]
    if direct:
        pieces = units // height
        first_gather = Gather(place, low(qkv_state))
        first_gather.sides()
        shard = [low(fc1_state)] + list(low(fc2_state).reshape(pieces, height, side)) + [low(proj_state)]
        second_gather = Gather(place, jnp.concatenate(shard, axis=1))
        plan = [(0, 0, hidden, height, 0)]
        plan += [(1, hidden + piece * side, side, units, piece * height) for piece in range(pieces)]
        plan += [(2, hidden + pieces * side, side, height, 0)]

    images, image_rows = patches_l.shape[0], patches_l.shape[1]
    projected, embed_large, kern, mine, sent = resize_forward(
        where,
        kernel_state,
        resize_s,
        resize_l,
        patches_l.reshape(images * image_rows, -1),
        place.mp,
    )
    if direct:
        embed_large, come = mine, (place.over_y(behind(sent, second_gather.first[1:3])),)
        waits = (first_gather.by_x, first_gather.by_y)
    else:
        kern = lax.psum(kern, "mp")
        embed_large = lax.psum_scatter(embed_large, "mp", scatter_dimension=0, tiled=True)
        come = waits = ()
    patches_own = pick(patches_s, place.column, 0)
    first_rows = patches_own.shape[0]
    inputs, normed_one = embed(
        patches_own, kern, embed_large, bilin_s, bilin_l, table_state, come, waits
    )

    if direct:
        first_gather.corner(normed_one)
        second_gather.sides(first_gather.far)
        factors = behind(projected, first_gather.far)
        factors = [factors] + [place.along_z(factors, flip) for flip in range(1, place.outer)]
        w_qkv, qkv_rows = assemble_product(
            place, normed_one, first_gather.parts, [(0, 0, wide, height, 0)]
        )
    else:
        w_qkv = gather_plain(qkv_state[0])
        qkv_rows = product(normed_one, w_qkv)
    pairs = D // LANES
    attention = []
    for call in range(1):
        waits = (second_gather.line,) if direct and call == 0 else ()
        attention.append(attend(qkv_rows, first_rows, image_rows, call * pairs, pairs, waits))
    attended = [call[0] for call in attention]

    if direct:
        factors = [jnp.stack(behind(factors, attended))]
        second_gather.corner((attended, factors[0]))
        w_fc1, w_fc2, w_proj = assemble(place, second_gather.parts, plan)
    else:
        w_proj, w_fc1, w_fc2 = [gather_plain(a[0]) for a in (proj_state, fc1_state, fc2_state)]
    middle, normed_two = merge(inputs, attended, w_proj, table_state)
    if direct:
        factors.append(place.over_x(behind(factors[0], w_proj)))
    block_out, back, grad_fc1, grad_fc2, bias_one_grad, bias_two_grad = feed(
        middle, cotangent, normed_two, w_fc1, w_fc2, bias_one, table_state
    )
    middle_grad, heads_up, middle_rows, grad_proj = merge_back(
        back, middle, cotangent, attended, w_proj, table_state, ()
    )
    waits = ()
    if direct:
        grads = behind((grad_fc1, grad_fc2), factors[1])
        scatter_f = Scatter(place, (*grads, grad_proj), height)
        factors += [place.over_core(part) for part in behind(factors, back)]
        waits = tuple(scatter_f.first[1::2]) + tuple(factors[2:])
    heads = [
        attend_back(
            qkv_rows, attended[call], heads_up, attention[call][1], first_rows, image_rows,
            call * pairs, waits,
        )
        for call in range(1)
    ]
    large_grad, small_grad = inputs_back(
        heads,
        w_qkv,
        inputs,
        middle_grad,
        table_state,
        patches_own,
        bilin_s,
        bilin_l,
        middle_rows,
        bias_one_grad,
        bias_two_grad,
        BF if direct else F32,
    )
    waits = tuple(scatter_f.second()) if direct else ()
    grad_qkv = qkv_grad(normed_one, heads, waits)
    kern_rows = patches_s.shape[2]
    if direct:
        line = spread_line(place, large_grad)
        scatter_f.third((line,))
        scatter_q = Scatter(place, (grad_qkv, small_grad), height, tuple(scatter_f.sent))
        scatter_q.second((scatter_f.lines[1],))
        own_rest, squares_f = scatter_f.last()
        scatter_q.third(tuple(scatter_f.lines[2:]))
        line = spread_rest(place, line, scatter_q.lines[1])
        part = base_all(place, factors, line)
        own_qkv, share = scatter_q.last(squares_f, (part,))
        base_grad, table_total, squares = base_total(
            place, part, resize_s, spread_rest(place, spread_line(place, share)), small_grad.shape[0]
        )
        own_fc2 = jnp.concatenate(
            [own_rest[:, hidden + piece * side : hidden + (piece + 1) * side] for piece in range(pieces)],
            axis=0,
        )
        owned = (own_qkv, own_rest[:, hidden + pieces * side :], own_rest[:, :hidden], own_fc2)
        squares = (squares, place.over_y(squares[:1]))
    else:
        large_all = lax.all_gather(large_grad, "mp", axis=0, tiled=True)
        sums = lax.psum(small_grad, ("dp", "mp"))
        sums = sums.reshape(D // LANES // 2, -1, 2, LANES).transpose(1, 2, 0, 3).reshape(-1, D)
        table_total = sums[kern_rows : kern_rows + TROWS]
        part = lax.dot_general(
            resize_s,
            sums[:kern_rows].reshape(3, -1, D).transpose(1, 0, 2).reshape(-1, 3 * D),
            TN,
            precision=lax.Precision.HIGHEST,
            preferred_element_type=F32,
        )
        base_grad = lax.psum(base_back(projected, large_all), "dp") + part
        owned = tuple(scatter_plain(g) for g in (grad_qkv, grad_proj, grad_fc1, grad_fc2))
        squares = sum(jnp.sum(piece * piece) for piece in owned)
        squares = lax.psum(squares, ("dp", "mp")) + jnp.sum(table_total * table_total)
        squares = squares + lax.psum(jnp.sum(base_grad * base_grad), "mp")
        squares = (jnp.pad(squares.reshape(1, 1), ((0, 0), (0, LANES - 1))),)
    count = step[0].astype(F32)
    fix_one = 1.0 / (1.0 - jnp.power(BETA_ONE, count))
    fix_two = 1.0 / (1.0 - jnp.power(BETA_TWO, count))
    grad_norm, kernel_new, kernel_moments, *blocks = adam(
        jnp.concatenate([jnp.stack([fix_one, fix_two]), rates]),
        squares,
        (kernel_state, qkv_state, proj_state, fc1_state, fc2_state, table_state),
        (base_grad, *owned, table_total),
    )
    grad_norm = grad_norm[0, 0]
    blocks = blocks[:-2] + [jnp.stack(blocks[-2:])]
    return (block_out, grad_norm, kernel_new, kernel_moments, *blocks)


def solution(mesh):
    placed = (
        P(None, "mp", None),
        P(None, "dp", "mp"),
        P(None, "dp", "mp"),
        P(None, "dp", "mp"),
        P(None, "dp", "mp"),
        P(),
        P("dp", None, None),
        P("dp", None, None),
        P(None, "mp"),
        P(None, "mp"),
        P(),
        P(),
        P(("dp", "mp"), None),
        P(),
        P(),
    )
    return jax.shard_map(
        body,
        mesh=mesh,
        in_specs=placed,
        out_specs=(
            P(("dp", "mp"), None),
            P(),
            P("mp", None),
            P(None, "mp", None),
            P("dp", "mp"),
            P(None, "dp", "mp"),
            P("dp", "mp"),
            P(None, "dp", "mp"),
            P("dp", "mp"),
            P(None, "dp", "mp"),
            P("dp", "mp"),
            P(None, "dp", "mp"),
            P(),
            P(),
        ),
        check_vma=False,
    )
```

```python
import functools
import math

import jax
import jax.numpy as jnp
from jax import lax
from jax.experimental import pallas as pl
from jax.experimental.pallas import tpu as pltpu
from jax.sharding import PartitionSpec as P

D = 768
HEADS = 12
HEAD_DIM = 64
FF = 3072
BASE = 32
POS_GRID = 7
GRID_S = 28
GRID_L = 4
TROWS = 60

NORM_EPS = 1e-06
BETA_ONE = 0.5
BETA_TWO = 0.5
DECAY = 0.05
ADAM_EPS = 1e-08
TINY = 1e-37
MASKED = -1e30
LOG2E = 1.4426950408889634
LANES = 128
MIB = 2**20

BF = jnp.bfloat16
F32 = jnp.float32
NN = (((1,), (0,)), ((), ()))
NT = (((1,), (1,)), ((), ()))
TN = (((0,), (0,)), ((), ()))


def shape_of(dims, dtype):
    return jax.ShapeDtypeStruct(dims, dtype)


def params(mib=56):
    return pltpu.CompilerParams(vmem_limit_bytes=mib * MIB)


def cost(flops, moved):
    return pl.CostEstimate(flops=int(flops), bytes_accessed=int(moved), transcendentals=0)


def dot(left, right, dims=NN):
    return lax.dot_general(left, right, dims, preferred_element_type=F32)


def run(kernel, operands, out_shape, deps=(), in_specs=None, name=None, micros=1, mib=56, **rest):
    count, skip = len(operands), len(deps)

    def inner(*refs):
        kernel(*refs[:count], *refs[count + skip :])

    if in_specs is None:
        in_specs = [pl.BlockSpec(memory_space=pltpu.VMEM)] * count
    return pl.pallas_call(
        inner,
        in_specs=list(in_specs) + [pl.BlockSpec(memory_space=pl.ANY)] * skip,
        out_shape=out_shape,
        compiler_params=params(mib),
        cost_estimate=cost(micros * 1e7, 0),
        name=name,
        **rest,
    )(*operands, *deps)


def whole(array):
    return pl.BlockSpec(array.shape, lambda *i: (0,) * len(array.shape))


SCALARS = pl.BlockSpec(memory_space=pltpu.SMEM)
INSIDE = pl.BlockSpec(memory_space=pltpu.VMEM)


def first_state(state):
    return pl.BlockSpec((1,) + state.shape[1:], lambda *i: (0, 0, 0))


def halves(value):
    high = value.astype(BF)
    return high, (value - high.astype(F32)).astype(BF)


def dot_fine(left, right, dims=NN):
    left_high, left_low = halves(left)
    right_high, right_low = halves(right)
    return dot(left_high, right_high, dims) + (
        dot(left_high, right_low, dims) + dot(left_low, right_high, dims)
    )


def norm_forward(inputs):
    centered = inputs - jnp.mean(inputs, axis=-1, keepdims=True)
    inverse = lax.rsqrt(jnp.mean(centered * centered, axis=-1, keepdims=True) + NORM_EPS)
    return centered * inverse, inverse


def norm_backward(upstream, normalized, inverse, gain_row):
    scaled = upstream * gain_row
    inner = jnp.mean(scaled * normalized, axis=-1, keepdims=True)
    result = inverse * (scaled - jnp.mean(scaled, axis=-1, keepdims=True) - normalized * inner)
    return (
        result,
        jnp.sum(upstream * normalized, axis=0, keepdims=True),
        jnp.sum(upstream, axis=0, keepdims=True),
    )


def resize_kernel(
    where_ref,
    base_ref,
    small_ref,
    large_ref,
    patch_ref,
    projected_ref,
    embed_ref,
    kern_ref,
    mine_ref,
    send_ref,
    turned,
    pixels_ref,
):
    rows = embed_ref.shape[0]

    @pl.when(pl.program_id(0) == 0)
    def _():
        embed_ref[...] = jnp.zeros_like(embed_ref)
        kern_ref[...] = jnp.zeros_like(kern_ref)
        count = large_ref.shape[0]
        for start in range(0, rows, LANES):
            size = min(LANES, rows - start)
            patch = patch_ref[start : start + size, :].astype(F32)
            if size < LANES:
                patch = jnp.concatenate(
                    [patch, jnp.zeros((LANES - size, patch.shape[1]), F32)], axis=0
                )
            turned[...] = patch.T
            for channel in range(3):
                across = turned[pl.ds(channel, count, stride=3), :].T
                pixels_ref[channel * rows + start : channel * rows + start + size, :] = across[
                    :size
                ].astype(BF)

    base = base_ref[0]
    width = base.shape[1] // 3
    large_high, large_low = halves(large_ref[...])
    pixels = pixels_ref[...]
    projected = dot(pixels, large_high) + dot(pixels, large_low)
    kern_ref[...] += dot_fine(small_ref[...], base)
    total = embed_ref[...]
    for channel in range(3):
        part = projected[channel * rows : (channel + 1) * rows]
        projected_ref[channel] = part.astype(BF)
        total += dot_fine(part, base[:, channel * width : (channel + 1) * width])
    embed_ref[...] = total

    @pl.when(pl.program_id(0) == pl.num_programs(0) - 1)
    def _():
        part, y = mine_ref.shape[0], where_ref[3]
        mine_ref[...] = embed_ref[pl.ds(pl.multiple_of(y * part, 8), part), :]
        other = embed_ref[pl.ds(pl.multiple_of((1 - y) * part, 8), part), :]
        send_ref[:, : 3 * width] = kern_ref[...].astype(BF)
        if 2 * part == send_ref.shape[0]:
            high, low = halves(other)
            send_ref[:part, 3 * width :] = high
            send_ref[part:, 3 * width :] = low


def resize_forward(where, kernel_state, resize_s, resize_l, patches, parts):
    base_rows, wide = kernel_state.shape[1:]
    count = base_rows // LANES
    rows = patches.shape[0]
    columns = 3 * rows
    shapes = [
        shape_of((3, rows, base_rows), BF),
        shape_of((rows, wide // 3), F32),
        shape_of((resize_s.shape[0], wide), F32),
        shape_of((rows // parts, wide // 3), F32),
        shape_of((resize_s.shape[0], wide + wide // 3), BF),
    ]
    return run(
        resize_kernel,
        (where, kernel_state, resize_s, resize_l, patches),
        shapes,
        (),
        [
            SCALARS,
            pl.BlockSpec((1, LANES, wide), lambda i: (0, i, 0)),
            pl.BlockSpec((resize_s.shape[0], LANES), lambda i: (0, i)),
            pl.BlockSpec((resize_l.shape[0], LANES), lambda i: (0, i)),
            whole(patches),
        ],
        grid=(count,),
        out_specs=[pl.BlockSpec((3, rows, LANES), lambda i: (0, 0, i))]
        + [whole(shape) for shape in shapes[1:]],
        scratch_shapes=[
            pltpu.VMEM((patches.shape[1], LANES), F32),
            pltpu.VMEM((columns, resize_l.shape[0]), BF),
        ],
        name="resize",
        micros=9,
        mib=52,
    )


def embed_kernel(
    patch_ref, kern_ref, large_ref, bilin_s_ref, bilin_l_ref, table_ref, *refs
):
    table = table_ref[0]
    first = POS_GRID * POS_GRID
    pixels = kern_ref.shape[0]
    width = table.shape[1]
    x_ref, a_ref, woven = refs[-3:]
    part = large_ref.shape[0]
    if len(refs) == 4:
        come_ref = refs[0]
        come = come_ref[:, 3 * width :].astype(F32)
        large_part = large_ref[...] + (come[:part] + come[part:])
    else:
        come_ref, large_part = None, large_ref[...]
    tiles = width // LANES
    for channel in range(3):
        for tile in range(tiles):
            start = channel * width + tile * LANES
            value = kern_ref[:, start : start + LANES]
            if come_ref is not None:
                value = value + come_ref[:, start : start + LANES].astype(F32)
            woven[tile, pl.ds(channel, pixels, stride=3), :] = value
    kern = jnp.concatenate([woven[tile].astype(BF) for tile in range(tiles)], axis=1)
    grid_rows = table[:first]
    bias = table[first : first + 1]
    small = patch_ref.shape[0]
    x_ref[:small, :] = (
        dot(patch_ref[...], kern) + dot_fine(bilin_s_ref[...], grid_rows) + bias
    )
    tokens = bilin_l_ref.shape[0]
    placed = dot_fine(bilin_l_ref[...], grid_rows) + bias
    for image in range(large_ref.shape[0] // tokens):
        part = slice(image * tokens, (image + 1) * tokens)
        x_ref[small + image * tokens : small + (image + 1) * tokens, :] = large_part[part] + placed
    normal, _ = norm_forward(x_ref[...])
    a_ref[...] = (normal * table[first + 1 : first + 2] + table[first + 2 : first + 3]).astype(BF)


def embed(patches, kern, large, bilin_s, bilin_l, table_state, come=(), deps=()):
    rows = patches.shape[0] + large.shape[0]
    width = table_state.shape[2]
    return run(
        embed_kernel,
        (patches, kern, large, bilin_s, bilin_l, table_state, *come),
        [shape_of((rows, width), F32), shape_of((rows, width), BF)],
        deps,
        [INSIDE] * 5 + [first_state(table_state)] + [INSIDE] * len(come),
        grid=(1,),
        out_specs=[INSIDE] * 2,
        scratch_shapes=[pltpu.VMEM((width // LANES, patches.shape[1], LANES), F32)],
        name="embed",
        mib=12,
        micros=5,
    )


def product_kernel(left_ref, right_ref, out_ref):
    columns = out_ref.shape[1]
    block = min(columns, D)
    for start in range(0, columns, block):
        across = slice(start, start + block)
        out_ref[:, across] = dot(left_ref[...], right_ref[:, across]).astype(BF)


def product(left, right):
    return run(
        product_kernel,
        (left, right),
        shape_of((left.shape[0], right.shape[1]), BF),
        out_specs=INSIDE,
        name="project",
        micros=7,
        mib=14,
    )


def assemble_product_kernel(outer, plan, where_ref, left_ref, *refs):
    assemble_kernel(outer, plan, where_ref, *refs[:-1])
    product_kernel(left_ref, refs[-2], refs[-1])


def assemble_product(place, left, parts, plan):
    outer, height = parts[0].shape[:2]
    (_, _, width, rows, _) = plan[0]
    shape = (place.dp * rows, 2 * width)
    return run(
        functools.partial(assemble_product_kernel, outer, plan),
        (place.where, left, *parts),
        [shape_of(shape, BF), shape_of((left.shape[0], shape[1]), BF)],
        (),
        [SCALARS] + [INSIDE] * 9,
        out_specs=[INSIDE] * 2,
        name="project",
        micros=8,
        mib=14,
    )


def image_features(rows, first_rows, image_rows):
    row = lax.broadcasted_iota(jnp.int32, (rows, LANES), 0)
    lane = lax.broadcasted_iota(jnp.int32, (rows, LANES), 1) % HEAD_DIM
    label = jnp.where(row < first_rows, 0, 1 + (row - first_rows) // image_rows)
    count = 1 + (rows - first_rows) // image_rows
    own = label == lane
    query = jnp.where(own | (lane >= count), 0.0, MASKED).astype(BF)
    return query, jnp.where(own, 1.0, 0.0).astype(BF)


def attend_kernel(first_rows, image_rows, chunks, q_ref, k_ref, v_ref, out_ref, log_ref):
    rows = q_ref.shape[0]
    query_mark, key_mark = image_features(rows, first_rows, image_rows)
    low = lax.broadcasted_iota(jnp.int32, (rows, LANES), 1) < HEAD_DIM
    step = rows // chunks
    queries = q_ref[...] * jnp.asarray(HEAD_DIM**-0.5, BF)
    keys, values = k_ref[...], v_ref[...]
    ones = jnp.ones((rows, LANES), BF)
    results = []
    for head in range(2):
        mine = low if head == 0 else ~low
        query = jnp.where(mine, queries, query_mark)
        key = jnp.where(mine, keys, key_mark)
        value = jnp.where(mine, values, ones)
        outs, logs = [], []
        for chunk in range(chunks):
            scores = dot(query[chunk * step : (chunk + 1) * step], key, NT)
            largest = jnp.max(scores, axis=1, keepdims=True)
            probs = jnp.exp2(scores * LOG2E - largest * LOG2E)
            summed = dot(probs.astype(BF), value)
            rolled = pltpu.roll(summed, HEAD_DIM, 1)
            outs.append(summed / rolled)
            logs.append(largest * LOG2E + jnp.log2(jnp.where(mine[:step], rolled, summed)))
        results.append(jnp.concatenate(outs, axis=0))
        log_ref[0, 8 * head : 8 * head + 8, :] = jnp.concatenate(logs, axis=0).T[:8]
    out_ref[...] = jnp.where(low, results[0], results[1]).astype(BF)


def attend(qkv, first_rows, image_rows, start, count, deps=()):
    rows, wide = qkv.shape
    pairs = wide // 3 // LANES
    chunks = 3 if rows % 48 == 0 else 1
    part = lambda offset: pl.BlockSpec((rows, LANES), lambda i: (0, offset + i))
    return run(
        functools.partial(attend_kernel, first_rows, image_rows, chunks),
        (qkv, qkv, qkv),
        [shape_of((rows, count * LANES), BF), shape_of((count, 16, rows), F32)],
        deps,
        [part(start), part(pairs + start), part(2 * pairs + start)],
        grid=(count,),
        out_specs=[part(0), pl.BlockSpec((1, 16, rows), lambda i: (i, 0, 0))],
        name="attend",
        mib=12,
        micros=3 * count,
    )


def merge_kernel(x_ref, w_ref, table_ref, *refs):
    attended, (middle_ref, a_ref) = refs[:-2], refs[-2:]
    first = POS_GRID * POS_GRID
    table = table_ref[0]
    middle = x_ref[...] + table[first + 5 : first + 6]
    start = 0
    for part in attended:
        size = part.shape[1]
        middle = middle + dot(part[...], w_ref[start : start + size, :])
        start += size
    middle_ref[...] = middle
    normal, _ = norm_forward(middle)
    a_ref[...] = (normal * table[first + 3 : first + 4] + table[first + 4 : first + 5]).astype(BF)


def merge(inputs, attended, w_proj, table_state, deps=()):
    rows, width = inputs.shape
    return run(
        merge_kernel,
        (inputs, w_proj, table_state, *attended),
        [shape_of((rows, width), F32), shape_of((rows, width), BF)],
        deps,
        [INSIDE, INSIDE, first_state(table_state)] + [INSIDE] * len(attended),
        grid=(1,),
        out_specs=[INSIDE] * 2,
        name="merge",
        mib=12,
        micros=6,
    )


def merge_parts_kernel(outer, plan, count, where_ref, x_ref, table_ref, *refs):
    attended, parts, outs = refs[:count], refs[count : count + 8], refs[count + 8 :]
    assemble_kernel(outer, plan, where_ref, *parts, outs[2])
    merge_kernel(x_ref, outs[2], table_ref, *attended, *outs[:2])


def merge_parts(place, inputs, attended, parts, start, table_state):
    rows, width = inputs.shape
    outer, height, columns = parts[0].shape
    side = columns - start
    plan = [(0, 0, side, height, 0)]
    piece = pl.BlockSpec((outer, height, side), lambda i: (0, 0, start // side))
    return run(
        functools.partial(merge_parts_kernel, outer, plan, len(attended)),
        (place.where, inputs, table_state, *attended, *parts),
        [
            shape_of((rows, width), F32),
            shape_of((rows, width), BF),
            shape_of((place.dp * height, 2 * side), BF),
        ],
        (),
        [SCALARS, INSIDE, first_state(table_state)] + [INSIDE] * len(attended) + [piece] * 8,
        grid=(1,),
        out_specs=[INSIDE] * 3,
        name="merge",
        micros=6,
        mib=14,
    )


def feed_kernel(
    middle_ref,
    cotangent_ref,
    a_ref,
    w_one_ref,
    w_two_ref,
    bias_ref,
    table_ref,
    out_ref,
    grad_ref,
    g_one_ref,
    g_two_ref,
    b_one_ref,
    b_two_ref,
    turned,
    upstream,
):
    place = pl.program_id(0)

    @pl.when(place == 0)
    def _():
        first = POS_GRID * POS_GRID
        turned[...] = a_ref[...].T
        low = cotangent_ref[...].astype(BF)
        upstream[...] = low
        out_ref[...] = middle_ref[...] + table_ref[0][first + 6 : first + 7]
        grad_ref[...] = jnp.zeros_like(grad_ref)
        b_two_ref[...] = jnp.sum(low.astype(F32), axis=0, keepdims=True)

    block = bias_ref.shape[1]
    part = pl.ds(pl.multiple_of(place * block, LANES), block)
    w_one, w_two, dz = w_one_ref[:, part], w_two_ref[part, :], upstream[...]
    hidden = dot(a_ref[...], w_one) + bias_ref[...]
    phi = 0.5 * (1.0 + lax.erf(hidden * 0.7071067811865476))
    active = (hidden * phi).astype(BF)
    slope = phi + hidden * jnp.exp(-0.5 * hidden * hidden) * 0.3989422804014327
    change = dot(dz, w_two, NT) * slope
    b_one_ref[...] = jnp.sum(change, axis=0, keepdims=True)
    change = change.astype(BF)
    out_ref[...] += dot(active, w_two)
    grad_ref[...] += dot(change, w_one, NT)
    g_one_ref[...] = dot(turned[...], change).astype(BF)
    g_two_ref[...] = dot(active, dz, TN).astype(BF)


def feed(middle, cotangent, normed, bias_one, table_state, w_one, w_two):
    rows, width = normed.shape
    hidden = bias_one.shape[1]
    block = D
    across = pl.BlockSpec((width, block), lambda i: (0, i))
    down = pl.BlockSpec((block, width), lambda i: (i, 0))
    line = pl.BlockSpec((1, block), lambda i: (0, i))
    return run(
        feed_kernel,
        (middle, cotangent, normed, w_one, w_two, bias_one, table_state),
        [
            shape_of((rows, width), F32),
            shape_of((rows, width), F32),
            shape_of((width, hidden), BF),
            shape_of((hidden, width), BF),
            shape_of((1, hidden), F32),
            shape_of((1, width), F32),
        ],
        (),
        [INSIDE] * 5 + [line, first_state(table_state)],
        grid=(hidden // block,),
        out_specs=[INSIDE, INSIDE, across, down, line, INSIDE],
        scratch_shapes=[pltpu.VMEM((width, rows), BF), pltpu.VMEM((rows, width), BF)],
        name="feed",
        mib=24,
        micros=9 * (hidden // block),
    )


def merge_back_kernel(count, grad_ref, middle_ref, cotangent_ref, w_ref, table_ref, *refs):
    attended = refs[:count]
    back_ref, heads_ref, rows_ref, g_ref = refs[count:]
    first = POS_GRID * POS_GRID
    normal, inverse = norm_forward(middle_ref[...])
    change, gain, shift = norm_backward(
        grad_ref[...], normal, inverse, table_ref[0][first + 3 : first + 4]
    )
    back = cotangent_ref[...] + change
    back_ref[...] = back
    low = back.astype(BF)
    heads_ref[...] = dot(low, w_ref[...], NT).astype(BF)
    start = 0
    for part in attended:
        size = part.shape[1]
        g_ref[start : start + size, :] = dot(part[...], low, TN).astype(BF)
        start += size
    rows_ref[0:1, :] = gain
    rows_ref[1:2, :] = shift
    rows_ref[2:3, :] = jnp.sum(low.astype(F32), axis=0, keepdims=True)


def merge_back(grad, middle, cotangent, attended, w_proj, table_state, deps=()):
    rows, width = middle.shape
    return run(
        functools.partial(merge_back_kernel, len(attended)),
        (grad, middle, cotangent, w_proj, table_state, *attended),
        [
            shape_of((rows, width), F32),
            shape_of((rows, width), BF),
            shape_of((8, width), F32),
            shape_of(w_proj.shape, BF),
        ],
        deps,
        [INSIDE, INSIDE, INSIDE, INSIDE, first_state(table_state)] + [INSIDE] * len(attended),
        grid=(1,),
        out_specs=[INSIDE] * 4,
        name="merge_back",
        mib=20,
        micros=9,
    )


def attend_back_kernel(
    first_rows, image_rows, chunks, q_ref, k_ref, v_ref, out_ref, up_ref, log_ref, grad_ref
):
    rows = q_ref.shape[0]
    query_mark, key_mark = image_features(rows, first_rows, image_rows)
    low = lax.broadcasted_iota(jnp.int32, (rows, LANES), 1) < HEAD_DIM
    step = rows // chunks
    queries = q_ref[...] * jnp.asarray(HEAD_DIM**-0.5, BF)
    keys, values, up = k_ref[...], v_ref[...], up_ref[...]
    overlap = (out_ref[...].astype(F32) * up.astype(F32)).T
    zeros = jnp.zeros((rows, LANES), BF)
    grads = ([], [], [])
    for head in range(2):
        mine = low if head == 0 else ~low
        query = jnp.where(mine, queries, query_mark)
        key = jnp.where(mine, keys, key_mark)
        value = jnp.where(mine, values, zeros)
        inner = jnp.sum(overlap[HEAD_DIM * head : HEAD_DIM * (head + 1)], axis=0, keepdims=True)
        totals = log_ref[0, 8 * head : 8 * head + 1, :]
        query_grad = jnp.zeros((rows, LANES), F32)
        key_grads, value_grads = [], []
        for chunk in range(chunks):
            part = slice(chunk * step, (chunk + 1) * step)
            scores = dot(key[part], query, NT)
            probs = jnp.exp2(scores * LOG2E - totals)
            value_grads.append(dot(probs.astype(BF), up))
            change = (probs * (dot(value[part], up, NT) - inner)).astype(BF)
            key_grads.append(dot(change, queries))
            query_grad = query_grad + dot(change, keys[part], TN)
        grads[0].append(query_grad * HEAD_DIM**-0.5)
        grads[1].append(jnp.concatenate(key_grads, axis=0))
        grads[2].append(jnp.concatenate(value_grads, axis=0))
    for place, pair in enumerate(grads):
        grad_ref[place] = jnp.where(low, pair[0], pair[1]).astype(BF)


def attend_back(qkv, attended, upstream, logs, first_rows, image_rows, start, deps=()):
    rows, wide = qkv.shape
    pairs, count = wide // 3 // LANES, attended.shape[1] // LANES
    part = lambda offset: pl.BlockSpec((rows, LANES), lambda i: (0, offset + i))
    return run(
        functools.partial(attend_back_kernel, first_rows, image_rows, 1),
        (qkv, qkv, qkv, attended, upstream, logs),
        shape_of((3, rows, count * LANES), BF),
        deps,
        [
            part(start),
            part(pairs + start),
            part(2 * pairs + start),
            part(0),
            part(start),
            pl.BlockSpec((1, 16, rows), lambda i: (i, 0, 0)),
        ],
        grid=(count,),
        out_specs=pl.BlockSpec((3, rows, LANES), lambda i: (0, 0, i)),
        name="attend_back",
        mib=18,
        micros=5 * count,
    )


def qkv_grad_kernel(a_ref, *refs):
    turned = a_ref[...].T
    heads, out = refs[:-1], refs[-1]
    start = 0
    for kind in range(3):
        for part in heads:
            size = part.shape[2]
            out[:, start : start + size] = dot(turned, part[kind]).astype(BF)
            start += size


def qkv_grad(normed, heads, deps=()):
    width = normed.shape[1]
    return run(
        qkv_grad_kernel,
        (normed, *heads),
        shape_of((width, 3 * width), BF),
        deps,
        out_specs=INSIDE,
        name="qkv_grad",
        mib=12,
        micros=6,
    )


def inputs_back_kernel(
    w_ref,
    x_ref,
    back_ref,
    table_ref,
    patch_ref,
    bilin_s_ref,
    bilin_l_ref,
    middle_rows_ref,
    b_one_ref,
    b_two_ref,
    *refs,
):
    heads, (large_ref, small_ref, woven, small_grad) = refs[:-4], refs[-4:]
    width = x_ref.shape[1]
    total, start = None, 0
    for kind in range(3):
        for part in heads:
            size = part.shape[2]
            value = dot(part[kind], w_ref[:, start : start + size], NT)
            total = value if total is None else total + value
            start += size
    first = POS_GRID * POS_GRID
    normal, inverse = norm_forward(x_ref[...])
    change, gain, shift = norm_backward(total, normal, inverse, table_ref[0][first + 1 : first + 2])
    grad = back_ref[...] + change
    low = grad.astype(BF)
    small = patch_ref.shape[0]
    large_ref[...] = low[small:]
    kern = dot(patch_ref[...], low[:small], TN)
    pixels = kern.shape[0] // 3
    for tile in range(width // LANES):
        woven[tile] = kern[:, tile * LANES : (tile + 1) * LANES]
        for channel in range(3):
            small_grad[
                channel * pixels : (channel + 1) * pixels, tile * LANES : (tile + 1) * LANES
            ] = woven[tile, pl.ds(channel, pixels, stride=3), :]
    table_grad_ref = small_grad.at[3 * pixels :]
    table_grad_ref[...] = jnp.zeros_like(table_grad_ref)
    tokens = bilin_l_ref.shape[0]
    large = grad[small : small + tokens]
    for image in range(1, (grad.shape[0] - small) // tokens):
        large = large + grad[small + image * tokens : small + (image + 1) * tokens]
    table_grad_ref[:first, :] = dot_fine(bilin_s_ref[...], grad[:small], TN) + dot_fine(
        bilin_l_ref[...], large, TN
    )
    table_grad_ref[first : first + 1, :] = jnp.sum(grad, axis=0, keepdims=True)
    table_grad_ref[first + 1 : first + 2, :] = gain
    table_grad_ref[first + 2 : first + 3, :] = shift
    table_grad_ref[first + 3 : first + 6, :] = middle_rows_ref[0:3, :]
    table_grad_ref[first + 6 : first + 7, :] = b_two_ref[...]
    for line in range(b_one_ref.shape[1] // width):
        table_grad_ref[first + 7 + line : first + 8 + line, :] = b_one_ref[
            :, line * width : (line + 1) * width
        ]
    rows = small_grad.shape[0]
    count = width // LANES // 2
    for tile in range(2 * count):
        side, level = divmod(tile, count)
        small_ref[level * rows : (level + 1) * rows, side * LANES : (side + 1) * LANES] = small_grad[
            :, tile * LANES : (tile + 1) * LANES
        ].astype(small_ref.dtype)


def inputs_back(
    heads, w_qkv, inputs, back, table_state, patches, bilin_s, bilin_l, rows_grads, bias_one, bias_two, kind
):
    rows, width = inputs.shape
    large = rows - patches.shape[0]
    operands = (
        w_qkv, inputs, back, table_state, patches, bilin_s, bilin_l, rows_grads, bias_one, bias_two, *heads
    )
    specs = [INSIDE] * len(operands)
    specs[3] = first_state(table_state)
    small = small_rows(patches.shape[1])
    return run(
        inputs_back_kernel,
        operands,
        [shape_of((large, width), BF), shape_of((small * width // LANES // 2, 2 * LANES), kind)],
        (),
        specs,
        grid=(1,),
        out_specs=[INSIDE] * 2,
        scratch_shapes=[
            pltpu.VMEM((width // LANES, patches.shape[1], LANES), F32),
            pltpu.VMEM((small, width), F32),
        ],
        name="inputs_back",
        mib=20,
        micros=13,
    )


def small_rows(pixels):
    return -(-(pixels + TROWS) // 256) * 256


def base_back_kernel(projected_ref, large_ref, out_ref):
    width = large_ref.shape[1]
    large = large_ref[...]
    for channel in range(3):
        out_ref[:, channel * width : (channel + 1) * width] = dot(projected_ref[channel], large, TN)


def base_back(projected, large):
    rows, wide = projected.shape[2], 3 * large.shape[1]
    return run(
        base_back_kernel,
        (projected, large),
        shape_of((rows, wide), F32),
        out_specs=INSIDE,
        name="base_back",
        mib=16,
        micros=8,
    )


def base_all_kernel(outer, where_ref, *refs):
    parts, line_ref, out_ref, projected, large = refs[:4], *refs[4:]
    height = line_ref.shape[1]
    z, x, core, y = where_ref[0], where_ref[1], where_ref[2], where_ref[3]
    for place in range(line_ref.shape[0]):
        flip, pair = z ^ (place % outer), x ^ (place // outer % 2)
        block = flip * 4 + pair * 2 + (core ^ (place // outer // 4))
        row = pl.multiple_of((block * 2 + (y ^ (place // outer // 2 % 2))) * height, 16)
        large[pl.ds(row, height), :] = line_ref[place]
    rows = parts[0].shape[2]
    for place, part in enumerate(parts):
        for flip in range(outer):
            block = (z ^ flip) * 4 + (x ^ (place % 2)) * 2 + (core ^ (place // 2))
            for channel in range(3):
                projected[channel, pl.ds(pl.multiple_of(block * rows, 16), rows), :] = part[flip, channel]
    base_back_kernel(projected, large, out_ref)


def base_all(place, parts, line):
    outer, _, rows, columns = parts[0].shape
    count, height, width = line.shape
    return run(
        functools.partial(base_all_kernel, outer),
        (place.where, *parts, line),
        shape_of((columns, 3 * width), F32),
        (),
        [SCALARS] + [INSIDE] * 5,
        out_specs=INSIDE,
        scratch_shapes=[
            pltpu.VMEM((3, place.dp * rows, columns), BF),
            pltpu.VMEM((count * height, width), BF),
        ],
        name="base_back",
        mib=16,
        micros=8,
    )


def base_total_kernel(outer, where_ref, part_ref, small_ref, line_ref, out_ref, table_ref, squares_ref, sums):
    pixels = small_ref.shape[0]
    width = part_ref.shape[1] // 3
    count = width // LANES // 2
    height = sums.shape[1] * sums.shape[0] // line_ref.shape[0]
    rows = sums.shape[1] // count
    z, x, core, y = where_ref[0], where_ref[1], where_ref[2], where_ref[3]
    squares = jnp.zeros((1, LANES), F32)
    for place in range(line_ref.shape[0]):
        flip, pair, side, single = z ^ (place % outer), place // outer % 2, place // outer // 2 % 2, place // outer // 4
        block = flip * 4 + (x ^ pair) * 2 + (core ^ single)
        sums[y ^ side, pl.ds(pl.multiple_of(block * height, 8), height), :] = line_ref[place, :height]
    for block in range(line_ref.shape[0]):
        flip, pair, single, side = (block // 8) ^ z, (block // 4 % 2) ^ x, (block // 2 % 2) ^ core, (block % 2) ^ y
        squares = squares + line_ref[((single * 2 + side) * 2 + pair) * outer + flip, height : height + 1]
    squares_all = squares
    small = jnp.concatenate(
        [
            sums[tile // count, tile % count * rows : (tile % count + 1) * rows, :]
            for tile in range(2 * count)
        ],
        axis=1,
    )
    table = small[3 * pixels : 3 * pixels + table_ref.shape[0]]
    table_ref[...] = table
    lines = jnp.sum(table * table, axis=0, keepdims=True)
    for start in range(0, width, LANES):
        squares_all = squares_all + lines[:, start : start + LANES]
    squares_ref[1:2, :] = squares_all
    squares = jnp.zeros((1, LANES), F32)
    for channel in range(3):
        across = slice(channel * width, (channel + 1) * width)
        value = part_ref[:, across] + dot_fine(
            small_ref[...], small[channel * pixels : (channel + 1) * pixels], TN
        )
        out_ref[:, across] = value
        lines = jnp.sum(value * value, axis=0, keepdims=True)
        for start in range(0, width, LANES):
            squares = squares + lines[:, start : start + LANES]
    squares_ref[0:1, :] = squares


def base_total(place, part, resize_s, line, sums_rows):
    return run(
        functools.partial(base_total_kernel, place.outer),
        (place.where, part, resize_s, line),
        [shape_of(part.shape, F32), shape_of((TROWS, part.shape[1] // 3), F32), shape_of((2, LANES), F32)],
        (),
        [SCALARS] + [INSIDE] * 3,
        out_specs=[INSIDE] * 3,
        scratch_shapes=[pltpu.VMEM((2, sums_rows, LANES), F32)],
        name="base_total",
        mib=12,
        micros=5,
    )


def adam_kernel(count, squares_count, scalars_ref, *refs):
    squares, refs = refs[:squares_count], refs[squares_count:]
    states, gradients, outs = refs[:count], refs[count : 2 * count], refs[2 * count :]
    norm_ref, outs = outs[0], outs[1:]
    total = sum(jnp.sum(part[...], axis=0, keepdims=True) for part in squares)
    norm = jnp.sqrt(jnp.sum(total, axis=1, keepdims=True))
    clip_level = 0.5 * math.sqrt(3 * BASE * BASE * D + 4 * D * D + 2 * D * FF + TROWS * D)
    factor = clip_level / jnp.maximum(norm, clip_level)
    fix_one, fix_two = scalars_ref[0], scalars_ref[1]

    def update(place, rows):
        state_ref = states[place]
        master, old_first, old_second = [state_ref[entry, rows, :] for entry in range(3)]
        clipped = gradients[place][rows, :] * factor
        first = BETA_ONE * (old_first + clipped)
        second = BETA_TWO * (old_second + clipped * clipped)
        square = second * fix_two
        below = square * lax.rsqrt(jnp.maximum(square, TINY)) + ADAM_EPS
        guess = pl.reciprocal(below, approx=True)
        guess = guess * (2.0 - below * guess)
        rate = scalars_ref[2 + place]
        new = master * (1.0 - rate * DECAY) - (first * guess) * (rate * fix_one)
        return new, first, second

    step = pl.program_id(0)
    outs[0][...], outs[1][0], outs[1][1] = update(0, slice(None))

    @pl.when(step == 0)
    def _():
        norm_ref[...] = jnp.broadcast_to(norm, norm_ref.shape)
        for place in range(1, count - 1):
            new, first, second = update(place, slice(None))
            outs[2 * place][...] = new
            outs[2 * place + 1][0] = first
            outs[2 * place + 1][1] = second
        outs[-3][...], outs[-2][...], outs[-1][...] = update(count - 1, slice(None))


def adam(scalars, squares, states, gradients):
    rows, columns = states[0].shape[1:]
    part = min(rows, 64)
    out_specs = [
        INSIDE,
        pl.BlockSpec((part, columns), lambda i: (i, 0)),
        pl.BlockSpec((2, part, columns), lambda i: (0, i, 0)),
    ]
    out_shapes = [shape_of((1, LANES), F32), shape_of((rows, columns), F32), shape_of((2, rows, columns), F32)]
    for state in states[1:-1]:
        out_shapes += [shape_of(state.shape[1:], F32), shape_of((2,) + state.shape[1:], F32)]
    out_shapes += [shape_of(states[-1].shape[1:], F32)] * 3
    out_specs += [INSIDE] * (len(out_shapes) - 3)
    return run(
        functools.partial(adam_kernel, len(states), len(squares)),
        (scalars, *squares, *states, *gradients),
        out_shapes,
        (),
        [SCALARS]
        + [INSIDE] * len(squares)
        + [pl.BlockSpec((3, part, columns), lambda i: (0, i, 0))]
        + [INSIDE] * (len(states) - 1)
        + [pl.BlockSpec((part, columns), lambda i: (i, 0))]
        + [INSIDE] * (len(states) - 1),
        grid=(rows // part,),
        out_specs=out_specs,
        name="optimizer",
        mib=18,
        micros=15,
    )


class Place:
    def __init__(self):
        self.dp, self.mp = lax.axis_size("dp"), lax.axis_size("mp")
        self.index, self.column = lax.axis_index("dp"), lax.axis_index("mp")
        self.direct = self.mp == 2 and self.dp in (8, 16, 32, 64)
        self.outer = self.dp // 4
        self.z, self.x, self.core = self.index // 4, (self.index // 2) % 2, self.index % 2
        core = self.core if self.direct else jnp.zeros_like(self.core)
        self.where = jnp.stack([self.z, self.x, core, self.column]).astype(jnp.int32)

    def over_core(self, value):
        return lax.ppermute(value, "dp", [(i, i ^ 1) for i in range(self.dp)])

    def over_x(self, value):
        return lax.ppermute(value, "dp", [(i, i ^ 2) for i in range(self.dp)])

    def over_y(self, value):
        return lax.ppermute(value, "mp", [(0, 1), (1, 0)])

    def over_corner(self, value):
        return lax.ppermute(value, ("dp", "mp"), [(i, i ^ 5) for i in range(2 * self.dp)])

    def along_z(self, value, flip):
        return lax.ppermute(value, "dp", [(i, i ^ (4 * flip)) for i in range(self.dp)])


def pick(value, index, axis):
    return lax.dynamic_index_in_dim(value, index, axis, keepdims=False)


def assemble_kernel(outer, plan, where_ref, *refs):
    parts, wholes = refs[:8], refs[8:]
    height = parts[0].shape[1]
    z, x, core, y = where_ref[0], where_ref[1], where_ref[2], where_ref[3]
    for place, part in enumerate(parts):
        far_x, far_y, far_core = place & 1, (place >> 1) & 1, place >> 2
        column = y if far_y == 0 else 1 - y
        pair = x if far_x == 0 else 1 - x
        single = core if far_core == 0 else 1 - core
        for slot in range(outer):
            block = (z ^ slot) * 4 + pair * 2 + single
            for array, start, width, rows, offset in plan:
                wholes[array][
                    pl.ds(pl.multiple_of(block * rows + offset, 16), height),
                    pl.ds(pl.multiple_of(column * width, LANES), width),
                ] = part[slot, :, start : start + width]


def assemble(place, parts, plan, deps=()):
    outer = parts[0].shape[0]
    sizes = {array: (place.dp * rows, 2 * width) for array, _, width, rows, _ in plan}
    return run(
        functools.partial(assemble_kernel, outer, plan),
        (place.where, *parts),
        [shape_of(sizes[array], BF) for array in sorted(sizes)],
        deps,
        [SCALARS] + [INSIDE] * 8,
        out_specs=[INSIDE] * len(sizes),
        name="assemble",
        mib=14,
        micros=4,
    )


def behind(value, after):
    return lax.optimization_barrier((value, after))[0]


class Gather:
    def __init__(self, place, own):
        self.place = place
        self.first = [own] + [place.along_z(own, flip) for flip in range(1, place.outer)]

    def sides(self, after=()):
        place = self.place
        self.line = jnp.stack(behind(self.first, after))
        self.by_x, self.by_y = place.over_x(self.line), place.over_y(self.line)

    def corner(self, after=()):
        place, half = self.place, self.place.outer // 2
        by_x, by_y = behind((self.by_x, self.by_y), after)
        self.far = (place.over_y(by_x[:half]), place.over_x(by_y[half:]))
        near = [self.line, self.by_x, self.by_y, jnp.concatenate(self.far, axis=0)]
        self.parts = near + [place.over_core(part) for part in near]


def add_low(left, right):
    return left + right


def first_sum_kernel(plan, where_ref, *refs):
    count = len(plan)
    keeps, comes, outs = refs[:count], refs[count : 2 * count], refs[2 * count :]
    x, core, y = where_ref[1], where_ref[2], where_ref[3]
    height = outs[0].shape[2]
    half = keeps[0].shape[0] // 4
    for keep, come, (width, start) in zip(keeps, comes, plan):
        for piece in range(keep.shape[2] // height):
            down = slice(piece * height, (piece + 1) * height)
            into = slice(start + piece * width, start + (piece + 1) * width)
            for column in range(2):
                across = slice(column * width, (column + 1) * width)
                for level in range(half):
                    for out, value in ((outs[0], x), (outs[1], 1 - x)):
                        at = 2 * level + value
                        out[column, level, :, into] = add_low(
                            keep[at, core, down, across], come[at, down, across]
                        )
            for place in range(2 * half):
                at = 2 * half + place
                for out, value in ((outs[2], y), (outs[3], 1 - y)):
                    across = pl.ds(pl.multiple_of(value * width, LANES), width)
                    out[place, :, into] = add_low(keep[at, core, down, across], come[at, down, across])


def second_sum_kernel(where_ref, *refs):
    x, y = where_ref[1], where_ref[3]
    keep, come, keep_low, come_low, *outs = refs
    for level in range(keep.shape[1]):
        for out, value in ((outs[0], y), (outs[1], 1 - y)):
            out[level] = add_low(keep[value, level], come[value, level])
    for level in range(keep_low.shape[0] // 2):
        for out, value in ((outs[2], x), (outs[3], 1 - x)):
            at = 2 * level + value
            out[level] = add_low(keep_low[at], come_low[at])


def third_sum_kernel(where_ref, *refs):
    line = refs[-1]
    z, outer = where_ref[0], line.shape[0]
    operands, outs = refs[: -1 - outer], refs[-1 - outer : -1]
    start = 0
    for keep, come in zip(operands[0::2], operands[1::2]):
        for level in range(keep.shape[0]):
            line[start + level] = add_low(keep[level], come[level])
        start += keep.shape[0]
    for shift, out in enumerate(outs):
        out[...] = line[z ^ shift]


def last_sum_kernel(wide, more, *refs):
    parts, outs = refs[: len(refs) - 2 - more], refs[len(refs) - 2 - more :]
    total_ref, share_ref = outs[-2:]
    total = parts[0][...].astype(F32)
    for part in parts[1:]:
        total = total + part[...].astype(F32)
    total_ref[...] = total[:, :wide]
    lines = jnp.sum(total[:, :wide] * total[:, :wide], axis=0, keepdims=True)
    squares = lines[:, :LANES]
    for start in range(LANES, wide, LANES):
        squares = squares + lines[:, start : start + LANES]
    if more:
        height = total.shape[0]
        share_ref[:height, :] = total[:, wide:]
        share_ref[height:, :] = jnp.zeros((8, LANES), F32)
        share_ref[height : height + 1, :] = squares + outs[0][...]
    else:
        share_ref[...] = squares


class Scatter:
    def __init__(self, place, grads, height, deps=()):
        self.place = place
        half = place.outer // 2
        keeps = [g.reshape(2 * place.outer, 2, g.shape[0] // place.dp, g.shape[1]) for g in grads]
        comes = [place.over_core(pick(keep, 1 - place.core, 1)) for keep in keeps]
        plan, total = [], 0
        for keep in keeps:
            plan.append((keep.shape[3] // 2, total))
            total += keep.shape[2] // height * keep.shape[3] // 2
        shapes = [shape_of((2, half, height, total), BF)] * 2
        shapes += [shape_of((2 * half, height, total), BF)] * 2
        self.first = self.call(functools.partial(first_sum_kernel, plan), (*keeps, *comes), shapes, deps)
        self.came_first = (place.over_x(self.first[1]), place.over_y(self.first[3]))
        self.size = (height, total)

    def call(self, kernel, operands, shapes, deps=(), name="sum", **rest):
        return run(
            kernel,
            (self.place.where, *operands),
            shapes,
            deps,
            [SCALARS] + [INSIDE] * len(operands),
            out_specs=[INSIDE] * len(shapes),
            name=name,
            micros=2,
            mib=14,
            **rest,
        )

    def second(self, deps=()):
        place = self.place
        operands = [v for pair in zip(self.first[0::2], self.came_first) for v in pair]
        shapes = [shape_of((place.outer // 2,) + self.size, BF)] * 4
        self.next = self.call(second_sum_kernel, operands, shapes, deps)
        self.came_second = (place.over_y(self.next[1]), place.over_x(self.next[3]))
        return self.next[1::2]

    def third(self, deps=()):
        place, outer = self.place, self.place.outer
        operands = [v for pair in zip(self.next[0::2], self.came_second) for v in pair]
        lines = self.call(
            third_sum_kernel,
            operands,
            [shape_of(self.size, BF)] * outer,
            deps,
            scratch_shapes=[pltpu.VMEM((outer,) + self.size, BF)],
        )
        self.sent = lines[1:]
        self.lines = [lines[0]] + [
            place.along_z(line, shift) for shift, line in enumerate(lines[1:], start=1)
        ]
        return self.lines

    def last(self, squares=None, deps=()):
        height, wide = self.size
        if squares is None:
            share, more = shape_of((1, LANES), F32), ()
        else:
            wide -= LANES
            share, more = shape_of((height + 8, LANES), F32), (squares,)
        return run(
            functools.partial(last_sum_kernel, wide, len(more)),
            tuple(self.lines) + more,
            [shape_of((height, wide), F32), share],
            deps,
            out_specs=[INSIDE] * 2,
            name="total",
        mib=8,
            micros=1,
        )


def spread_line(place, share):
    return jnp.stack([share] + [place.along_z(share, flip) for flip in range(1, place.outer)])


def spread_rest(place, line, after=()):
    near = [line, place.over_x(line), place.over_y(line), place.over_corner(line)]
    near = jnp.concatenate(behind(near, after), axis=0)
    return jnp.concatenate([near, place.over_core(near)], axis=0)


def scatter_plain(grad):
    rows = lax.psum_scatter(grad, "dp", scatter_dimension=0, tiled=True)
    return lax.psum_scatter(rows, "mp", scatter_dimension=1, tiled=True).astype(F32)


def gather_plain(shard):
    rows = lax.all_gather(shard.astype(BF), "dp", axis=0, tiled=True)
    return lax.all_gather(rows, "mp", axis=1, tiled=True)


def body(
    kernel_state,
    qkv_state,
    proj_state,
    fc1_state,
    fc2_state,
    table_state,
    patches_s,
    patches_l,
    resize_s,
    resize_l,
    bilin_s,
    bilin_l,
    cotangent,
    rates,
    step,
):
    place = Place()
    where, direct = place.where, place.direct
    first = POS_GRID * POS_GRID
    bias_one = table_state[0, first + 7 :].reshape(1, -1)
    low = lambda state: state[0].astype(BF)
    height, wide = qkv_state.shape[1:]
    hidden = fc1_state.shape[2]
    units = fc2_state.shape[1]
    side = proj_state.shape[2]
    if direct:
        pieces = units // height
        first_gather = Gather(place, low(qkv_state))
        first_gather.sides()
        shard = [low(fc1_state)] + list(low(fc2_state).reshape(pieces, height, side)) + [low(proj_state)]
        second_gather = Gather(place, jnp.concatenate(shard, axis=1))
        plan = [(0, 0, hidden, height, 0)]
        plan += [(1, hidden + piece * side, side, units, piece * height) for piece in range(pieces)]

    images, image_rows = patches_l.shape[0], patches_l.shape[1]
    projected, embed_large, kern, mine, sent = resize_forward(
        where,
        kernel_state,
        resize_s,
        resize_l,
        patches_l.reshape(images * image_rows, -1),
        place.mp,
    )
    if direct:
        embed_large, come = mine, (place.over_y(behind(sent, second_gather.first[1:3])),)
        waits = (first_gather.by_x, first_gather.by_y)
    else:
        kern = lax.psum(kern, "mp")
        embed_large = lax.psum_scatter(embed_large, "mp", scatter_dimension=0, tiled=True)
        come = waits = ()
    patches_own = pick(patches_s, place.column, 0)
    first_rows = patches_own.shape[0]
    inputs, normed_one = embed(
        patches_own, kern, embed_large, bilin_s, bilin_l, table_state, come, waits
    )

    if direct:
        first_gather.corner(normed_one)
        second_gather.sides(first_gather.far)
        factors = behind(projected, first_gather.far)
        factors = [factors] + [place.along_z(factors, flip) for flip in range(1, place.outer)]
        w_qkv, qkv_rows = assemble_product(
            place, normed_one, first_gather.parts, [(0, 0, wide, height, 0)]
        )
    else:
        w_qkv = gather_plain(qkv_state[0])
        qkv_rows = product(normed_one, w_qkv)
    pairs = D // LANES
    attention = []
    for call in range(1):
        waits = (second_gather.line,) if direct and call == 0 else ()
        attention.append(attend(qkv_rows, first_rows, image_rows, call * pairs, pairs, waits))
    attended = [call[0] for call in attention]

    if direct:
        factors = [jnp.stack(behind(factors, attended))]
        second_gather.corner((attended, factors[0]))
        factors.append(place.over_x(behind(factors[0], second_gather.far)))
        middle, normed_two, w_proj = merge_parts(
            place, inputs, attended, second_gather.parts, hidden + pieces * side, table_state
        )
        matrices = assemble(place, second_gather.parts, plan, (normed_two,))
    else:
        w_proj, *matrices = [gather_plain(a[0]) for a in (proj_state, fc1_state, fc2_state)]
        middle, normed_two = merge(inputs, attended, w_proj, table_state)
    block_out, back, grad_fc1, grad_fc2, bias_one_grad, bias_two_grad = feed(
        middle, cotangent, normed_two, bias_one, table_state, *matrices
    )
    middle_grad, heads_up, middle_rows, grad_proj = merge_back(
        back, middle, cotangent, attended, w_proj, table_state, ()
    )
    waits = ()
    if direct:
        grads = behind((grad_fc1, grad_fc2), factors[1])
        scatter_f = Scatter(place, (*grads, grad_proj), height)
        factors += [place.over_core(part) for part in behind(factors, back)]
        waits = tuple(scatter_f.first[1::2])
    heads = [
        attend_back(
            qkv_rows, attended[call], heads_up, attention[call][1], first_rows, image_rows,
            call * pairs, waits,
        )
        for call in range(1)
    ]
    large_grad, small_grad = inputs_back(
        heads,
        w_qkv,
        inputs,
        middle_grad,
        table_state,
        patches_own,
        bilin_s,
        bilin_l,
        middle_rows,
        bias_one_grad,
        bias_two_grad,
        BF if direct else F32,
    )
    waits = tuple(scatter_f.second(tuple(factors[2:]))) if direct else ()
    grad_qkv = qkv_grad(normed_one, heads, waits)
    kern_rows = patches_s.shape[2]
    if direct:
        line = spread_line(place, large_grad)
        scatter_f.third((line,))
        scatter_q = Scatter(place, (grad_qkv, small_grad), height, tuple(scatter_f.sent))
        scatter_q.second((scatter_f.lines[1],))
        own_rest, squares_f = scatter_f.last()
        scatter_q.third(tuple(scatter_f.lines[2:]))
        line = spread_rest(place, line, scatter_q.lines[1])
        part = base_all(place, factors, line)
        own_qkv, share = scatter_q.last(squares_f, (part,))
        base_grad, table_total, squares = base_total(
            place, part, resize_s, spread_rest(place, spread_line(place, share)), small_grad.shape[0]
        )
        own_fc2 = jnp.concatenate(
            [own_rest[:, hidden + piece * side : hidden + (piece + 1) * side] for piece in range(pieces)],
            axis=0,
        )
        owned = (own_qkv, own_rest[:, hidden + pieces * side :], own_rest[:, :hidden], own_fc2)
        squares = (squares, place.over_y(squares[:1]))
    else:
        large_all = lax.all_gather(large_grad, "mp", axis=0, tiled=True)
        sums = lax.psum(small_grad, ("dp", "mp"))
        sums = sums.reshape(D // LANES // 2, -1, 2, LANES).transpose(1, 2, 0, 3).reshape(-1, D)
        table_total = sums[kern_rows : kern_rows + TROWS]
        part = lax.dot_general(
            resize_s,
            sums[:kern_rows].reshape(3, -1, D).transpose(1, 0, 2).reshape(-1, 3 * D),
            TN,
            precision=lax.Precision.HIGHEST,
            preferred_element_type=F32,
        )
        base_grad = lax.psum(base_back(projected, large_all), "dp") + part
        owned = tuple(scatter_plain(g) for g in (grad_qkv, grad_proj, grad_fc1, grad_fc2))
        squares = sum(jnp.sum(piece * piece) for piece in owned)
        squares = lax.psum(squares, ("dp", "mp")) + jnp.sum(table_total * table_total)
        squares = squares + lax.psum(jnp.sum(base_grad * base_grad), "mp")
        squares = (jnp.pad(squares.reshape(1, 1), ((0, 0), (0, LANES - 1))),)
    count = step[0].astype(F32)
    fix_one = 1.0 / (1.0 - jnp.power(BETA_ONE, count))
    fix_two = 1.0 / (1.0 - jnp.power(BETA_TWO, count))
    grad_norm, kernel_new, kernel_moments, *blocks = adam(
        jnp.concatenate([jnp.stack([fix_one, fix_two]), rates]),
        squares,
        (kernel_state, qkv_state, proj_state, fc1_state, fc2_state, table_state),
        (base_grad, *owned, table_total),
    )
    grad_norm = grad_norm[0, 0]
    blocks = blocks[:-2] + [jnp.stack(blocks[-2:])]
    return (block_out, grad_norm, kernel_new, kernel_moments, *blocks)


def solution(mesh):
    placed = (
        P(None, "mp", None),
        P(None, "dp", "mp"),
        P(None, "dp", "mp"),
        P(None, "dp", "mp"),
        P(None, "dp", "mp"),
        P(),
        P("dp", None, None),
        P("dp", None, None),
        P(None, "mp"),
        P(None, "mp"),
        P(),
        P(),
        P(("dp", "mp"), None),
        P(),
        P(),
    )
    return jax.shard_map(
        body,
        mesh=mesh,
        in_specs=placed,
        out_specs=(
            P(("dp", "mp"), None),
            P(),
            P("mp", None),
            P(None, "mp", None),
            P("dp", "mp"),
            P(None, "dp", "mp"),
            P("dp", "mp"),
            P(None, "dp", "mp"),
            P("dp", "mp"),
            P(None, "dp", "mp"),
            P("dp", "mp"),
            P(None, "dp", "mp"),
            P(),
            P(),
        ),
        check_vma=False,
    )
```

```python
import functools
import math

import jax
import jax.numpy as jnp
from jax import lax
from jax.experimental import pallas as pl
from jax.experimental.pallas import tpu as pltpu
from jax.sharding import PartitionSpec as P

D = 768
HEADS = 12
HEAD_DIM = 64
FF = 3072
BASE = 32
POS_GRID = 7
GRID_S = 28
GRID_L = 4
TROWS = 60

NORM_EPS = 1e-06
BETA_ONE = 0.5
BETA_TWO = 0.5
DECAY = 0.05
ADAM_EPS = 1e-08
TINY = 1e-37
MASKED = -1e30
LOG2E = 1.4426950408889634
LANES = 128
MIB = 2**20

BF = jnp.bfloat16
F32 = jnp.float32
NN = (((1,), (0,)), ((), ()))
NT = (((1,), (1,)), ((), ()))
TN = (((0,), (0,)), ((), ()))


def shape_of(dims, dtype):
    return jax.ShapeDtypeStruct(dims, dtype)


def params(mib=56):
    return pltpu.CompilerParams(vmem_limit_bytes=mib * MIB)


def cost(flops, moved):
    return pl.CostEstimate(flops=int(flops), bytes_accessed=int(moved), transcendentals=0)


def dot(left, right, dims=NN):
    return lax.dot_general(left, right, dims, preferred_element_type=F32)


def run(kernel, operands, out_shape, deps=(), in_specs=None, name=None, micros=1, mib=56, **rest):
    count, skip = len(operands), len(deps)

    def inner(*refs):
        kernel(*refs[:count], *refs[count + skip :])

    if in_specs is None:
        in_specs = [pl.BlockSpec(memory_space=pltpu.VMEM)] * count
    return pl.pallas_call(
        inner,
        in_specs=list(in_specs) + [pl.BlockSpec(memory_space=pl.ANY)] * skip,
        out_shape=out_shape,
        compiler_params=params(mib),
        cost_estimate=cost(micros * 1e7, 0),
        name=name,
        **rest,
    )(*operands, *deps)


def whole(array):
    return pl.BlockSpec(array.shape, lambda *i: (0,) * len(array.shape))


SCALARS = pl.BlockSpec(memory_space=pltpu.SMEM)
INSIDE = pl.BlockSpec(memory_space=pltpu.VMEM)


def first_state(state):
    return pl.BlockSpec((1,) + state.shape[1:], lambda *i: (0, 0, 0))


def halves(value):
    high = value.astype(BF)
    return high, (value - high.astype(F32)).astype(BF)


def dot_fine(left, right, dims=NN):
    left_high, left_low = halves(left)
    right_high, right_low = halves(right)
    return dot(left_high, right_high, dims) + (
        dot(left_high, right_low, dims) + dot(left_low, right_high, dims)
    )


def norm_forward(inputs):
    centered = inputs - jnp.mean(inputs, axis=-1, keepdims=True)
    inverse = lax.rsqrt(jnp.mean(centered * centered, axis=-1, keepdims=True) + NORM_EPS)
    return centered * inverse, inverse


def norm_backward(upstream, normalized, inverse, gain_row):
    scaled = upstream * gain_row
    inner = jnp.mean(scaled * normalized, axis=-1, keepdims=True)
    result = inverse * (scaled - jnp.mean(scaled, axis=-1, keepdims=True) - normalized * inner)
    return (
        result,
        jnp.sum(upstream * normalized, axis=0, keepdims=True),
        jnp.sum(upstream, axis=0, keepdims=True),
    )


def resize_kernel(
    where_ref,
    base_ref,
    small_ref,
    large_ref,
    patch_ref,
    projected_ref,
    embed_ref,
    kern_ref,
    mine_ref,
    send_ref,
    turned,
    pixels_ref,
):
    rows = embed_ref.shape[0]

    @pl.when(pl.program_id(0) == 0)
    def _():
        embed_ref[...] = jnp.zeros_like(embed_ref)
        kern_ref[...] = jnp.zeros_like(kern_ref)
        count = large_ref.shape[0]
        for start in range(0, rows, LANES):
            size = min(LANES, rows - start)
            patch = patch_ref[start : start + size, :].astype(F32)
            if size < LANES:
                patch = jnp.concatenate(
                    [patch, jnp.zeros((LANES - size, patch.shape[1]), F32)], axis=0
                )
            turned[...] = patch.T
            for channel in range(3):
                across = turned[pl.ds(channel, count, stride=3), :].T
                pixels_ref[channel * rows + start : channel * rows + start + size, :] = across[
                    :size
                ].astype(BF)

    base = base_ref[0]
    width = base.shape[1] // 3
    large_high, large_low = halves(large_ref[...])
    pixels = pixels_ref[...]
    projected = dot(pixels, large_high) + dot(pixels, large_low)
    kern_ref[...] += dot_fine(small_ref[...], base)
    total = embed_ref[...]
    for channel in range(3):
        part = projected[channel * rows : (channel + 1) * rows]
        projected_ref[channel] = part.astype(BF)
        total += dot_fine(part, base[:, channel * width : (channel + 1) * width])
    embed_ref[...] = total

    @pl.when(pl.program_id(0) == pl.num_programs(0) - 1)
    def _():
        part, y = mine_ref.shape[0], where_ref[3]
        mine_ref[...] = embed_ref[pl.ds(pl.multiple_of(y * part, 8), part), :]
        other = embed_ref[pl.ds(pl.multiple_of((1 - y) * part, 8), part), :]
        send_ref[:, : 3 * width] = kern_ref[...].astype(BF)
        if 2 * part == send_ref.shape[0]:
            high, low = halves(other)
            send_ref[:part, 3 * width :] = high
            send_ref[part:, 3 * width :] = low


def resize_forward(where, kernel_state, resize_s, resize_l, patches, parts):
    base_rows, wide = kernel_state.shape[1:]
    count = base_rows // LANES
    rows = patches.shape[0]
    columns = 3 * rows
    shapes = [
        shape_of((3, rows, base_rows), BF),
        shape_of((rows, wide // 3), F32),
        shape_of((resize_s.shape[0], wide), F32),
        shape_of((rows // parts, wide // 3), F32),
        shape_of((resize_s.shape[0], wide + wide // 3), BF),
    ]
    return run(
        resize_kernel,
        (where, kernel_state, resize_s, resize_l, patches),
        shapes,
        (),
        [
            SCALARS,
            pl.BlockSpec((1, LANES, wide), lambda i: (0, i, 0)),
            pl.BlockSpec((resize_s.shape[0], LANES), lambda i: (0, i)),
            pl.BlockSpec((resize_l.shape[0], LANES), lambda i: (0, i)),
            whole(patches),
        ],
        grid=(count,),
        out_specs=[pl.BlockSpec((3, rows, LANES), lambda i: (0, 0, i))]
        + [whole(shape) for shape in shapes[1:]],
        scratch_shapes=[
            pltpu.VMEM((patches.shape[1], LANES), F32),
            pltpu.VMEM((columns, resize_l.shape[0]), BF),
        ],
        name="resize",
        micros=9,
        mib=52,
    )


def embed_kernel(
    patch_ref, kern_ref, large_ref, bilin_s_ref, bilin_l_ref, table_ref, *refs
):
    table = table_ref[0]
    first = POS_GRID * POS_GRID
    pixels = kern_ref.shape[0]
    width = table.shape[1]
    x_ref, a_ref, woven = refs[-3:]
    part = large_ref.shape[0]
    if len(refs) == 4:
        come_ref = refs[0]
        come = come_ref[:, 3 * width :].astype(F32)
        large_part = large_ref[...] + (come[:part] + come[part:])
    else:
        come_ref, large_part = None, large_ref[...]
    tiles = width // LANES
    for channel in range(3):
        for tile in range(tiles):
            start = channel * width + tile * LANES
            value = kern_ref[:, start : start + LANES]
            if come_ref is not None:
                value = value + come_ref[:, start : start + LANES].astype(F32)
            woven[tile, pl.ds(channel, pixels, stride=3), :] = value
    kern = jnp.concatenate([woven[tile].astype(BF) for tile in range(tiles)], axis=1)
    grid_rows = table[:first]
    bias = table[first : first + 1]
    small = patch_ref.shape[0]
    x_ref[:small, :] = (
        dot(patch_ref[...], kern) + dot_fine(bilin_s_ref[...], grid_rows) + bias
    )
    tokens = bilin_l_ref.shape[0]
    placed = dot_fine(bilin_l_ref[...], grid_rows) + bias
    for image in range(large_ref.shape[0] // tokens):
        part = slice(image * tokens, (image + 1) * tokens)
        x_ref[small + image * tokens : small + (image + 1) * tokens, :] = large_part[part] + placed
    normal, _ = norm_forward(x_ref[...])
    a_ref[...] = (normal * table[first + 1 : first + 2] + table[first + 2 : first + 3]).astype(BF)


def embed(patches, kern, large, bilin_s, bilin_l, table_state, come=(), deps=()):
    rows = patches.shape[0] + large.shape[0]
    width = table_state.shape[2]
    return run(
        embed_kernel,
        (patches, kern, large, bilin_s, bilin_l, table_state, *come),
        [shape_of((rows, width), F32), shape_of((rows, width), BF)],
        deps,
        [INSIDE] * 5 + [first_state(table_state)] + [INSIDE] * len(come),
        grid=(1,),
        out_specs=[INSIDE] * 2,
        scratch_shapes=[pltpu.VMEM((width // LANES, patches.shape[1], LANES), F32)],
        name="embed",
        mib=12,
        micros=5,
    )


def product_kernel(left_ref, right_ref, out_ref):
    columns = out_ref.shape[1]
    block = min(columns, D)
    for start in range(0, columns, block):
        across = slice(start, start + block)
        out_ref[:, across] = dot(left_ref[...], right_ref[:, across]).astype(BF)


def product(left, right):
    return run(
        product_kernel,
        (left, right),
        shape_of((left.shape[0], right.shape[1]), BF),
        out_specs=INSIDE,
        name="project",
        micros=7,
        mib=14,
    )


def assemble_product_kernel(outer, plan, where_ref, left_ref, *refs):
    assemble_kernel(outer, plan, where_ref, *refs[:-1])
    product_kernel(left_ref, refs[-2], refs[-1])


def assemble_product(place, left, parts, plan):
    outer, height = parts[0].shape[:2]
    (_, _, width, rows, _) = plan[0]
    shape = (place.dp * rows, 2 * width)
    return run(
        functools.partial(assemble_product_kernel, outer, plan),
        (place.where, left, *parts),
        [shape_of(shape, BF), shape_of((left.shape[0], shape[1]), BF)],
        (),
        [SCALARS] + [INSIDE] * 9,
        out_specs=[INSIDE] * 2,
        name="project",
        micros=8,
        mib=14,
    )


def image_features(rows, first_rows, image_rows):
    row = lax.broadcasted_iota(jnp.int32, (rows, LANES), 0)
    lane = lax.broadcasted_iota(jnp.int32, (rows, LANES), 1) % HEAD_DIM
    label = jnp.where(row < first_rows, 0, 1 + (row - first_rows) // image_rows)
    count = 1 + (rows - first_rows) // image_rows
    own = label == lane
    query = jnp.where(own | (lane >= count), 0.0, MASKED).astype(BF)
    return query, jnp.where(own, 1.0, 0.0).astype(BF)


def attend_kernel(first_rows, image_rows, chunks, q_ref, k_ref, v_ref, out_ref, log_ref):
    rows = q_ref.shape[0]
    query_mark, key_mark = image_features(rows, first_rows, image_rows)
    low = lax.broadcasted_iota(jnp.int32, (rows, LANES), 1) < HEAD_DIM
    step = rows // chunks
    queries = q_ref[...] * jnp.asarray(HEAD_DIM**-0.5, BF)
    keys, values = k_ref[...], v_ref[...]
    ones = jnp.ones((rows, LANES), BF)
    results = []
    for head in range(2):
        mine = low if head == 0 else ~low
        query = jnp.where(mine, queries, query_mark)
        key = jnp.where(mine, keys, key_mark)
        value = jnp.where(mine, values, ones)
        outs, logs = [], []
        for chunk in range(chunks):
            scores = dot(query[chunk * step : (chunk + 1) * step], key, NT)
            largest = jnp.max(scores, axis=1, keepdims=True)
            probs = jnp.exp2(scores * LOG2E - largest * LOG2E)
            summed = dot(probs.astype(BF), value)
            rolled = pltpu.roll(summed, HEAD_DIM, 1)
            outs.append(summed / rolled)
            logs.append(largest * LOG2E + jnp.log2(jnp.where(mine[:step], rolled, summed)))
        results.append(jnp.concatenate(outs, axis=0))
        log_ref[0, 8 * head : 8 * head + 8, :] = jnp.concatenate(logs, axis=0).T[:8]
    out_ref[...] = jnp.where(low, results[0], results[1]).astype(BF)


def attend(qkv, first_rows, image_rows, start, count, deps=()):
    rows, wide = qkv.shape
    pairs = wide // 3 // LANES
    chunks = 3 if rows % 48 == 0 else 1
    part = lambda offset: pl.BlockSpec((rows, LANES), lambda i: (0, offset + i))
    return run(
        functools.partial(attend_kernel, first_rows, image_rows, chunks),
        (qkv, qkv, qkv),
        [shape_of((rows, count * LANES), BF), shape_of((count, 16, rows), F32)],
        deps,
        [part(start), part(pairs + start), part(2 * pairs + start)],
        grid=(count,),
        out_specs=[part(0), pl.BlockSpec((1, 16, rows), lambda i: (i, 0, 0))],
        name="attend",
        mib=8,
        micros=3 * count,
    )


def merge_kernel(x_ref, w_ref, table_ref, *refs):
    attended, (middle_ref, a_ref) = refs[:-2], refs[-2:]
    first = POS_GRID * POS_GRID
    table = table_ref[0]
    middle = x_ref[...] + table[first + 5 : first + 6]
    start = 0
    for part in attended:
        size = part.shape[1]
        middle = middle + dot(part[...], w_ref[start : start + size, :])
        start += size
    middle_ref[...] = middle
    normal, _ = norm_forward(middle)
    a_ref[...] = (normal * table[first + 3 : first + 4] + table[first + 4 : first + 5]).astype(BF)


def merge(inputs, attended, w_proj, table_state, deps=()):
    rows, width = inputs.shape
    return run(
        merge_kernel,
        (inputs, w_proj, table_state, *attended),
        [shape_of((rows, width), F32), shape_of((rows, width), BF)],
        deps,
        [INSIDE, INSIDE, first_state(table_state)] + [INSIDE] * len(attended),
        grid=(1,),
        out_specs=[INSIDE] * 2,
        name="merge",
        mib=12,
        micros=6,
    )


def merge_parts_kernel(outer, plan, count, where_ref, x_ref, table_ref, *refs):
    attended, parts, outs = refs[:count], refs[count : count + 8], refs[count + 8 :]
    assemble_kernel(outer, plan, where_ref, *parts, outs[2])
    merge_kernel(x_ref, outs[2], table_ref, *attended, *outs[:2])


def merge_parts(place, inputs, attended, parts, start, table_state):
    rows, width = inputs.shape
    outer, height, columns = parts[0].shape
    side = columns - start
    plan = [(0, 0, side, height, 0)]
    piece = pl.BlockSpec((outer, height, side), lambda i: (0, 0, start // side))
    return run(
        functools.partial(merge_parts_kernel, outer, plan, len(attended)),
        (place.where, inputs, table_state, *attended, *parts),
        [
            shape_of((rows, width), F32),
            shape_of((rows, width), BF),
            shape_of((place.dp * height, 2 * side), BF),
        ],
        (),
        [SCALARS, INSIDE, first_state(table_state)] + [INSIDE] * len(attended) + [piece] * 8,
        grid=(1,),
        out_specs=[INSIDE] * 3,
        name="merge",
        micros=6,
        mib=14,
    )


def feed_kernel(
    middle_ref,
    cotangent_ref,
    a_ref,
    w_one_ref,
    w_two_ref,
    bias_ref,
    table_ref,
    out_ref,
    grad_ref,
    g_one_ref,
    g_two_ref,
    b_one_ref,
    b_two_ref,
    turned,
    upstream,
):
    place = pl.program_id(0)

    @pl.when(place == 0)
    def _():
        first = POS_GRID * POS_GRID
        turned[...] = a_ref[...].T
        low = cotangent_ref[...].astype(BF)
        upstream[...] = low
        out_ref[...] = middle_ref[...] + table_ref[0][first + 6 : first + 7]
        grad_ref[...] = jnp.zeros_like(grad_ref)
        b_two_ref[...] = jnp.sum(low.astype(F32), axis=0, keepdims=True)

    block = bias_ref.shape[1]
    part = pl.ds(pl.multiple_of(place * block, LANES), block)
    w_one, w_two, dz = w_one_ref[:, part], w_two_ref[part, :], upstream[...]
    hidden = dot(a_ref[...], w_one) + bias_ref[...]
    phi = 0.5 * (1.0 + lax.erf(hidden * 0.7071067811865476))
    active = (hidden * phi).astype(BF)
    slope = phi + hidden * jnp.exp(-0.5 * hidden * hidden) * 0.3989422804014327
    change = dot(dz, w_two, NT) * slope
    b_one_ref[...] = jnp.sum(change, axis=0, keepdims=True)
    change = change.astype(BF)
    out_ref[...] += dot(active, w_two)
    grad_ref[...] += dot(change, w_one, NT)
    g_one_ref[...] = dot(turned[...], change).astype(BF)
    g_two_ref[...] = dot(active, dz, TN).astype(BF)


def feed(middle, cotangent, normed, bias_one, table_state, w_one, w_two):
    rows, width = normed.shape
    hidden = bias_one.shape[1]
    block = D
    across = pl.BlockSpec((width, block), lambda i: (0, i))
    down = pl.BlockSpec((block, width), lambda i: (i, 0))
    line = pl.BlockSpec((1, block), lambda i: (0, i))
    return run(
        feed_kernel,
        (middle, cotangent, normed, w_one, w_two, bias_one, table_state),
        [
            shape_of((rows, width), F32),
            shape_of((rows, width), F32),
            shape_of((width, hidden), BF),
            shape_of((hidden, width), BF),
            shape_of((1, hidden), F32),
            shape_of((1, width), F32),
        ],
        (),
        [INSIDE] * 5 + [line, first_state(table_state)],
        grid=(hidden // block,),
        out_specs=[INSIDE, INSIDE, across, down, line, INSIDE],
        scratch_shapes=[pltpu.VMEM((width, rows), BF), pltpu.VMEM((rows, width), BF)],
        name="feed",
        mib=20,
        micros=9 * (hidden // block),
    )


def merge_back_kernel(count, grad_ref, middle_ref, cotangent_ref, w_ref, table_ref, *refs):
    attended = refs[:count]
    back_ref, heads_ref, rows_ref, g_ref = refs[count:]
    first = POS_GRID * POS_GRID
    normal, inverse = norm_forward(middle_ref[...])
    change, gain, shift = norm_backward(
        grad_ref[...], normal, inverse, table_ref[0][first + 3 : first + 4]
    )
    back = cotangent_ref[...] + change
    back_ref[...] = back
    low = back.astype(BF)
    heads_ref[...] = dot(low, w_ref[...], NT).astype(BF)
    start = 0
    for part in attended:
        size = part.shape[1]
        g_ref[start : start + size, :] = dot(part[...], low, TN).astype(BF)
        start += size
    rows_ref[0:1, :] = gain
    rows_ref[1:2, :] = shift
    rows_ref[2:3, :] = jnp.sum(low.astype(F32), axis=0, keepdims=True)


def merge_back(grad, middle, cotangent, attended, w_proj, table_state, deps=()):
    rows, width = middle.shape
    return run(
        functools.partial(merge_back_kernel, len(attended)),
        (grad, middle, cotangent, w_proj, table_state, *attended),
        [
            shape_of((rows, width), F32),
            shape_of((rows, width), BF),
            shape_of((8, width), F32),
            shape_of(w_proj.shape, BF),
        ],
        deps,
        [INSIDE, INSIDE, INSIDE, INSIDE, first_state(table_state)] + [INSIDE] * len(attended),
        grid=(1,),
        out_specs=[INSIDE] * 4,
        name="merge_back",
        mib=14,
        micros=9,
    )


def attend_back_kernel(
    first_rows, image_rows, chunks, q_ref, k_ref, v_ref, out_ref, up_ref, log_ref, grad_ref
):
    rows = q_ref.shape[0]
    query_mark, key_mark = image_features(rows, first_rows, image_rows)
    low = lax.broadcasted_iota(jnp.int32, (rows, LANES), 1) < HEAD_DIM
    step = rows // chunks
    queries = q_ref[...] * jnp.asarray(HEAD_DIM**-0.5, BF)
    keys, values, up = k_ref[...], v_ref[...], up_ref[...]
    overlap = (out_ref[...].astype(F32) * up.astype(F32)).T
    zeros = jnp.zeros((rows, LANES), BF)
    grads = ([], [], [])
    for head in range(2):
        mine = low if head == 0 else ~low
        query = jnp.where(mine, queries, query_mark)
        key = jnp.where(mine, keys, key_mark)
        value = jnp.where(mine, values, zeros)
        inner = jnp.sum(overlap[HEAD_DIM * head : HEAD_DIM * (head + 1)], axis=0, keepdims=True)
        totals = log_ref[0, 8 * head : 8 * head + 1, :]
        query_grad = jnp.zeros((rows, LANES), F32)
        key_grads, value_grads = [], []
        for chunk in range(chunks):
            part = slice(chunk * step, (chunk + 1) * step)
            scores = dot(key[part], query, NT)
            probs = jnp.exp2(scores * LOG2E - totals)
            value_grads.append(dot(probs.astype(BF), up))
            change = (probs * (dot(value[part], up, NT) - inner)).astype(BF)
            key_grads.append(dot(change, queries))
            query_grad = query_grad + dot(change, keys[part], TN)
        grads[0].append(query_grad * HEAD_DIM**-0.5)
        grads[1].append(jnp.concatenate(key_grads, axis=0))
        grads[2].append(jnp.concatenate(value_grads, axis=0))
    for place, pair in enumerate(grads):
        grad_ref[place] = jnp.where(low, pair[0], pair[1]).astype(BF)


def attend_back(qkv, attended, upstream, logs, first_rows, image_rows, start, deps=()):
    rows, wide = qkv.shape
    pairs, count = wide // 3 // LANES, attended.shape[1] // LANES
    part = lambda offset: pl.BlockSpec((rows, LANES), lambda i: (0, offset + i))
    return run(
        functools.partial(attend_back_kernel, first_rows, image_rows, 1),
        (qkv, qkv, qkv, attended, upstream, logs),
        shape_of((3, rows, count * LANES), BF),
        deps,
        [
            part(start),
            part(pairs + start),
            part(2 * pairs + start),
            part(0),
            part(start),
            pl.BlockSpec((1, 16, rows), lambda i: (i, 0, 0)),
        ],
        grid=(count,),
        out_specs=pl.BlockSpec((3, rows, LANES), lambda i: (0, 0, i)),
        name="attend_back",
        mib=14,
        micros=5 * count,
    )


def qkv_grad_kernel(a_ref, *refs):
    turned = a_ref[...].T
    heads, out = refs[:-1], refs[-1]
    start = 0
    for kind in range(3):
        for part in heads:
            size = part.shape[2]
            out[:, start : start + size] = dot(turned, part[kind]).astype(BF)
            start += size


def qkv_grad(normed, heads, deps=()):
    width = normed.shape[1]
    return run(
        qkv_grad_kernel,
        (normed, *heads),
        shape_of((width, 3 * width), BF),
        deps,
        out_specs=INSIDE,
        name="qkv_grad",
        mib=12,
        micros=6,
    )


def inputs_back_kernel(
    w_ref,
    x_ref,
    back_ref,
    table_ref,
    patch_ref,
    bilin_s_ref,
    bilin_l_ref,
    middle_rows_ref,
    b_one_ref,
    b_two_ref,
    *refs,
):
    heads, (large_ref, small_ref, woven, small_grad) = refs[:-4], refs[-4:]
    width = x_ref.shape[1]
    total, start = None, 0
    for kind in range(3):
        for part in heads:
            size = part.shape[2]
            value = dot(part[kind], w_ref[:, start : start + size], NT)
            total = value if total is None else total + value
            start += size
    first = POS_GRID * POS_GRID
    normal, inverse = norm_forward(x_ref[...])
    change, gain, shift = norm_backward(total, normal, inverse, table_ref[0][first + 1 : first + 2])
    grad = back_ref[...] + change
    low = grad.astype(BF)
    small = patch_ref.shape[0]
    large_ref[...] = low[small:]
    kern = dot(patch_ref[...], low[:small], TN)
    pixels = kern.shape[0] // 3
    for tile in range(width // LANES):
        woven[tile] = kern[:, tile * LANES : (tile + 1) * LANES]
        for channel in range(3):
            small_grad[
                channel * pixels : (channel + 1) * pixels, tile * LANES : (tile + 1) * LANES
            ] = woven[tile, pl.ds(channel, pixels, stride=3), :]
    table_grad_ref = small_grad.at[3 * pixels :]
    table_grad_ref[...] = jnp.zeros_like(table_grad_ref)
    tokens = bilin_l_ref.shape[0]
    large = grad[small : small + tokens]
    for image in range(1, (grad.shape[0] - small) // tokens):
        large = large + grad[small + image * tokens : small + (image + 1) * tokens]
    table_grad_ref[:first, :] = dot_fine(bilin_s_ref[...], grad[:small], TN) + dot_fine(
        bilin_l_ref[...], large, TN
    )
    table_grad_ref[first : first + 1, :] = jnp.sum(grad, axis=0, keepdims=True)
    table_grad_ref[first + 1 : first + 2, :] = gain
    table_grad_ref[first + 2 : first + 3, :] = shift
    table_grad_ref[first + 3 : first + 6, :] = middle_rows_ref[0:3, :]
    table_grad_ref[first + 6 : first + 7, :] = b_two_ref[...]
    for line in range(b_one_ref.shape[1] // width):
        table_grad_ref[first + 7 + line : first + 8 + line, :] = b_one_ref[
            :, line * width : (line + 1) * width
        ]
    rows = small_grad.shape[0]
    count = width // LANES // 2
    for tile in range(2 * count):
        side, level = divmod(tile, count)
        small_ref[level * rows : (level + 1) * rows, side * LANES : (side + 1) * LANES] = small_grad[
            :, tile * LANES : (tile + 1) * LANES
        ].astype(small_ref.dtype)


def inputs_back(
    heads, w_qkv, inputs, back, table_state, patches, bilin_s, bilin_l, rows_grads, bias_one, bias_two, kind
):
    rows, width = inputs.shape
    large = rows - patches.shape[0]
    operands = (
        w_qkv, inputs, back, table_state, patches, bilin_s, bilin_l, rows_grads, bias_one, bias_two, *heads
    )
    specs = [INSIDE] * len(operands)
    specs[3] = first_state(table_state)
    small = small_rows(patches.shape[1])
    return run(
        inputs_back_kernel,
        operands,
        [shape_of((large, width), BF), shape_of((small * width // LANES // 2, 2 * LANES), kind)],
        (),
        specs,
        grid=(1,),
        out_specs=[INSIDE] * 2,
        scratch_shapes=[
            pltpu.VMEM((width // LANES, patches.shape[1], LANES), F32),
            pltpu.VMEM((small, width), F32),
        ],
        name="inputs_back",
        mib=16,
        micros=13,
    )


def small_rows(pixels):
    return -(-(pixels + TROWS) // 256) * 256


def base_back_kernel(projected_ref, large_ref, out_ref):
    width = large_ref.shape[1]
    large = large_ref[...]
    for channel in range(3):
        out_ref[:, channel * width : (channel + 1) * width] = dot(projected_ref[channel], large, TN)


def base_back(projected, large):
    rows, wide = projected.shape[2], 3 * large.shape[1]
    return run(
        base_back_kernel,
        (projected, large),
        shape_of((rows, wide), F32),
        out_specs=INSIDE,
        name="base_back",
        mib=12,
        micros=8,
    )


def base_all_kernel(outer, where_ref, *refs):
    parts, line_ref, out_ref, projected, large = refs[:4], *refs[4:]
    height = line_ref.shape[1]
    z, x, core, y = where_ref[0], where_ref[1], where_ref[2], where_ref[3]
    for place in range(line_ref.shape[0]):
        flip, pair = z ^ (place % outer), x ^ (place // outer % 2)
        block = flip * 4 + pair * 2 + (core ^ (place // outer // 4))
        row = pl.multiple_of((block * 2 + (y ^ (place // outer // 2 % 2))) * height, 16)
        large[pl.ds(row, height), :] = line_ref[place]
    rows = parts[0].shape[2]
    for place, part in enumerate(parts):
        for flip in range(outer):
            block = (z ^ flip) * 4 + (x ^ (place % 2)) * 2 + (core ^ (place // 2))
            for channel in range(3):
                projected[channel, pl.ds(pl.multiple_of(block * rows, 16), rows), :] = part[flip, channel]
    base_back_kernel(projected, large, out_ref)


def base_all(place, parts, line):
    outer, _, rows, columns = parts[0].shape
    count, height, width = line.shape
    return run(
        functools.partial(base_all_kernel, outer),
        (place.where, *parts, line),
        shape_of((columns, 3 * width), F32),
        (),
        [SCALARS] + [INSIDE] * 5,
        out_specs=INSIDE,
        scratch_shapes=[
            pltpu.VMEM((3, place.dp * rows, columns), BF),
            pltpu.VMEM((count * height, width), BF),
        ],
        name="base_back",
        mib=12,
        micros=8,
    )


def base_total_kernel(outer, where_ref, part_ref, small_ref, line_ref, out_ref, table_ref, squares_ref, sums):
    pixels = small_ref.shape[0]
    width = part_ref.shape[1] // 3
    count = width // LANES // 2
    height = sums.shape[1] * sums.shape[0] // line_ref.shape[0]
    rows = sums.shape[1] // count
    z, x, core, y = where_ref[0], where_ref[1], where_ref[2], where_ref[3]
    squares = jnp.zeros((1, LANES), F32)
    for place in range(line_ref.shape[0]):
        flip, pair, side, single = z ^ (place % outer), place // outer % 2, place // outer // 2 % 2, place // outer // 4
        block = flip * 4 + (x ^ pair) * 2 + (core ^ single)
        sums[y ^ side, pl.ds(pl.multiple_of(block * height, 8), height), :] = line_ref[place, :height]
    for block in range(line_ref.shape[0]):
        flip, pair, single, side = (block // 8) ^ z, (block // 4 % 2) ^ x, (block // 2 % 2) ^ core, (block % 2) ^ y
        squares = squares + line_ref[((single * 2 + side) * 2 + pair) * outer + flip, height : height + 1]
    squares_all = squares
    small = jnp.concatenate(
        [
            sums[tile // count, tile % count * rows : (tile % count + 1) * rows, :]
            for tile in range(2 * count)
        ],
        axis=1,
    )
    table = small[3 * pixels : 3 * pixels + table_ref.shape[0]]
    table_ref[...] = table
    lines = jnp.sum(table * table, axis=0, keepdims=True)
    for start in range(0, width, LANES):
        squares_all = squares_all + lines[:, start : start + LANES]
    squares_ref[1:2, :] = squares_all
    squares = jnp.zeros((1, LANES), F32)
    for channel in range(3):
        across = slice(channel * width, (channel + 1) * width)
        value = part_ref[:, across] + dot_fine(
            small_ref[...], small[channel * pixels : (channel + 1) * pixels], TN
        )
        out_ref[:, across] = value
        lines = jnp.sum(value * value, axis=0, keepdims=True)
        for start in range(0, width, LANES):
            squares = squares + lines[:, start : start + LANES]
    squares_ref[0:1, :] = squares


def base_total(place, part, resize_s, line, sums_rows):
    return run(
        functools.partial(base_total_kernel, place.outer),
        (place.where, part, resize_s, line),
        [shape_of(part.shape, F32), shape_of((TROWS, part.shape[1] // 3), F32), shape_of((2, LANES), F32)],
        (),
        [SCALARS] + [INSIDE] * 3,
        out_specs=[INSIDE] * 3,
        scratch_shapes=[pltpu.VMEM((2, sums_rows, LANES), F32)],
        name="base_total",
        mib=10,
        micros=5,
    )


def adam_kernel(count, squares_count, scalars_ref, *refs):
    squares, refs = refs[:squares_count], refs[squares_count:]
    states, gradients, outs = refs[:count], refs[count : 2 * count], refs[2 * count :]
    norm_ref, outs = outs[0], outs[1:]
    total = sum(jnp.sum(part[...], axis=0, keepdims=True) for part in squares)
    norm = jnp.sqrt(jnp.sum(total, axis=1, keepdims=True))
    clip_level = 0.5 * math.sqrt(3 * BASE * BASE * D + 4 * D * D + 2 * D * FF + TROWS * D)
    factor = clip_level / jnp.maximum(norm, clip_level)
    fix_one, fix_two = scalars_ref[0], scalars_ref[1]

    def update(place, rows):
        state_ref = states[place]
        master, old_first, old_second = [state_ref[entry, rows, :] for entry in range(3)]
        clipped = gradients[place][rows, :] * factor
        first = BETA_ONE * (old_first + clipped)
        second = BETA_TWO * (old_second + clipped * clipped)
        square = second * fix_two
        below = square * lax.rsqrt(jnp.maximum(square, TINY)) + ADAM_EPS
        guess = pl.reciprocal(below, approx=True)
        guess = guess * (2.0 - below * guess)
        rate = scalars_ref[2 + place]
        new = master * (1.0 - rate * DECAY) - (first * guess) * (rate * fix_one)
        return new, first, second

    step = pl.program_id(0)
    outs[0][...], outs[1][0], outs[1][1] = update(0, slice(None))

    @pl.when(step == 0)
    def _():
        norm_ref[...] = jnp.broadcast_to(norm, norm_ref.shape)
        for place in range(1, count - 1):
            new, first, second = update(place, slice(None))
            outs[2 * place][...] = new
            outs[2 * place + 1][0] = first
            outs[2 * place + 1][1] = second
        outs[-3][...], outs[-2][...], outs[-1][...] = update(count - 1, slice(None))


def adam(scalars, squares, states, gradients):
    rows, columns = states[0].shape[1:]
    part = min(rows, 64)
    out_specs = [
        INSIDE,
        pl.BlockSpec((part, columns), lambda i: (i, 0)),
        pl.BlockSpec((2, part, columns), lambda i: (0, i, 0)),
    ]
    out_shapes = [shape_of((1, LANES), F32), shape_of((rows, columns), F32), shape_of((2, rows, columns), F32)]
    for state in states[1:-1]:
        out_shapes += [shape_of(state.shape[1:], F32), shape_of((2,) + state.shape[1:], F32)]
    out_shapes += [shape_of(states[-1].shape[1:], F32)] * 3
    out_specs += [INSIDE] * (len(out_shapes) - 3)
    return run(
        functools.partial(adam_kernel, len(states), len(squares)),
        (scalars, *squares, *states, *gradients),
        out_shapes,
        (),
        [SCALARS]
        + [INSIDE] * len(squares)
        + [pl.BlockSpec((3, part, columns), lambda i: (0, i, 0))]
        + [INSIDE] * (len(states) - 1)
        + [pl.BlockSpec((part, columns), lambda i: (i, 0))]
        + [INSIDE] * (len(states) - 1),
        grid=(rows // part,),
        out_specs=out_specs,
        name="optimizer",
        mib=14,
        micros=15,
    )


class Place:
    def __init__(self):
        self.dp, self.mp = lax.axis_size("dp"), lax.axis_size("mp")
        self.index, self.column = lax.axis_index("dp"), lax.axis_index("mp")
        self.direct = self.mp == 2 and self.dp in (8, 16, 32, 64)
        self.outer = self.dp // 4
        self.z, self.x, self.core = self.index // 4, (self.index // 2) % 2, self.index % 2
        core = self.core if self.direct else jnp.zeros_like(self.core)
        self.where = jnp.stack([self.z, self.x, core, self.column]).astype(jnp.int32)

    def over_core(self, value):
        return lax.ppermute(value, "dp", [(i, i ^ 1) for i in range(self.dp)])

    def over_x(self, value):
        return lax.ppermute(value, "dp", [(i, i ^ 2) for i in range(self.dp)])

    def over_y(self, value):
        return lax.ppermute(value, "mp", [(0, 1), (1, 0)])

    def over_corner(self, value):
        return lax.ppermute(value, ("dp", "mp"), [(i, i ^ 5) for i in range(2 * self.dp)])

    def along_z(self, value, flip):
        return lax.ppermute(value, "dp", [(i, i ^ (4 * flip)) for i in range(self.dp)])


def pick(value, index, axis):
    return lax.dynamic_index_in_dim(value, index, axis, keepdims=False)


def assemble_kernel(outer, plan, where_ref, *refs):
    parts, wholes = refs[:8], refs[8:]
    height = parts[0].shape[1]
    z, x, core, y = where_ref[0], where_ref[1], where_ref[2], where_ref[3]
    for place, part in enumerate(parts):
        far_x, far_y, far_core = place & 1, (place >> 1) & 1, place >> 2
        column = y if far_y == 0 else 1 - y
        pair = x if far_x == 0 else 1 - x
        single = core if far_core == 0 else 1 - core
        for slot in range(outer):
            block = (z ^ slot) * 4 + pair * 2 + single
            for array, start, width, rows, offset in plan:
                wholes[array][
                    pl.ds(pl.multiple_of(block * rows + offset, 16), height),
                    pl.ds(pl.multiple_of(column * width, LANES), width),
                ] = part[slot, :, start : start + width]


def assemble(place, parts, plan, deps=()):
    outer = parts[0].shape[0]
    sizes = {array: (place.dp * rows, 2 * width) for array, _, width, rows, _ in plan}
    return run(
        functools.partial(assemble_kernel, outer, plan),
        (place.where, *parts),
        [shape_of(sizes[array], BF) for array in sorted(sizes)],
        deps,
        [SCALARS] + [INSIDE] * 8,
        out_specs=[INSIDE] * len(sizes),
        name="assemble",
        mib=14,
        micros=4,
    )


def behind(value, after):
    return lax.optimization_barrier((value, after))[0]


class Gather:
    def __init__(self, place, own):
        self.place = place
        self.first = [own] + [place.along_z(own, flip) for flip in range(1, place.outer)]

    def sides(self, after=()):
        place = self.place
        self.line = jnp.stack(behind(self.first, after))
        self.by_x, self.by_y = place.over_x(self.line), place.over_y(self.line)

    def corner(self, after=()):
        place, half = self.place, self.place.outer // 2
        by_x, by_y = behind((self.by_x, self.by_y), after)
        self.far = (place.over_y(by_x[:half]), place.over_x(by_y[half:]))
        near = [self.line, self.by_x, self.by_y, jnp.concatenate(self.far, axis=0)]
        self.parts = near + [place.over_core(part) for part in near]


def add_low(left, right):
    return left + right


def first_sum_kernel(plan, where_ref, *refs):
    count = len(plan)
    keeps, comes, outs = refs[:count], refs[count : 2 * count], refs[2 * count :]
    x, core, y = where_ref[1], where_ref[2], where_ref[3]
    height = outs[0].shape[2]
    half = keeps[0].shape[0] // 4
    for keep, come, (width, start) in zip(keeps, comes, plan):
        for piece in range(keep.shape[2] // height):
            down = slice(piece * height, (piece + 1) * height)
            into = slice(start + piece * width, start + (piece + 1) * width)
            for column in range(2):
                across = slice(column * width, (column + 1) * width)
                for level in range(half):
                    for out, value in ((outs[0], x), (outs[1], 1 - x)):
                        at = 2 * level + value
                        out[column, level, :, into] = add_low(
                            keep[at, core, down, across], come[at, down, across]
                        )
            for place in range(2 * half):
                at = 2 * half + place
                for out, value in ((outs[2], y), (outs[3], 1 - y)):
                    across = pl.ds(pl.multiple_of(value * width, LANES), width)
                    out[place, :, into] = add_low(keep[at, core, down, across], come[at, down, across])


def second_sum_kernel(where_ref, *refs):
    x, y = where_ref[1], where_ref[3]
    keep, come, keep_low, come_low, *outs = refs
    for level in range(keep.shape[1]):
        for out, value in ((outs[0], y), (outs[1], 1 - y)):
            out[level] = add_low(keep[value, level], come[value, level])
    for level in range(keep_low.shape[0] // 2):
        for out, value in ((outs[2], x), (outs[3], 1 - x)):
            at = 2 * level + value
            out[level] = add_low(keep_low[at], come_low[at])


def third_sum_kernel(where_ref, *refs):
    line = refs[-1]
    z, outer = where_ref[0], line.shape[0]
    operands, outs = refs[: -1 - outer], refs[-1 - outer : -1]
    start = 0
    for keep, come in zip(operands[0::2], operands[1::2]):
        for level in range(keep.shape[0]):
            line[start + level] = add_low(keep[level], come[level])
        start += keep.shape[0]
    for shift, out in enumerate(outs):
        out[...] = line[z ^ shift]


def last_sum_kernel(wide, more, *refs):
    parts, outs = refs[: len(refs) - 2 - more], refs[len(refs) - 2 - more :]
    total_ref, share_ref = outs[-2:]
    total = parts[0][...].astype(F32)
    for part in parts[1:]:
        total = total + part[...].astype(F32)
    total_ref[...] = total[:, :wide]
    lines = jnp.sum(total[:, :wide] * total[:, :wide], axis=0, keepdims=True)
    squares = lines[:, :LANES]
    for start in range(LANES, wide, LANES):
        squares = squares + lines[:, start : start + LANES]
    if more:
        height = total.shape[0]
        share_ref[:height, :] = total[:, wide:]
        share_ref[height:, :] = jnp.zeros((8, LANES), F32)
        share_ref[height : height + 1, :] = squares + outs[0][...]
    else:
        share_ref[...] = squares


class Scatter:
    def __init__(self, place, grads, height, deps=()):
        self.place = place
        half = place.outer // 2
        keeps = [g.reshape(2 * place.outer, 2, g.shape[0] // place.dp, g.shape[1]) for g in grads]
        comes = [place.over_core(pick(keep, 1 - place.core, 1)) for keep in keeps]
        plan, total = [], 0
        for keep in keeps:
            plan.append((keep.shape[3] // 2, total))
            total += keep.shape[2] // height * keep.shape[3] // 2
        shapes = [shape_of((2, half, height, total), BF)] * 2
        shapes += [shape_of((2 * half, height, total), BF)] * 2
        self.first = self.call(functools.partial(first_sum_kernel, plan), (*keeps, *comes), shapes, deps)
        self.came_first = (place.over_x(self.first[1]), place.over_y(self.first[3]))
        self.size = (height, total)

    def call(self, kernel, operands, shapes, deps=(), name="sum", **rest):
        return run(
            kernel,
            (self.place.where, *operands),
            shapes,
            deps,
            [SCALARS] + [INSIDE] * len(operands),
            out_specs=[INSIDE] * len(shapes),
            name=name,
            micros=2,
            mib=14,
            **rest,
        )

    def second(self, deps=()):
        place = self.place
        operands = [v for pair in zip(self.first[0::2], self.came_first) for v in pair]
        shapes = [shape_of((place.outer // 2,) + self.size, BF)] * 4
        self.next = self.call(second_sum_kernel, operands, shapes, deps)
        self.came_second = (place.over_y(self.next[1]), place.over_x(self.next[3]))
        return self.next[1::2]

    def third(self, deps=()):
        place, outer = self.place, self.place.outer
        operands = [v for pair in zip(self.next[0::2], self.came_second) for v in pair]
        lines = self.call(
            third_sum_kernel,
            operands,
            [shape_of(self.size, BF)] * outer,
            deps,
            scratch_shapes=[pltpu.VMEM((outer,) + self.size, BF)],
        )
        self.sent = lines[1:]
        self.lines = [lines[0]] + [
            place.along_z(line, shift) for shift, line in enumerate(lines[1:], start=1)
        ]
        return self.lines

    def last(self, squares=None, deps=()):
        height, wide = self.size
        if squares is None:
            share, more = shape_of((1, LANES), F32), ()
        else:
            wide -= LANES
            share, more = shape_of((height + 8, LANES), F32), (squares,)
        return run(
            functools.partial(last_sum_kernel, wide, len(more)),
            tuple(self.lines) + more,
            [shape_of((height, wide), F32), share],
            deps,
            out_specs=[INSIDE] * 2,
            name="total",
        mib=8,
            micros=1,
        )


def spread_line(place, share):
    return jnp.stack([share] + [place.along_z(share, flip) for flip in range(1, place.outer)])


def spread_rest(place, line, after=()):
    near = [line, place.over_x(line), place.over_y(line), place.over_corner(line)]
    near = jnp.concatenate(behind(near, after), axis=0)
    return jnp.concatenate([near, place.over_core(near)], axis=0)


def scatter_plain(grad):
    rows = lax.psum_scatter(grad, "dp", scatter_dimension=0, tiled=True)
    return lax.psum_scatter(rows, "mp", scatter_dimension=1, tiled=True).astype(F32)


def gather_plain(shard):
    rows = lax.all_gather(shard.astype(BF), "dp", axis=0, tiled=True)
    return lax.all_gather(rows, "mp", axis=1, tiled=True)


def body(
    kernel_state,
    qkv_state,
    proj_state,
    fc1_state,
    fc2_state,
    table_state,
    patches_s,
    patches_l,
    resize_s,
    resize_l,
    bilin_s,
    bilin_l,
    cotangent,
    rates,
    step,
):
    place = Place()
    where, direct = place.where, place.direct
    first = POS_GRID * POS_GRID
    bias_one = table_state[0, first + 7 :].reshape(1, -1)
    low = lambda state: state[0].astype(BF)
    height, wide = qkv_state.shape[1:]
    hidden = fc1_state.shape[2]
    units = fc2_state.shape[1]
    side = proj_state.shape[2]
    if direct:
        pieces = units // height
        first_gather = Gather(place, low(qkv_state))
        first_gather.sides()
        shard = [low(fc1_state)] + list(low(fc2_state).reshape(pieces, height, side)) + [low(proj_state)]
        second_gather = Gather(place, jnp.concatenate(shard, axis=1))
        plan = [(0, 0, hidden, height, 0)]
        plan += [(1, hidden + piece * side, side, units, piece * height) for piece in range(pieces)]

    images, image_rows = patches_l.shape[0], patches_l.shape[1]
    projected, embed_large, kern, mine, sent = resize_forward(
        where,
        kernel_state,
        resize_s,
        resize_l,
        patches_l.reshape(images * image_rows, -1),
        place.mp,
    )
    if direct:
        embed_large, come = mine, (place.over_y(behind(sent, second_gather.first[1:3])),)
        waits = (first_gather.by_x, first_gather.by_y)
    else:
        kern = lax.psum(kern, "mp")
        embed_large = lax.psum_scatter(embed_large, "mp", scatter_dimension=0, tiled=True)
        come = waits = ()
    patches_own = pick(patches_s, place.column, 0)
    first_rows = patches_own.shape[0]
    inputs, normed_one = embed(
        patches_own, kern, embed_large, bilin_s, bilin_l, table_state, come, waits
    )

    if direct:
        first_gather.corner(normed_one)
        second_gather.sides(first_gather.far)
        factors = behind(projected, first_gather.far)
        factors = [factors] + [place.along_z(factors, flip) for flip in range(1, place.outer)]
        w_qkv, qkv_rows = assemble_product(
            place, normed_one, first_gather.parts, [(0, 0, wide, height, 0)]
        )
    else:
        w_qkv = gather_plain(qkv_state[0])
        qkv_rows = product(normed_one, w_qkv)
    pairs = D // LANES
    attention = []
    for call in range(1):
        waits = (second_gather.line,) if direct and call == 0 else ()
        attention.append(attend(qkv_rows, first_rows, image_rows, call * pairs, pairs, waits))
    attended = [call[0] for call in attention]

    if direct:
        factors = [jnp.stack(behind(factors, attended))]
        second_gather.corner((attended, factors[0]))
        factors.append(place.over_x(behind(factors[0], second_gather.far)))
        middle, normed_two, w_proj = merge_parts(
            place, inputs, attended, second_gather.parts, hidden + pieces * side, table_state
        )
        matrices = assemble(place, second_gather.parts, plan, (normed_two,))
    else:
        w_proj, *matrices = [gather_plain(a[0]) for a in (proj_state, fc1_state, fc2_state)]
        middle, normed_two = merge(inputs, attended, w_proj, table_state)
    block_out, back, grad_fc1, grad_fc2, bias_one_grad, bias_two_grad = feed(
        middle, cotangent, normed_two, bias_one, table_state, *matrices
    )
    middle_grad, heads_up, middle_rows, grad_proj = merge_back(
        back, middle, cotangent, attended, w_proj, table_state, ()
    )
    waits = ()
    if direct:
        grads = behind((grad_fc1, grad_fc2), factors[1])
        scatter_f = Scatter(place, (*grads, grad_proj), height)
        factors += [place.over_core(part) for part in behind(factors, back)]
        waits = tuple(scatter_f.first[1::2])
    heads = [
        attend_back(
            qkv_rows, attended[call], heads_up, attention[call][1], first_rows, image_rows,
            call * pairs, waits,
        )
        for call in range(1)
    ]
    large_grad, small_grad = inputs_back(
        heads,
        w_qkv,
        inputs,
        middle_grad,
        table_state,
        patches_own,
        bilin_s,
        bilin_l,
        middle_rows,
        bias_one_grad,
        bias_two_grad,
        BF if direct else F32,
    )
    waits = tuple(scatter_f.second(tuple(factors[2:]))) if direct else ()
    grad_qkv = qkv_grad(normed_one, heads, waits)
    kern_rows = patches_s.shape[2]
    if direct:
        line = spread_line(place, large_grad)
        scatter_f.third((line,))
        scatter_q = Scatter(place, (grad_qkv, small_grad), height, tuple(scatter_f.sent))
        scatter_q.second((scatter_f.lines[1],))
        own_rest, squares_f = scatter_f.last()
        scatter_q.third(tuple(scatter_f.lines[2:]))
        line = spread_rest(place, line, scatter_q.lines[1])
        part = base_all(place, factors, line)
        own_qkv, share = scatter_q.last(squares_f, (part,))
        base_grad, table_total, squares = base_total(
            place, part, resize_s, spread_rest(place, spread_line(place, share)), small_grad.shape[0]
        )
        own_fc2 = jnp.concatenate(
            [own_rest[:, hidden + piece * side : hidden + (piece + 1) * side] for piece in range(pieces)],
            axis=0,
        )
        owned = (own_qkv, own_rest[:, hidden + pieces * side :], own_rest[:, :hidden], own_fc2)
        squares = (squares, place.over_y(squares[:1]))
    else:
        large_all = lax.all_gather(large_grad, "mp", axis=0, tiled=True)
        sums = lax.psum(small_grad, ("dp", "mp"))
        sums = sums.reshape(D // LANES // 2, -1, 2, LANES).transpose(1, 2, 0, 3).reshape(-1, D)
        table_total = sums[kern_rows : kern_rows + TROWS]
        part = lax.dot_general(
            resize_s,
            sums[:kern_rows].reshape(3, -1, D).transpose(1, 0, 2).reshape(-1, 3 * D),
            TN,
            precision=lax.Precision.HIGHEST,
            preferred_element_type=F32,
        )
        base_grad = lax.psum(base_back(projected, large_all), "dp") + part
        owned = tuple(scatter_plain(g) for g in (grad_qkv, grad_proj, grad_fc1, grad_fc2))
        squares = sum(jnp.sum(piece * piece) for piece in owned)
        squares = lax.psum(squares, ("dp", "mp")) + jnp.sum(table_total * table_total)
        squares = squares + lax.psum(jnp.sum(base_grad * base_grad), "mp")
        squares = (jnp.pad(squares.reshape(1, 1), ((0, 0), (0, LANES - 1))),)
    count = step[0].astype(F32)
    fix_one = 1.0 / (1.0 - jnp.power(BETA_ONE, count))
    fix_two = 1.0 / (1.0 - jnp.power(BETA_TWO, count))
    grad_norm, kernel_new, kernel_moments, *blocks = adam(
        jnp.concatenate([jnp.stack([fix_one, fix_two]), rates]),
        squares,
        (kernel_state, qkv_state, proj_state, fc1_state, fc2_state, table_state),
        (base_grad, *owned, table_total),
    )
    grad_norm = grad_norm[0, 0]
    blocks = blocks[:-2] + [jnp.stack(blocks[-2:])]
    return (block_out, grad_norm, kernel_new, kernel_moments, *blocks)


def solution(mesh):
    placed = (
        P(None, "mp", None),
        P(None, "dp", "mp"),
        P(None, "dp", "mp"),
        P(None, "dp", "mp"),
        P(None, "dp", "mp"),
        P(),
        P("dp", None, None),
        P("dp", None, None),
        P(None, "mp"),
        P(None, "mp"),
        P(),
        P(),
        P(("dp", "mp"), None),
        P(),
        P(),
    )
    return jax.shard_map(
        body,
        mesh=mesh,
        in_specs=placed,
        out_specs=(
            P(("dp", "mp"), None),
            P(),
            P("mp", None),
            P(None, "mp", None),
            P("dp", "mp"),
            P(None, "dp", "mp"),
            P("dp", "mp"),
            P(None, "dp", "mp"),
            P("dp", "mp"),
            P(None, "dp", "mp"),
            P("dp", "mp"),
            P(None, "dp", "mp"),
            P(),
            P(),
        ),
        check_vma=False,
    )
```
